32 devices in a mesh: lat: 4 (over y, x), fld: 8 (over z, core).
Axes of the slice: x: 2, y: 2, z: 4, core: 2. Of those that a mesh axis runs over, the one named last changes fastest.
Arguments:
- patches: bfloat16 [64, 16, 32, 512], P('fld', 'lat'), may hold values from -6 to 6
- segment_ids: int32 [64, 16, 32], P('fld'), may hold values from 0 to 2, as said below
- gain_attn: float32 [512], replicated, may hold values from 0.25 to 1.75
- bias_attn: float32 [512], replicated, may hold values from -2 to 2
- w_qkv: bfloat16 [512, 1536], replicated, may hold values from -0.25 to 0.25
- w_proj: bfloat16 [512, 512], replicated, may hold values from -0.5 to 0.5
- gain_mlp: float32 [512], replicated, may hold values from 0.25 to 1.75
- bias_mlp: float32 [512], replicated, may hold values from -2 to 2
- w_hidden: bfloat16 [512, 2048], replicated, may hold values from -0.25 to 0.25
- w_output: bfloat16 [2048, 512], replicated, may hold values from -0.1875 to 0.1875
- cotangent: bfloat16 [64, 16, 32, 512], P('fld', 'lat'), may hold values from -6 to 6
Outputs:
- layer_out: bfloat16 [64, 16, 32, 512], P('fld', 'lat')
- patch_grad: float32 [64, 16, 32, 512], P('fld', 'lat')
- attn_gain_grad: float32 [512], replicated
- attn_bias_grad: float32 [512], replicated
- qkv_grad: float32 [512, 1536], replicated
- proj_grad: float32 [512, 512], replicated
- mlp_gain_grad: float32 [512], replicated
- mlp_bias_grad: float32 [512], replicated
- hidden_grad: float32 [512, 2048], replicated
- output_grad: float32 [2048, 512], replicated
The draws below stay inside these ranges and needn't reach their ends.
Inputs may be any that keep to these rules, and one draw needn't show every extreme that they name: `segment_ids`: within a field the ids are the same in all 16 rows of a column and never fall from column 0 to column 31; column 0 holds 0 and the last column 2.
All inputs are finite; a program needn't handle non-finite values.
Results may differ from the reference program's by a relative error of at most 0.01.
Values may be sent and summed in bfloat16 or wider, within the bound.
A program may use at most 448 MiB of HBM per device.

```python
import jax
import jax.numpy as jnp
from jax import lax

D = 512
HEADS = 16
HEAD_DIM = 32
FF = 2048
ROWS = 16
COLS = 32
F_DEV = 8
FIELDS = 64


def draw_segment_ids(key, part):
    key = jax.random.fold_in(key, 7)
    boundaries = jax.random.randint(key, (FIELDS, 2), 1, COLS)
    column = jnp.arange(COLS)
    labels = (column[None, :] >= boundaries[:, :1]).astype(jnp.int32) + (column[None, :] >= boundaries[:, 1:]).astype(jnp.int32)
    return jnp.broadcast_to(labels[:, None, :], (FIELDS, ROWS, COLS)).astype(jnp.int32)


def steps_of(rng, shape, split, least, top_value):
    level, own = 1.0, jax.random.fold_in(rng, 6)
    for axis_at, parts in split:
        draws = jnp.exp(jax.random.uniform(jax.random.fold_in(own, axis_at), (parts,), jnp.float32, least / len(split), top_value / len(split)))
        level = level * jnp.repeat(draws, shape[axis_at] // parts).reshape([-1 if axis == axis_at else 1 for axis in range(len(shape))])
    return level


def noise(own_key, dims, deviation, limit, split=(), held_as=jnp.bfloat16):
    array = deviation * jax.random.normal(own_key, dims, jnp.float32)
    if split:
        array = array * steps_of(own_key, dims, split, -0.22, 0.18)
    return jnp.clip(array, -limit, limit).astype(held_as)


def setup_inputs(seed: int = 0) -> dict:
    streams_of = jax.random.split(jax.random.key(seed), 12)
    return {
        "patches": noise(streams_of[0], (FIELDS, ROWS, COLS, D), 1.0, 6.0, ((0, 8), (1, 4))),
        "segment_ids": draw_segment_ids(jax.random.fold_in(streams_of[11], 71), 0),
        "gain_attn": jnp.clip(1.0 + 0.15 * jax.random.normal(streams_of[2], (D,), jnp.float32), 0.25, 1.75),
        "bias_attn": noise(streams_of[3], (D,), 0.3, 2.0, (), jnp.float32),
        "w_qkv": noise(streams_of[4], (D, 3 * D), D ** -0.5, 0.25),
        "w_proj": noise(streams_of[5], (D, D), (D // 4) ** -0.5, 0.5),
        "gain_mlp": jnp.clip(1.0 + 0.15 * jax.random.normal(streams_of[6], (D,), jnp.float32), 0.25, 1.75),
        "bias_mlp": noise(streams_of[7], (D,), 0.3, 2.0, (), jnp.float32),
        "w_hidden": noise(streams_of[8], (D, FF), D ** -0.5, 0.25),
        "w_output": noise(streams_of[9], (FF, D), (FF // 2) ** -0.5, 0.1875),
        "cotangent": noise(streams_of[10], (FIELDS, ROWS, COLS, D), 1.0, 6.0, ((0, 8), (1, 4))),
    }


epsilon = 1e-06
highest = lax.Precision.HIGHEST

@jax.custom_vjp
def low(v):
    return lax.optimization_barrier(v.astype(jnp.bfloat16)).astype(jnp.float32)

@jax.custom_vjp
def low_back(v):
    return v

def low_keep(v):
    return (low(v), None)

def low_pass(kept, grad):
    return (grad,)

def back_keep(v):
    return (v, None)

def back_low(kept, grad):
    return (low(grad),)
low.defvjp(low_keep, low_pass)
low_back.defvjp(back_keep, back_low)

def layer_norm(values, norm_gain, norm_bias):
    center = lax.optimization_barrier(jnp.mean(values, axis=-1, keepdims=True))
    offsets = values - center
    variance = lax.optimization_barrier(jnp.mean(offsets * offsets, axis=-1, keepdims=True))
    return offsets * lax.rsqrt(variance + epsilon) * norm_gain + norm_bias

def window(padded, band_rows):
    pieces = []
    for shift_row in range(3):
        row_band = padded[:, shift_row:shift_row + band_rows]
        for offset in range(-4, 5):
            pieces.append(jnp.roll(row_band, -offset, axis=2))
    return jnp.stack(pieces, axis=3)

def layer(inputs, labels, parameters):
    gain_attn, bias_attn, w_qkv, w_proj, gain_mlp, bias_mlp, w_hidden, w_output = parameters
    fields, band_rows, columns, model_width = inputs.shape
    pad_shape = (fields, band_rows + 2, columns, HEADS, HEAD_DIM)
    normed = low(layer_norm(inputs, gain_attn, bias_attn))
    joined_qkv = low(low_back(jnp.einsum('frcd,de->frce', normed, w_qkv, precision=highest)))
    queries = joined_qkv[..., :model_width].reshape(fields, band_rows, columns, HEADS, HEAD_DIM)
    padded = jnp.pad(joined_qkv[..., model_width:], ((0, 0), (1, 1), (0, 0), (0, 0)))
    key_win = window(padded[..., :model_width].reshape(pad_shape), band_rows)
    value_win = window(padded[..., model_width:].reshape(pad_shape), band_rows)
    label_pad = jnp.pad(labels, ((0, 0), (1, 1), (0, 0)), constant_values=-1)
    allowed = (labels[..., None] == window(label_pad, band_rows))[:, :, :, None, :]
    raw_scores = low_back(jnp.einsum('frchd,frcjhd->frchj', queries, key_win, precision=highest))
    scores = jnp.where(allowed, raw_scores * HEAD_DIM ** (-0.5), -1000000000.0)
    attention = low(jax.nn.softmax(scores, axis=-1))
    context = jnp.einsum('frchj,frcjhd->frchd', attention, value_win, precision=highest)
    context = low(low_back(context.reshape(fields, band_rows, columns, model_width)))
    branch = low_back(jnp.einsum('frcd,de->frce', context, w_proj, precision=highest))
    residual = inputs + branch
    normed_mlp = low(layer_norm(residual, gain_mlp, bias_mlp))
    hidden_pre = low_back(jnp.einsum('frcd,de->frce', normed_mlp, w_hidden, precision=highest))
    activated = low(jax.nn.gelu(hidden_pre, approximate=False))
    return residual + jnp.einsum('frce,ed->frcd', activated, w_output, precision=highest)

def reference(patches, segment_ids, gain_attn, bias_attn, w_qkv, w_proj, gain_mlp, bias_mlp, w_hidden, w_output, cotangent):
    weights = tuple((item.astype(jnp.float32) for item in (gain_attn, bias_attn, w_qkv, w_proj, gain_mlp, bias_mlp, w_hidden, w_output)))
    groups = FIELDS // F_DEV
    group_shape = (groups, F_DEV, ROWS, COLS, D)
    inputs = patches.astype(jnp.float32).reshape(group_shape)
    labels = segment_ids.astype(jnp.int32).reshape(groups, F_DEV, ROWS, COLS)
    seeds = cotangent.astype(jnp.float32).reshape(group_shape)

    def accumulate(carry, group_items):
        inputs_group, labels_group, seeds_group = group_items

        def forward(values, *parameters):
            return layer(values, labels_group, parameters)
        outputs, pullback = jax.vjp(forward, inputs_group, *weights)
        gradients = pullback(seeds_group)
        summed = tuple((running + addend for running, addend in zip(carry, gradients[1:])))
        return (summed, (outputs, gradients[0]))
    initial = tuple((jnp.zeros_like(item) for item in weights))
    sums, (outputs, input_grads) = lax.scan(accumulate, initial, (inputs, labels, seeds))
    full_shape = (FIELDS, ROWS, COLS, D)
    return (outputs.reshape(full_shape).astype(jnp.bfloat16), input_grads.reshape(full_shape), sums[0], sums[1], sums[2], sums[3], sums[4], sums[5], sums[6], sums[7])
```

```python
import functools
import math

import jax
import jax.numpy as jnp
from jax import lax
from jax.experimental import pallas as pl
from jax.experimental.pallas import tpu as pltpu
from jax.sharding import PartitionSpec as P

HEAD_DIM = 32
GROUP = 8
WIDE = GROUP * HEAD_DIM
SCALE = HEAD_DIM ** -0.5
LOG2E = math.log2(math.e)
EPS = 1e-6
REACH = 4
NEG = -1e30
CHUNK = 512
BF = jnp.bfloat16
F32 = jnp.float32
MESH = pl.DeviceIdType.MESH

NT = (((1,), (1,)), ((), ()))
TN = (((0,), (0,)), ((), ()))


def dot(a, b, dims=None):
    if dims is None:
        return jnp.dot(a, b, preferred_element_type=F32)
    return lax.dot_general(a, b, dims, preferred_element_type=F32)


def normalize(x):
    center = jnp.mean(x, axis=-1, keepdims=True)
    off = x - center
    rstd = lax.rsqrt(jnp.mean(off * off, axis=-1, keepdims=True) + EPS)
    return off * rstd, rstd


def norm_pull(e, gain, n, rstd):
    ge = e * gain
    a = jnp.mean(ge, axis=-1, keepdims=True)
    b = jnp.mean(ge * n, axis=-1, keepdims=True)
    return (ge - a - n * b) * rstd


def gelu_both(u):
    z = jnp.abs(u) * (1.0 / math.sqrt(2.0))
    t = 1.0 / (1.0 + 0.3275911 * z)
    ex = jnp.exp2((u * u) * (-0.5 * LOG2E))
    poly = t * (0.254829592 + t * (-0.284496736 + t * (1.421413741 + t * (-1.453152027 + t * 1.061405429))))
    half = 0.5 * poly * ex
    cdf = jnp.where(u < 0, half, 1.0 - half)
    return u * cdf, cdf + u * (ex * (1.0 / math.sqrt(2.0 * math.pi)))


def row_sums(x):
    return jnp.sum(x, axis=0, keepdims=True)


class Plan:
    def __init__(self, mesh, fields, rows, cols, width, ff):
        self.lats = mesh.shape["lat"]
        self.flds = mesh.shape["fld"]
        self.zs = self.flds // 2
        self.fields, self.rows, self.cols = fields, rows, cols
        self.tf = rows * cols
        self.tokens = fields * self.tf
        self.width, self.ff = width, ff
        self.chunks = ff // CHUNK
        unit = 16 * self.lats * self.flds
        pad = lambda n: -(-n // unit) * unit
        blocks = width // 128
        mlp = CHUNK * blocks + width * (CHUNK // 128)
        self.sizes = [pad(mlp)] * self.chunks + [pad(width * blocks)] + [pad(width * (3 * WIDE // 128))] * 2


def body(plan, *refs):
    pn = plan
    np_ = len(pn.sizes)
    (patches, seg, gain_a, bias_a, w_qkv, w_proj, gain_m, bias_m, w_hid, w_out, cot) = refs[:11]
    out_layer, out_patch, out_vec = refs[11:14]
    out_ag = refs[14 : 14 + np_]
    sc = list(refs[14 + np_ :])

    def take(n=None):
        if n is None:
            return sc.pop(0)
        got = sc[:n]
        del sc[:n]
        return got

    wq, wp, wh, wo = take(4)
    pb, cb, segv, halo = take(4)
    normed, qb, kv, pt, ctx, res, nm, acco, accg, act, gpre, gctx, dq, dacc, edge = take(15)
    hsend, hrecv, bm, bmf, biasb, vec, vrz, vrx, vrc = take(9)
    sb, rc, rx, rz, ag = take(np_), take(np_), take(np_), take(np_), take(np_)
    in_sem, out_sem, halo_s, halo_r, back_s, back_r, rs_s, rs_r, v_s, v_r = take(10)

    lat = lax.axis_index("lat")
    fld = lax.axis_index("fld")
    core = lax.rem(fld, 2)
    z = lax.div(fld, 2)
    L, Z = pn.lats, pn.zs
    FD, R, C, TF, T, D = pn.fields, pn.rows, pn.cols, pn.tf, pn.tokens, pn.width

    ins = [(patches, pb), (w_qkv, wq), (seg, segv), (w_proj, wp), (cot, cb), (w_hid, wh), (w_out, wo)]
    loads = [pltpu.make_async_copy(s, d, in_sem.at[i]) for i, (s, d) in enumerate(ins)]
    for c in loads:
        c.start()

    pair = (lat, fld + 1 - 2 * core)
    lat_peers = [(lax.rem(lat + k, L), fld) for k in range(1, L)]
    z_peers = [(lat, lax.rem(z + k, Z) * 2 + core) for k in range(1, Z)]
    barrier = pltpu.get_barrier_semaphore()
    everyone = [pair] + lat_peers + z_peers
    for d in everyone:
        pl.semaphore_signal(barrier, inc=1, device_id=d, device_id_type=MESH)
    pl.semaphore_wait(barrier, len(everyone))

    up, down = (lat - 1, fld), (lat + 1, fld)
    has_up, has_down = lat > 0, lat < L - 1

    def remote(src, dst, s, r, dev):
        return pltpu.make_async_remote_copy(
            src_ref=src, dst_ref=dst, send_sem=s, recv_sem=r, device_id=dev, device_id_type=MESH
        )

    def arrived(ref, sem):
        pltpu.make_async_copy(ref, ref, sem).wait()

    halo_up = remote(patches.at[:, pl.ds(0, C)], halo.at[1], halo_s.at[0], halo_r.at[1], up)
    halo_dn = remote(patches.at[:, pl.ds(TF - C, C)], halo.at[0], halo_s.at[1], halo_r.at[0], down)
    pl.when(has_up)(halo_up.start)
    pl.when(has_down)(halo_dn.start)

    def rows_of(p):
        n = pn.sizes[p]
        return n, n // 2, n // 2 // L, n // 2 // L // Z

    def at(i, n):
        return pl.ds(pl.multiple_of(i * n, 16), n)

    def rs_pair(p):
        n, h, s, w = rows_of(p)
        remote(sb[p].at[at(1 - core, h)], rc[p], rs_s.at[p, 0], rs_r.at[p, 0], pair).start()

    def rs_lat(p):
        n, h, s, w = rows_of(p)
        arrived(rc[p], rs_r.at[p, 0])
        mine = sb[p].at[at(core, h)]
        mine[...] = (mine[...].astype(F32) + rc[p][...].astype(F32)).astype(BF)
        for k, dev in enumerate(lat_peers):
            src = sb[p].at[pl.ds(pl.multiple_of(core * h + dev[0] * s, 16), s)]
            remote(src, rx[p].at[k], rs_s.at[p, 1], rs_r.at[p, 1], dev).start()

    def rs_z(p):
        n, h, s, w = rows_of(p)
        arrived(rx[p], rs_r.at[p, 1])
        base = core * h + lat * s
        mine = sb[p].at[pl.ds(pl.multiple_of(base, 16), s)]
        total = mine[...].astype(F32)
        for k in range(L - 1):
            total = total + rx[p][k].astype(F32)
        mine[...] = total.astype(BF)
        for k, dev in enumerate(z_peers):
            zi = lax.rem(z + k + 1, Z)
            src = sb[p].at[pl.ds(pl.multiple_of(base + zi * w, 16), w)]
            remote(src, rz[p].at[k], rs_s.at[p, 2], rs_r.at[p, 2], dev).start()

    def ag_z(p):
        n, h, s, w = rows_of(p)
        arrived(rz[p], rs_r.at[p, 2])
        spot = pl.ds(pl.multiple_of(core * h + lat * s + z * w, 16), w)
        total = sb[p][spot, :].astype(F32)
        for k in range(Z - 1):
            total = total + rz[p][k].astype(F32)
        ag[p][spot, :] = total.astype(BF)
        for dev in z_peers:
            remote(ag[p].at[spot], ag[p].at[spot], rs_s.at[p, 3], rs_r.at[p, 3], dev).start()

    def ag_lat(p):
        n, h, s, w = rows_of(p)
        arrived(ag[p].at[pl.ds(0, (Z - 1) * w)], rs_r.at[p, 3])
        spot = pl.ds(pl.multiple_of(core * h + lat * s, 16), s)
        for dev in lat_peers:
            remote(ag[p].at[spot], ag[p].at[spot], rs_s.at[p, 4], rs_r.at[p, 4], dev).start()

    def ag_pair(p):
        n, h, s, w = rows_of(p)
        arrived(ag[p].at[pl.ds(0, (L - 1) * s)], rs_r.at[p, 4])
        spot = at(core, h)
        remote(ag[p].at[spot], ag[p].at[spot], rs_s.at[p, 5], rs_r.at[p, 5], pair).start()

    def ag_out(p):
        n, h, s, w = rows_of(p)
        arrived(ag[p].at[pl.ds(0, h)], rs_r.at[p, 5])
        pltpu.make_async_copy(ag[p], out_ag[p], out_sem.at[2 + p]).start()

    def finish(p):
        n, h, s, w = rows_of(p)
        for i, m in enumerate((h, (L - 1) * s, (Z - 1) * w, (Z - 1) * w, (L - 1) * s, h)):
            arrived(sb[p].at[pl.ds(0, m)], rs_s.at[p, i])
        pltpu.make_async_copy(ag[p], out_ag[p], out_sem.at[2 + p]).wait()

    stages = (rs_pair, rs_lat, rs_z, ag_z, ag_lat, ag_pair, ag_out)

    def put(p, start, value):
        rows, lanes = value.shape
        low = value.astype(BF)
        for j in range(lanes // 128):
            sb[p][start + j * rows : start + (j + 1) * rows, :] = low[:, j * 128 : (j + 1) * 128]

    rid = lax.broadcasted_iota(jnp.int32, (WIDE, WIDE), 0) // HEAD_DIM
    cid = lax.broadcasted_iota(jnp.int32, (WIDE, WIDE), 1) // HEAD_DIM
    same = jnp.where(rid == cid, 1.0, 0.0)
    bm[...] = same.astype(BF)
    bmf[...] = same

    ga, ba = gain_a[...].reshape(1, D), bias_a[...].reshape(1, D)
    gm, bmlp = gain_m[...].reshape(1, D), bias_m[...].reshape(1, D)
    loads[0].wait()

    def norm_one(f, carry):
        n, _ = normalize(pb[f].astype(F32))
        normed[pl.ds(pl.multiple_of(f * TF, TF), TF), :] = (n * ga + ba).astype(BF)
        return carry

    lax.fori_loop(0, FD, norm_one, 0)
    loads[1].wait()
    qb[...] = dot(normed[...], wq[:, :D]).astype(BF)
    for j in range(2):
        part = dot(normed[...], wq[:, (j + 1) * D : (j + 2) * D]).astype(BF)
        kv[:, C : C + TF, j * D : (j + 1) * D] = part.reshape(FD, TF, D)

    loads[2].wait()
    kcol = lax.broadcasted_iota(jnp.int32, (C, WIDE), 0)
    qcol = lax.rem(lax.broadcasted_iota(jnp.int32, (C, WIDE), 1), C)
    away = jnp.abs(kcol - qcol)
    near = jnp.minimum(away, C - away) <= REACH
    diag = lax.broadcasted_iota(jnp.int32, (C, C), 0) == lax.broadcasted_iota(jnp.int32, (C, C), 1)
    for f in range(FD):
        line = segv[f, 0:1, :].astype(F32)
        across = jnp.concatenate([line] * GROUP, axis=1)
        along = jnp.sum(jnp.where(diag, line, 0.0), axis=1, keepdims=True)
        biasb[f] = jnp.where(jnp.logical_and(near, along == across), 0.0, NEG)
    pole_top = jnp.where(has_up, 0.0, NEG)
    pole_bottom = jnp.where(has_down, 0.0, NEG)

    for side, ok, copy in ((0, has_up, halo_dn), (1, has_down, halo_up)):
        pl.when(ok)(copy.wait_recv)

        @pl.when(jnp.logical_not(ok))
        def _():
            halo[side] = jnp.zeros((FD, C, D), BF)

        n, _unused = normalize(halo[side].reshape(FD * C, D).astype(F32))
        low = (n * ga + ba).astype(BF)
        edge_kv = dot(low, wq[:, D:]).astype(BF).reshape(FD, C, 2 * D)
        start = 0 if side == 0 else TF + C
        kv[:, start : start + C, :] = edge_kv

    def diagonal(o):
        o = o * bmf[...]
        total = o[0:HEAD_DIM]
        for h in range(1, GROUP):
            total = total + o[h * HEAD_DIM : (h + 1) * HEAD_DIM]
        return total

    def widened(q):
        return jnp.concatenate([q] * GROUP, axis=0) * bm[...]

    def attend(f, carry):
        bias = biasb[f]
        for g in range(2):
            lanes = slice(g * WIDE, (g + 1) * WIDE)
            vlanes = slice(D + g * WIDE, D + (g + 1) * WIDE)
            for r in range(R):
                tok = pl.ds(pl.multiple_of(f * TF + r * C, C), C)
                win = slice(r * C, (r + 3) * C)
                s = dot(kv[f, win, lanes], widened(qb[tok, lanes]), NT)
                top = bias + pole_top if r == 0 else bias
                low = bias + pole_bottom if r == R - 1 else bias
                s = s + jnp.concatenate([top, bias, low], axis=0)
                m = jnp.max(s, axis=0, keepdims=True)
                p = jnp.exp2((s - m) * (SCALE * LOG2E))
                p = (p * (1.0 / row_sums(p))).astype(BF)
                pt[f, g * R + r] = p
                ctx[tok, lanes] = diagonal(dot(p, kv[f, win, vlanes], TN)).astype(BF)
        return carry

    lax.fori_loop(0, FD, attend, 0)

    loads[3].wait()
    res[...] = pb[...].reshape(T, D).astype(F32) + dot(ctx[...], wp[...])

    def norm_two(f, carry):
        tok = pl.ds(pl.multiple_of(f * TF, TF), TF)
        n, _ = normalize(res[tok, :])
        nm[tok, :] = (n * gm + bmlp).astype(BF)
        return carry

    lax.fori_loop(0, FD, norm_two, 0)

    for i in (4, 5, 6):
        loads[i].wait()
    tile = min(256, T)
    for c in range(pn.chunks):
        cs = slice(c * CHUNK, (c + 1) * CHUNK)

        def mlp_tile(t, carry, c=c, cs=cs):
            tok = pl.ds(pl.multiple_of(t * tile, tile), tile)
            hidden = dot(nm[tok, :], wh[:, cs])
            back = dot(cb[tok, :], wo[cs, :], NT)
            a, da = gelu_both(hidden)
            a = a.astype(BF)
            gp = (da * back).astype(BF)
            act[tok, :] = a
            gpre[tok, :] = gp
            fwd = dot(a, wo[cs, :])
            bwd = dot(gp, wh[:, cs], NT)
            if c == 0:
                acco[tok, :] = fwd
                accg[tok, :] = bwd
            else:
                acco[tok, :] += fwd
                accg[tok, :] += bwd
            return carry

        lax.fori_loop(0, T // tile, mlp_tile, 0)
        put(c, 0, dot(act[...], cb[...], TN))
        put(c, CHUNK * (D // 128), dot(nm[...], gpre[...], TN))
        for back in range(min(c + 1, 4)):
            stages[back](c - back)

    zero = jnp.zeros((1, D), F32)

    def mlp_end(f, carry):
        dg, db = carry
        tok = pl.ds(pl.multiple_of(f * TF, TF), TF)
        x = res[tok, :]
        act[tok, :] = (x + acco[tok, :]).astype(BF)
        n, rstd = normalize(x)
        e = accg[tok, :]
        gr = cb[tok, :].astype(F32) + norm_pull(e, gm, n, rstd)
        res[tok, :] = gr
        gpre[tok, :] = gr.astype(BF)
        return dg + row_sums(e * n), db + row_sums(e)

    mlp_gain, mlp_bias = lax.fori_loop(0, FD, mlp_end, (zero, zero))
    layer_copy = pltpu.make_async_copy(act, out_layer, out_sem.at[0])
    layer_copy.start()
    pj = pn.chunks
    put(pj, 0, dot(ctx[...], gpre[...], TN))
    gctx[...] = dot(gpre[...], wp[...], NT).astype(BF)

    todo = {}
    order = []
    nc = pn.chunks
    for step in range(1, 8):
        line = []
        if step == 1:
            line.append((0, pj))
        for p in range(nc):
            st = step + nc - 1 - p
            if st < 7:
                line.append((st, p))
        if 2 <= step:
            line.append((step - 1, pj))
        order.append(line)

    def run(line):
        for st, p in line:
            stages[st](p)

    def back_group(g, hooks):
        lanes = slice(g * WIDE, (g + 1) * WIDE)
        vlanes = slice(D + g * WIDE, D + (g + 1) * WIDE)

        def back_field(f, carry):
            for when, line in hooks:
                pl.when(f == when)(functools.partial(run, line))
            dacc[...] = jnp.zeros_like(dacc)
            for r in range(R):
                tok = pl.ds(pl.multiple_of(f * TF + r * C, C), C)
                win = slice(r * C, (r + 3) * C)
                qd = widened(qb[tok, lanes])
                dod = widened(gctx[tok, lanes])
                k = kv[f, win, lanes]
                p = pt[f, g * R + r]
                dp = dot(kv[f, win, vlanes], dod, NT)
                wide = p.astype(F32)
                pd = wide * dp
                ds = ((pd - wide * row_sums(pd)) * SCALE).astype(BF)
                dq[g, tok, 0:WIDE] = diagonal(dot(ds, k, TN)).astype(BF)
                dacc[win, 0:WIDE] += dot(ds, qd)
                dacc[win, WIDE:] += dot(p, dod)
            hsend[g, 0, f] = dacc[0:C, :].astype(BF)
            hsend[g, 1, f] = dacc[TF + C :, :].astype(BF)
            edge[0, f] = dacc[C : 2 * C, :]
            edge[1, f] = dacc[TF : TF + C, :]
            if R > 2:
                mid = pl.ds(pl.multiple_of(f * TF + C, C), TF - 2 * C)
                dq[g, mid, WIDE:] = dacc[2 * C : TF, :].astype(BF)
            return carry

        lax.fori_loop(0, FD, back_field, 0)
        to_up = remote(hsend.at[g, 0], hrecv.at[g, 1], back_s.at[g, 0], back_r.at[g, 1], up)
        to_dn = remote(hsend.at[g, 1], hrecv.at[g, 0], back_s.at[g, 1], back_r.at[g, 0], down)
        pl.when(has_up)(to_up.start)
        pl.when(has_down)(to_dn.start)
        return to_up, to_dn

    def back_edges(g, to_up, to_dn):
        pl.when(has_up)(to_dn.wait_recv)
        pl.when(has_down)(to_up.wait_recv)
        for side, ok, row in ((0, has_up, 0), (1, has_down, R - 1)):

            def add(f, carry, side=side, ok=ok, row=row):
                tok = pl.ds(pl.multiple_of(f * TF + row * C, C), C)
                more = jnp.where(ok, hrecv[g, side, f].astype(F32), 0.0)
                dq[g, tok, WIDE:] = (edge[side, f] + more).astype(BF)
                return carry

            lax.fori_loop(0, FD, add, 0)

    half = FD // 2
    copies = []
    for g in range(2):
        if g == 0:
            hooks = [(0, order[0]), (half, order[1])]
        else:
            hooks = [(0, order[3]), (half, order[4])]
        pairs = back_group(g, hooks)
        copies += pairs
        back_edges(g, *pairs)
        put(pj + 1 + g, 0, dot(normed[...], dq[g], TN))
        if g == 0:
            run(order[2])
            rs_pair(pj + 1)
            rs_lat(pj + 1)
        else:
            rs_pair(pj + 2)
            run(order[5])
            rs_z(pj + 1)
            rs_lat(pj + 2)

    def last_tile(f, carry):
        dg, db = carry
        tok = pl.ds(pl.multiple_of(f * TF, TF), TF)
        e = None
        for g in range(2):
            for j in range(3):
                w = wq[:, j * D + g * WIDE : j * D + (g + 1) * WIDE]
                term = dot(dq[g, tok, j * WIDE : (j + 1) * WIDE], w, NT)
                e = term if e is None else e + term
        n, rstd = normalize(pb[f].astype(F32))
        acco[tok, :] = res[tok, :] + norm_pull(e, ga, n, rstd)
        return dg + row_sums(e * n), db + row_sums(e)

    attn_gain, attn_bias = lax.fori_loop(0, FD, last_tile, (zero, zero))
    patch_copy = pltpu.make_async_copy(acco, out_patch, out_sem.at[1])
    patch_copy.start()
    vec[...] = jnp.concatenate([attn_gain, attn_bias, mlp_gain, mlp_bias, zero, zero, zero, zero], axis=0)

    def vec_send(buf, slot, peers, i):
        buf[slot] = vec[...]
        for dev in peers:
            remote(vec, buf.at[slot], v_s.at[i], v_r.at[i], dev).start()

    def vec_sum(buf, count, i):
        arrived(buf.at[pl.ds(0, count - 1)], v_r.at[i])
        arrived(buf.at[pl.ds(0, count - 1)], v_s.at[i])
        total = buf[0]
        for k in range(1, count):
            total = total + buf[k]
        vec[...] = total

    vec_send(vrz, z, z_peers, 0)
    run(order[6])
    ag_z(pj + 1)
    rs_z(pj + 2)
    vec_sum(vrz, Z, 0)
    vec_send(vrx, lat, lat_peers, 1)
    ag_lat(pj + 1)
    ag_z(pj + 2)
    vec_sum(vrx, L, 1)
    vec_send(vrc, core, [pair], 2)
    ag_pair(pj + 1)
    ag_lat(pj + 2)
    vec_sum(vrc, 2, 2)
    ag_out(pj + 1)
    ag_pair(pj + 2)
    vec_copy = pltpu.make_async_copy(vec, out_vec, in_sem.at[0])
    vec_copy.start()
    ag_out(pj + 2)

    pl.when(has_up)(halo_up.wait_send)
    pl.when(has_down)(halo_dn.wait_send)
    for to_up, to_dn in (copies[0:2], copies[2:4]):
        pl.when(has_up)(to_up.wait_send)
        pl.when(has_down)(to_dn.wait_send)
    layer_copy.wait()
    patch_copy.wait()
    vec_copy.wait()
    for p in range(np_):
        finish(p)


def widen(plan, *refs):
    pn = plan
    np_ = len(pn.sizes)
    ag, vec, layer, patch = refs[:np_], refs[np_], refs[np_ + 1], refs[np_ + 2]
    o_layer, o_patch, o_ag, o_ab, o_qkv, o_proj, o_mg, o_mb, o_hid, o_out = refs[np_ + 3 : np_ + 13]
    sc = list(refs[np_ + 13 :])
    low, wide = sc[:np_], sc[np_ : 2 * np_]
    in_sem, out_sem, pass_sem = sc[2 * np_ :]
    D = pn.width
    loads = [pltpu.make_async_copy(ag[p], low[p], in_sem.at[p]) for p in range(np_)]
    for c in loads:
        c.start()
    through = [
        pltpu.make_async_copy(layer, o_layer, pass_sem.at[0]),
        pltpu.make_async_copy(patch, o_patch, pass_sem.at[1]),
    ]
    for c in through:
        c.start()
    for i, o in enumerate((o_ag, o_ab, o_mg, o_mb)):
        o[...] = vec[i : i + 1, :].reshape(D)
    stores = []

    def store(src, dst):
        c = pltpu.make_async_copy(src, dst, out_sem.at[len(stores)])
        c.start()
        stores.append(c)

    def spread(p, start, rows, blocks, col):
        for j in range(blocks):
            wide[p][:, col + j * 128 : col + (j + 1) * 128] = low[p][
                start + j * rows : start + (j + 1) * rows, :
            ].astype(F32)

    for p in range(np_):
        loads[p].wait()
        if p < pn.chunks:
            spread(p, 0, CHUNK, D // 128, 0)
            store(wide[p].at[:, pl.ds(0, D)], o_out.at[pl.ds(p * CHUNK, CHUNK)])
            spread(p, CHUNK * (D // 128), D, CHUNK // 128, D)
            store(wide[p].at[:, pl.ds(D, CHUNK)], o_hid.at[:, pl.ds(p * CHUNK, CHUNK)])
        elif p == pn.chunks:
            spread(p, 0, D, D // 128, 0)
            store(wide[p], o_proj)
        else:
            g = p - pn.chunks - 1
            spread(p, 0, D, 3 * WIDE // 128, 0)
            for j in range(3):
                store(
                    wide[p].at[:, pl.ds(j * WIDE, WIDE)],
                    o_qkv.at[:, pl.ds(j * D + g * WIDE, WIDE)],
                )
    for c in stores + through:
        c.wait()


def per_device(mesh, patches, segment_ids, gain_attn, bias_attn, w_qkv, w_proj, gain_mlp, bias_mlp, w_hidden, w_output, cotangent):
    fields, rows, cols, width = patches.shape
    ff = w_hidden.shape[1]
    pn = Plan(mesh, fields, rows, cols, width, ff)
    np_ = len(pn.sizes)
    T, TF, D, C, R, FD = pn.tokens, pn.tf, width, cols, rows, fields
    L, Z = pn.lats, pn.zs
    anywhere = pl.BlockSpec(memory_space=pl.ANY)
    vmem = pl.BlockSpec(memory_space=pltpu.VMEM)
    V = pltpu.VMEM
    dma = pltpu.SemaphoreType.DMA
    scratch = [
        V((D, 3 * D), BF), V((D, D), BF), V((D, ff), BF), V((ff, D), BF),
        V((FD, TF, D), BF), V((T, D), BF), V(segment_ids.shape, jnp.int32), V((2, FD, C, D), BF),
        V((T, D), BF), V((T, D), BF), V((FD, TF + 2 * C, 2 * D), BF), V((FD, 2 * R, 3 * C, WIDE), BF),
        V((T, D), BF), V((T, D), F32), V((T, D), BF), V((T, D), F32), V((T, D), F32),
        V((T, CHUNK), BF), V((T, CHUNK), BF), V((T, D), BF), V((2, T, 3 * WIDE), BF),
        V((TF + 2 * C, 2 * WIDE), F32), V((2, FD, C, 2 * WIDE), F32),
        V((2, 2, FD, C, 2 * WIDE), BF), V((2, 2, FD, C, 2 * WIDE), BF),
        V((WIDE, WIDE), BF), V((WIDE, WIDE), F32), V((FD, C, WIDE), F32),
        V((8, D), F32), V((Z, 8, D), F32), V((L, 8, D), F32), V((2, 8, D), F32),
    ]
    scratch += [V((n, 128), BF) for n in pn.sizes]
    scratch += [V((n // 2, 128), BF) for n in pn.sizes]
    scratch += [V((L - 1, n // 2 // L, 128), BF) for n in pn.sizes]
    scratch += [V((Z - 1, n // 2 // L // Z, 128), BF) for n in pn.sizes]
    scratch += [V((n, 128), BF) for n in pn.sizes]
    scratch += [
        dma((7,)), dma((2 + np_,)), dma((2,)), dma((2,)), dma((2, 2)), dma((2, 2)),
        dma((np_, 6)), dma((np_, 6)), dma((3,)), dma((3,)),
    ]
    shape = jax.ShapeDtypeStruct
    outs = pl.pallas_call(
        functools.partial(body, pn),
        out_shape=[shape((T, D), BF), shape((T, D), F32), shape((8, D), F32)]
        + [shape((n, 128), BF) for n in pn.sizes],
        in_specs=[anywhere, anywhere, vmem, vmem, anywhere, anywhere, vmem, vmem, anywhere, anywhere, anywhere],
        out_specs=[anywhere] * (3 + np_),
        scratch_shapes=scratch,
        compiler_params=pltpu.CompilerParams(
            collective_id=0, has_side_effects=True, vmem_limit_bytes=62 * 2**20
        ),
        name="block",
    )(
        patches.reshape(FD, TF, D), segment_ids, gain_attn, bias_attn, w_qkv, w_proj, gain_mlp, bias_mlp,
        w_hidden, w_output, cotangent.reshape(T, D),
    )
    layer, patch, vec = outs[:3]
    ags = outs[3:]
    wides = [(D, D + CHUNK)] * pn.chunks + [(D, D)] + [(D, 3 * WIDE)] * 2
    final = pl.pallas_call(
        functools.partial(widen, pn),
        out_shape=[
            shape((T, D), BF), shape((T, D), F32), shape((D,), F32), shape((D,), F32), shape((D, 3 * D), F32),
            shape((D, D), F32), shape((D,), F32), shape((D,), F32), shape((D, ff), F32), shape((ff, D), F32),
        ],
        in_specs=[anywhere] * np_ + [vmem, anywhere, anywhere],
        out_specs=[anywhere, anywhere, vmem, vmem, anywhere, anywhere, vmem, vmem, anywhere, anywhere],
        scratch_shapes=[V((n, 128), BF) for n in pn.sizes]
        + [V(s, F32) for s in wides]
        + [dma((np_,)), dma((2 * pn.chunks + 7,)), dma((2,))],
        compiler_params=pltpu.CompilerParams(vmem_limit_bytes=40 * 2**20),
        name="widen",
    )(*ags, vec, layer, patch)
    block = (FD, R, C, D)
    return (final[0].reshape(block), final[1].reshape(block)) + tuple(final[2:])


def solution(mesh):
    band = P("fld", "lat", None, None)
    return jax.shard_map(
        functools.partial(per_device, mesh),
        mesh=mesh,
        in_specs=(band, P("fld", None, None)) + (P(),) * 8 + (band,),
        out_specs=(band, band) + (P(),) * 8,
        check_vma=False,
    )
```

```python
import functools
import math

import jax
import jax.numpy as jnp
from jax import lax
from jax.experimental import pallas as pl
from jax.experimental.pallas import tpu as pltpu
from jax.sharding import PartitionSpec as P

HEAD_DIM = 32
GROUP = 8
WIDE = GROUP * HEAD_DIM
SCALE = HEAD_DIM ** -0.5
LOG2E = math.log2(math.e)
EPS = 1e-6
REACH = 4
NEG = -1e30
CHUNK = 512
BF = jnp.bfloat16
F32 = jnp.float32
MESH = pl.DeviceIdType.MESH

NT = (((1,), (1,)), ((), ()))
TN = (((0,), (0,)), ((), ()))


def dot(a, b, dims=None):
    if dims is None:
        return jnp.dot(a, b, preferred_element_type=F32)
    return lax.dot_general(a, b, dims, preferred_element_type=F32)


def normalize(x):
    center = jnp.mean(x, axis=-1, keepdims=True)
    off = x - center
    rstd = lax.rsqrt(jnp.mean(off * off, axis=-1, keepdims=True) + EPS)
    return off * rstd, rstd


def norm_pull(e, gain, n, rstd):
    ge = e * gain
    a = jnp.mean(ge, axis=-1, keepdims=True)
    b = jnp.mean(ge * n, axis=-1, keepdims=True)
    return (ge - a - n * b) * rstd


def gelu_both(u):
    z = jnp.abs(u) * (1.0 / math.sqrt(2.0))
    t = 1.0 / (1.0 + 0.3275911 * z)
    ex = jnp.exp2((u * u) * (-0.5 * LOG2E))
    poly = t * (0.254829592 + t * (-0.284496736 + t * (1.421413741 + t * (-1.453152027 + t * 1.061405429))))
    half = 0.5 * poly * ex
    cdf = jnp.where(u < 0, half, 1.0 - half)
    return u * cdf, cdf + u * (ex * (1.0 / math.sqrt(2.0 * math.pi)))


def row_sums(x):
    return jnp.sum(x, axis=0, keepdims=True)


class Plan:
    def __init__(self, mesh, fields, rows, cols, width, ff):
        self.lats = mesh.shape["lat"]
        self.flds = mesh.shape["fld"]
        self.zs = self.flds // 2
        self.fields, self.rows, self.cols = fields, rows, cols
        self.tf = rows * cols
        self.tokens = fields * self.tf
        self.width, self.ff = width, ff
        self.chunks = ff // CHUNK
        self.size_of = {"core": 2, "x": 2, "y": self.lats // 2, "lat": self.lats, "z": self.zs}
        unit = 16 * self.lats * self.flds
        blocks = width // 128
        mlp = CHUNK * blocks + width * (CHUNK // 128)
        rows_needed = [mlp] * self.chunks + [width * blocks] + [width * (3 * WIDE // 128)] * 2
        self.sizes, self.subs = [], []
        for p, n in enumerate(rows_needed):
            n = -(-n // unit) * unit
            self.sizes.append(n)
            last = p >= len(rows_needed) - 1
            if last or n % (2 * unit):
                self.subs.append([(0, n, ("core", "lat", "z"))])
            else:
                self.subs.append([(0, n // 2, ("core", "x", "y", "z")), (n // 2, n // 2, ("core", "y", "x", "z"))])
        self.landing = []
        for subs in self.subs:
            total = 0
            for _, n, order in subs:
                for d in order:
                    n //= self.size_of[d]
                    total += n * (self.size_of[d] - 1)
            self.landing.append(total)
        self.n_subs = sum(len(s) for s in self.subs)


def body(plan, *refs):
    pn = plan
    np_ = len(pn.sizes)
    (patches, seg, gain_a, bias_a, w_qkv, w_proj, gain_m, bias_m, w_hid, w_out, cot) = refs[:11]
    out_layer, out_patch, out_vec = refs[11:14]
    out_ag = refs[14 : 14 + np_]
    sc = list(refs[14 + np_ :])

    def take(n):
        got = sc[:n]
        del sc[:n]
        return got

    wq, wp, wh, wo = take(4)
    pb, cb, segv, halo = take(4)
    normed, qb, kv, pt, ctx, res, nm, gres, act, gpre, gctx, dq, dacc, edge = take(14)
    hq, hg, lse, hlse, dst, hdst = take(6)
    bm, bmf, biasb, vec, vrz, vrx, vrc = take(7)
    sb, rb, ag = take(np_), take(np_), take(np_)
    in_sem, out_sem, halo_s, halo_r, back_s, back_r, rs_s, rs_r, v_s, v_r = take(10)

    lat = lax.axis_index("lat")
    fld = lax.axis_index("fld")
    core = lax.rem(fld, 2)
    z = lax.div(fld, 2)
    x = lax.rem(lat, 2)
    y = lax.div(lat, 2)
    L, Z, Y = pn.lats, pn.zs, pn.lats // 2
    FD, R, C, TF, T, D, FF = pn.fields, pn.rows, pn.cols, pn.tf, pn.tokens, pn.width, pn.ff

    ins = [(patches, pb), (w_qkv, wq), (seg, segv), (w_proj, wp), (cot, cb), (w_hid, wh), (w_out, wo)]
    loads = [pltpu.make_async_copy(s, d, in_sem.at[i]) for i, (s, d) in enumerate(ins)]
    for c in loads:
        c.start()

    me = {"core": core, "x": x, "y": y, "lat": lat, "z": z}

    def device(d, i):
        if d == "core":
            return lat, z * 2 + i
        if d == "x":
            return y * 2 + i, fld
        if d == "y":
            return i * 2 + x, fld
        if d == "lat":
            return i, fld
        return lat, i * 2 + core

    def peers(d):
        n = pn.size_of[d]
        places = [lax.rem(me[d] + k, n) for k in range(1, n)]
        return [(i, device(d, i)) for i in places]

    barrier = pltpu.get_barrier_semaphore()
    everyone = peers("core") + peers("lat") + peers("z")
    for _, dev in everyone:
        pl.semaphore_signal(barrier, inc=1, device_id=dev, device_id_type=MESH)
    pl.semaphore_wait(barrier, len(everyone))

    up, down = (lat - 1, fld), (lat + 1, fld)
    has_up, has_down = lat > 0, lat < L - 1

    def remote(src, dst, s, r, dev):
        return pltpu.make_async_remote_copy(
            src_ref=src, dst_ref=dst, send_sem=s, recv_sem=r, device_id=dev, device_id_type=MESH
        )

    def arrived(ref, sem):
        pltpu.make_async_copy(ref, ref, sem).wait()

    halo_up = remote(patches.at[:, pl.ds(0, C)], halo.at[1], halo_s.at[0], halo_r.at[1], up)
    halo_dn = remote(patches.at[:, pl.ds(TF - C, C)], halo.at[0], halo_s.at[1], halo_r.at[0], down)
    pl.when(has_up)(halo_up.start)
    pl.when(has_down)(halo_dn.start)

    def spot(off, n):
        return pl.ds(pl.multiple_of(off, 16), n)

    class Part:
        def __init__(self, p, number, start, n, order, land):
            self.p, self.number, self.order = p, number, order
            self.off, self.len, self.land = [start], [n], []
            for d in order:
                g = pn.size_of[d]
                n = n // g
                self.land.append(land)
                land += n * (g - 1)
                self.off.append(self.off[-1] + me[d] * n)
                self.len.append(n)
            self.end = land

        def moved(self, i):
            return self.len[i + 1] * (pn.size_of[self.order[i]] - 1)

        def scatter(self, i):
            n = self.len[i + 1]
            for k, (j, dev) in enumerate(peers(self.order[i])):
                src = sb[self.p].at[spot(self.off[i] + j * n, n)]
                dst = rb[self.p].at[pl.ds(self.land[i] + k * n, n)]
                remote(src, dst, rs_s.at[self.number, i], rs_r.at[self.number, i], dev).start()

        def add(self, i):
            n = self.len[i + 1]
            d = self.order[i]
            arrived(rb[self.p].at[pl.ds(self.land[i], self.moved(i))], rs_r.at[self.number, i])
            mine = spot(self.off[i + 1], n)
            total = sb[self.p][mine, :].astype(F32)
            for k in range(pn.size_of[d] - 1):
                total = total + rb[self.p][self.land[i] + k * n : self.land[i] + (k + 1) * n, :].astype(F32)
            to = ag if i == len(self.order) - 1 else sb
            to[self.p][mine, :] = total.astype(BF)

        def gather(self, i):
            s = 4 + i
            mine = ag[self.p].at[spot(self.off[i + 1], self.len[i + 1])]
            for _, dev in peers(self.order[i]):
                remote(mine, mine, rs_s.at[self.number, s], rs_r.at[self.number, s], dev).start()

        def gathered(self, i):
            arrived(ag[self.p].at[pl.ds(0, self.moved(i))], rs_r.at[self.number, 4 + i])

        def step(self, s):
            nd = len(self.order)
            if s < nd:
                if s > 0:
                    self.add(s - 1)
                self.scatter(s)
            elif s == nd:
                self.add(nd - 1)
                self.gather(nd - 1)
            else:
                self.gathered(2 * nd - s)
                if s < 2 * nd:
                    self.gather(2 * nd - 1 - s)

        def finish(self):
            for i in range(len(self.order)):
                for s in (i, 4 + i):
                    arrived(sb[self.p].at[pl.ds(0, self.moved(i))], rs_s.at[self.number, s])

    parts, number = [], 0
    for p in range(np_):
        mine, land = [], 0
        for start, n, order in pn.subs[p]:
            mine.append(Part(p, number, start, n, order, land))
            land = mine[-1].end
            number += 1
        parts.append(mine)
    reached = [0] * np_
    last_step = [2 * len(m[0].order) for m in parts]

    def hook(*pieces):
        steps = []
        for p in pieces:
            if reached[p] <= last_step[p]:
                steps.append((p, reached[p]))
                reached[p] += 1

        def run():
            for p, s in steps:
                for part in parts[p]:
                    part.step(s)
                if s == last_step[p]:
                    pltpu.make_async_copy(ag[p], out_ag[p], out_sem.at[2 + p]).start()

        return run

    def advance(*pieces):
        hook(*pieces)()

    def finish(p):
        for part in parts[p]:
            part.finish()
        pltpu.make_async_copy(ag[p], out_ag[p], out_sem.at[2 + p]).wait()

    def put(p, start, value):
        rows, lanes = value.shape
        low = value.astype(BF)
        for j in range(lanes // 128):
            sb[p][start + j * rows : start + (j + 1) * rows, :] = low[:, j * 128 : (j + 1) * 128]

    rid = lax.broadcasted_iota(jnp.int32, (WIDE, WIDE), 0) // HEAD_DIM
    cid = lax.broadcasted_iota(jnp.int32, (WIDE, WIDE), 1) // HEAD_DIM
    same = jnp.where(rid == cid, 1.0, 0.0)
    bm[...] = same.astype(BF)
    bmf[...] = same

    ga, ba = gain_a[...].reshape(1, D), bias_a[...].reshape(1, D)
    gm, bmlp = gain_m[...].reshape(1, D), bias_m[...].reshape(1, D)
    loads[0].wait()

    def norm_one(f, carry):
        n, _ = normalize(pb[f].astype(F32))
        normed[pl.ds(pl.multiple_of(f * TF, TF), TF), :] = (n * ga + ba).astype(BF)
        return carry

    lax.fori_loop(0, FD, norm_one, 0)
    loads[1].wait()
    qb[...] = dot(normed[...], wq[:, :D]).astype(BF)
    for j in range(2):
        part = dot(normed[...], wq[:, (j + 1) * D : (j + 2) * D]).astype(BF)
        kv[:, C : C + TF, j * D : (j + 1) * D] = part.reshape(FD, TF, D)

    loads[2].wait()
    kcol = lax.broadcasted_iota(jnp.int32, (C, WIDE), 0)
    qcol = lax.rem(lax.broadcasted_iota(jnp.int32, (C, WIDE), 1), C)
    away = jnp.abs(kcol - qcol)
    near = jnp.minimum(away, C - away) <= REACH
    diag = lax.broadcasted_iota(jnp.int32, (C, C), 0) == lax.broadcasted_iota(jnp.int32, (C, C), 1)
    for f in range(FD):
        line = segv[f, 0:1, :].astype(F32)
        across = jnp.concatenate([line] * GROUP, axis=1)
        along = jnp.sum(jnp.where(diag, line, 0.0), axis=1, keepdims=True)
        biasb[f] = jnp.where(jnp.logical_and(near, along == across), 0.0, NEG)
    pole_top = jnp.where(has_up, 0.0, NEG)
    pole_bottom = jnp.where(has_down, 0.0, NEG)

    def diagonal(o):
        o = o * bmf[...]
        total = o[0:HEAD_DIM]
        for h in range(1, GROUP):
            total = total + o[h * HEAD_DIM : (h + 1) * HEAD_DIM]
        return total

    def widened(q):
        return jnp.concatenate([q] * GROUP, axis=0) * bm[...]

    def attend(rows, f, carry):
        bias = biasb[f]
        for g in range(2):
            lanes = slice(g * WIDE, (g + 1) * WIDE)
            vlanes = slice(D + g * WIDE, D + (g + 1) * WIDE)
            for r in rows:
                tok = pl.ds(pl.multiple_of(f * TF + r * C, C), C)
                win = slice(r * C, (r + 3) * C)
                s = dot(kv[f, win, lanes], widened(qb[tok, lanes]), NT)
                top = bias + pole_top if r == 0 else bias
                low = bias + pole_bottom if r == R - 1 else bias
                s = s + jnp.concatenate([top, bias, low], axis=0)
                m = jnp.max(s, axis=0, keepdims=True)
                p = jnp.exp2((s - m) * (SCALE * LOG2E))
                total = row_sums(p)
                if r == 0 or r == R - 1:
                    lse[0 if r == 0 else 1, pl.ds(f * 2 + g, 1), :] = m * (SCALE * LOG2E) + jnp.log2(total)
                p = (p * (1.0 / total)).astype(BF)
                pt[f, g * R + r] = p
                ctx[tok, lanes] = diagonal(dot(p, kv[f, win, vlanes], TN)).astype(BF)
        return carry

    if R > 2:
        lax.fori_loop(0, FD, functools.partial(attend, range(1, R - 1)), 0)

    for side, ok, copy in ((0, has_up, halo_dn), (1, has_down, halo_up)):
        pl.when(ok)(copy.wait_recv)

        @pl.when(jnp.logical_not(ok))
        def _():
            halo[side] = jnp.zeros((FD, C, D), BF)

        n, _unused = normalize(halo[side].reshape(FD * C, D).astype(F32))
        low = (n * ga + ba).astype(BF)
        hq[side] = dot(low, wq[:, :D]).astype(BF)
        edge_kv = dot(low, wq[:, D:]).astype(BF).reshape(FD, C, 2 * D)
        start = 0 if side == 0 else TF + C
        kv[:, start : start + C, :] = edge_kv

    lax.fori_loop(0, FD, functools.partial(attend, (0, R - 1)), 0)

    loads[3].wait()
    per = max(1, 256 // TF)
    tile = per * TF

    def project(t, carry):
        tok = pl.ds(pl.multiple_of(t * tile, tile), tile)
        r = pb[pl.ds(t * per, per)].reshape(tile, D).astype(F32) + dot(ctx[tok, :], wp[...])
        res[tok, :] = r
        n, _ = normalize(r)
        nm[tok, :] = (n * gm + bmlp).astype(BF)
        return carry

    lax.fori_loop(0, T // tile, project, 0)

    for i in (4, 5, 6):
        loads[i].wait()
    mid = (T // tile) // 2
    mids = [(), (0,), (0, 1), (0, 1, 2)]
    ends = [(0,), (1,), (0, 2), (0, 1, 3)]
    for c in range(pn.chunks):
        cs = slice(c * CHUNK, (c + 1) * CHUNK)

        meanwhile = hook(*mids[c])

        def mlp_tile(t, carry, cs=cs, meanwhile=meanwhile):
            pl.when(t == mid)(meanwhile)
            tok = pl.ds(pl.multiple_of(t * tile, tile), tile)
            hidden = dot(nm[tok, :], wh[:, cs])
            back = dot(cb[tok, :], wo[cs, :], NT)
            a, da = gelu_both(hidden)
            act[tok, cs] = a.astype(BF)
            gpre[tok, cs] = (da * back).astype(BF)
            return carry

        lax.fori_loop(0, T // tile, mlp_tile, 0)
        put(c, 0, dot(act[:, cs], cb[...], TN))
        put(c, CHUNK * (D // 128), dot(nm[...], gpre[:, cs], TN))
        advance(*ends[c])

    zero = jnp.zeros((1, D), F32)

    def mlp_end(t, carry):
        dg, db = carry
        tok = pl.ds(pl.multiple_of(t * tile, tile), tile)
        e = dot(gpre[tok, :], wh[...], NT)
        n, rstd = normalize(res[tok, :])
        gr = cb[tok, :].astype(F32) + norm_pull(e, gm, n, rstd)
        gres[tok, :] = gr
        low = gr.astype(BF)
        nm[tok, :] = low
        gctx[pl.ds(t * per, per)] = dot(low, wp[...], NT).astype(BF).reshape(per, TF, D)
        return dg + row_sums(e * n), db + row_sums(e)

    mlp_gain, mlp_bias = lax.fori_loop(0, T // tile, mlp_end, (zero, zero))
    pj = pn.chunks
    g_up = remote(gctx.at[:, pl.ds(0, C)], hg.at[1], back_s.at[0], back_r.at[1], up)
    g_dn = remote(gctx.at[:, pl.ds(TF - C, C)], hg.at[0], back_s.at[1], back_r.at[0], down)
    l_up = remote(lse.at[0], hlse.at[1], back_s.at[2], back_r.at[3], up)
    l_dn = remote(lse.at[1], hlse.at[0], back_s.at[3], back_r.at[2], down)
    for to_up, to_dn in ((g_up, g_dn), (l_up, l_dn)):
        pl.when(has_up)(to_up.start)
        pl.when(has_down)(to_dn.start)
    advance(1, 2)
    put(pj, 0, dot(ctx[...], nm[...], TN))
    advance(0, 3, pj)

    def back_group(g, hooks):
        lanes = slice(g * WIDE, (g + 1) * WIDE)
        vlanes = slice(D + g * WIDE, D + (g + 1) * WIDE)

        def back_field(f, carry):
            for when, do in hooks.items():
                pl.when(f == when)(do)
            dacc[...] = jnp.zeros_like(dacc)
            for r in range(R):
                tok = pl.ds(pl.multiple_of(f * TF + r * C, C), C)
                win = slice(r * C, (r + 3) * C)
                qd = widened(qb[tok, lanes])
                dod = widened(gctx[f, r * C : (r + 1) * C, lanes])
                k = kv[f, win, lanes]
                p = pt[f, g * R + r]
                dp = dot(kv[f, win, vlanes], dod, NT)
                wide = p.astype(F32)
                pd = wide * dp
                total = row_sums(pd)
                if r == 0 or r == R - 1:
                    dst[g, 0 if r == 0 else 1, pl.ds(f, 1), :] = total
                ds = ((pd - wide * total) * SCALE).astype(BF)
                dq[g, tok, 0:WIDE] = diagonal(dot(ds, k, TN)).astype(BF)
                dacc[win, 0:WIDE] += dot(ds, qd)
                dacc[win, WIDE:] += dot(p, dod)
            edge[g, 0, f] = dacc[C : 2 * C, :]
            edge[g, 1, f] = dacc[TF : TF + C, :]
            if R > 2:
                inner = pl.ds(pl.multiple_of(f * TF + C, C), TF - 2 * C)
                dq[g, inner, WIDE:] = dacc[2 * C : TF, :].astype(BF)
            return carry

        lax.fori_loop(0, FD, back_field, 0)
        to_up = remote(dst.at[g, 0], hdst.at[g, 1], back_s.at[4 + 2 * g], back_r.at[5 + 2 * g], up)
        to_dn = remote(dst.at[g, 1], hdst.at[g, 0], back_s.at[5 + 2 * g], back_r.at[4 + 2 * g], down)
        pl.when(has_up)(to_up.start)
        pl.when(has_down)(to_dn.start)
        return to_up, to_dn

    def back_edges(g, sent):
        lanes = slice(g * WIDE, (g + 1) * WIDE)
        vlanes = slice(D + g * WIDE, D + (g + 1) * WIDE)
        for to_up, to_dn in sent:
            pl.when(has_up)(to_dn.wait_recv)
            pl.when(has_down)(to_up.wait_recv)

        def one(f, carry):
            for side, ok, row in ((0, has_up, 0), (1, has_down, R - 1)):
                tok = pl.ds(pl.multiple_of(f * TF + row * C, C), C)
                keys = slice((row + 1) * C, (row + 2) * C)
                qd = widened(hq[side, pl.ds(pl.multiple_of(f * C, C), C), lanes])
                dod = widened(hg[side, f, :, lanes])
                s = dot(kv[f, keys, lanes], qd, NT) + biasb[f]
                p = jnp.exp2(s * (SCALE * LOG2E) - hlse[side, pl.ds(f * 2 + g, 1), :])
                p = jnp.where(ok, p, 0.0)
                dp = dot(kv[f, keys, vlanes], dod, NT)
                ds = p * (dp - hdst[g, side, pl.ds(f, 1), :]) * SCALE
                ds = jnp.where(ok, ds, 0.0).astype(BF)
                dk = edge[g, side, f, :, 0:WIDE] + jnp.where(ok, dot(ds, qd), 0.0)
                dv = edge[g, side, f, :, WIDE:] + jnp.where(ok, dot(p.astype(BF), dod), 0.0)
                dq[g, tok, WIDE : 2 * WIDE] = dk.astype(BF)
                dq[g, tok, 2 * WIDE :] = dv.astype(BF)
            return carry

        lax.fori_loop(0, FD, one, 0)
        put(pj + 1 + g, 0, dot(normed[...], dq[g], TN))

    every = list(range(pj + 1))
    sent0 = back_group(0, {1: hook(1, 2), 3: hook(0, 3, pj), 5: hook(1, 2), 7: hook(0, 3, pj)})

    early = {0: hook(1, 2), 2: hook(0, 3, pj)}
    start_first = hook(pj + 1)

    def first_edges():
        back_edges(0, ((g_up, g_dn), (l_up, l_dn), sent0))
        start_first()

    sent1 = back_group(1, early | {4: first_edges, 5: hook(1, 2, pj + 1), 6: hook(3, pj), 7: hook(2, pj)})
    advance(3, pj + 1)
    back_edges(1, (sent1,))
    advance(pj + 2)
    advance(pj + 1, *every)

    def out_tile(t, carry):
        tok = pl.ds(pl.multiple_of(t * tile, tile), tile)
        nm[tok, :] = (res[tok, :] + dot(act[tok, :], wo[...])).astype(BF)
        return carry

    lax.fori_loop(0, T // tile, out_tile, 0)
    layer_copy = pltpu.make_async_copy(nm, out_layer, out_sem.at[0])
    layer_copy.start()
    advance(pj + 2)
    advance(pj + 1, *every)

    def last_tile(t, carry):
        dg, db = carry
        tok = pl.ds(pl.multiple_of(t * tile, tile), tile)
        e = None
        for g in range(2):
            for j in range(3):
                w = wq[:, j * D + g * WIDE : j * D + (g + 1) * WIDE]
                term = dot(dq[g, tok, j * WIDE : (j + 1) * WIDE], w, NT)
                e = term if e is None else e + term
        n, rstd = normalize(pb[pl.ds(t * per, per)].reshape(tile, D).astype(F32))
        gres[tok, :] += norm_pull(e, ga, n, rstd)
        return dg + row_sums(e * n), db + row_sums(e)

    attn_gain, attn_bias = lax.fori_loop(0, T // tile, last_tile, (zero, zero))
    patch_copy = pltpu.make_async_copy(gres, out_patch, out_sem.at[1])
    patch_copy.start()
    vec[...] = jnp.concatenate([attn_gain, attn_bias, mlp_gain, mlp_bias, zero, zero, zero, zero], axis=0)

    def vec_send(buf, d, i):
        buf[me[d]] = vec[...]
        for _, dev in peers(d):
            remote(vec, buf.at[me[d]], v_s.at[i], v_r.at[i], dev).start()

    def vec_sum(buf, d, i):
        count = pn.size_of[d]
        arrived(buf.at[pl.ds(0, count - 1)], v_r.at[i])
        arrived(buf.at[pl.ds(0, count - 1)], v_s.at[i])
        total = buf[0]
        for k in range(1, count):
            total = total + buf[k]
        vec[...] = total

    vec_send(vrz, "z", 0)
    advance(pj + 2)
    advance(pj + 1, *every)
    vec_sum(vrz, "z", 0)
    vec_send(vrx, "lat", 1)
    advance(pj + 2)
    advance(pj + 1, *every)
    vec_sum(vrx, "lat", 1)
    vec_send(vrc, "core", 2)
    advance(pj + 2)
    advance(pj + 1, *every)
    vec_sum(vrc, "core", 2)
    vec_copy = pltpu.make_async_copy(vec, out_vec, in_sem.at[0])
    vec_copy.start()
    for p in range(np_):
        while reached[p] <= last_step[p]:
            advance(p)

    pl.when(has_up)(halo_up.wait_send)
    pl.when(has_down)(halo_dn.wait_send)
    for to_up, to_dn in ((g_up, g_dn), (l_up, l_dn), sent0, sent1):
        pl.when(has_up)(to_up.wait_send)
        pl.when(has_down)(to_dn.wait_send)
    layer_copy.wait()
    patch_copy.wait()
    vec_copy.wait()
    for p in range(np_):
        finish(p)


def widen(plan, *refs):
    pn = plan
    np_ = len(pn.sizes)
    ag, vec, layer, patch = refs[:np_], refs[np_], refs[np_ + 1], refs[np_ + 2]
    o_layer, o_patch, o_ag, o_ab, o_qkv, o_proj, o_mg, o_mb, o_hid, o_out = refs[np_ + 3 : np_ + 13]
    sc = list(refs[np_ + 13 :])
    low, wide = sc[:np_], sc[np_ : 2 * np_]
    kept_layer, kept_patch, in_sem, out_sem, pass_sem = sc[2 * np_ :]
    D = pn.width
    loads = [pltpu.make_async_copy(ag[p], low[p], in_sem.at[p]) for p in range(np_)]
    for c in loads:
        c.start()
    through = [
        (pltpu.make_async_copy(a, b, pass_sem.at[2 * i]), pltpu.make_async_copy(b, c, pass_sem.at[2 * i + 1]))
        for i, (a, b, c) in enumerate(((layer, kept_layer, o_layer), (patch, kept_patch, o_patch)))
    ]
    for arrive, _ in through:
        arrive.start()
    for i, o in enumerate((o_ag, o_ab, o_mg, o_mb)):
        o[...] = vec[i : i + 1, :].reshape(D)
    stores = []

    def store(src, dst):
        c = pltpu.make_async_copy(src, dst, out_sem.at[len(stores)])
        c.start()
        stores.append(c)

    def spread(p, start, rows, blocks, col):
        for j in range(blocks):
            wide[p][:, col + j * 128 : col + (j + 1) * 128] = low[p][
                start + j * rows : start + (j + 1) * rows, :
            ].astype(F32)

    for p in range(np_):
        loads[p].wait()
        if p == np_ - 1:
            for arrive, leave in through:
                arrive.wait()
                leave.start()
        if p < pn.chunks:
            spread(p, 0, CHUNK, D // 128, 0)
            store(wide[p].at[:, pl.ds(0, D)], o_out.at[pl.ds(p * CHUNK, CHUNK)])
            spread(p, CHUNK * (D // 128), D, CHUNK // 128, D)
            store(wide[p].at[:, pl.ds(D, CHUNK)], o_hid.at[:, pl.ds(p * CHUNK, CHUNK)])
        elif p == pn.chunks:
            spread(p, 0, D, D // 128, 0)
            store(wide[p], o_proj)
        else:
            g = p - pn.chunks - 1
            spread(p, 0, D, 3 * WIDE // 128, 0)
            for j in range(3):
                store(
                    wide[p].at[:, pl.ds(j * WIDE, WIDE)],
                    o_qkv.at[:, pl.ds(j * D + g * WIDE, WIDE)],
                )
    for c in stores + [leave for _, leave in through]:
        c.wait()


def per_device(mesh, patches, segment_ids, gain_attn, bias_attn, w_qkv, w_proj, gain_mlp, bias_mlp, w_hidden, w_output, cotangent):
    fields, rows, cols, width = patches.shape
    ff = w_hidden.shape[1]
    pn = Plan(mesh, fields, rows, cols, width, ff)
    np_ = len(pn.sizes)
    T, TF, D, C, R, FD = pn.tokens, pn.tf, width, cols, rows, fields
    L, Z = pn.lats, pn.zs
    anywhere = pl.BlockSpec(memory_space=pl.ANY)
    vmem = pl.BlockSpec(memory_space=pltpu.VMEM)
    V = pltpu.VMEM
    dma = pltpu.SemaphoreType.DMA
    scratch = [
        V((D, 3 * D), BF), V((D, D), BF), V((D, ff), BF), V((ff, D), BF),
        V((FD, TF, D), BF), V((T, D), BF), V(segment_ids.shape, jnp.int32), V((2, FD, C, D), BF),
        V((T, D), BF), V((T, D), BF), V((FD, TF + 2 * C, 2 * D), BF), V((FD, 2 * R, 3 * C, WIDE), BF),
        V((T, D), BF), V((T, D), F32), V((T, D), BF), V((T, D), F32),
        V((T, ff), BF), V((T, ff), BF), V((FD, TF, D), BF), V((2, T, 3 * WIDE), BF),
        V((TF + 2 * C, 2 * WIDE), F32), V((2, 2, FD, C, 2 * WIDE), F32),
        V((2, FD * C, D), BF), V((2, FD, C, D), BF),
        V((2, 2 * FD, WIDE), F32), V((2, 2 * FD, WIDE), F32), V((2, 2, FD, WIDE), F32), V((2, 2, FD, WIDE), F32),
        V((WIDE, WIDE), BF), V((WIDE, WIDE), F32), V((FD, C, WIDE), F32),
        V((8, D), F32), V((Z, 8, D), F32), V((L, 8, D), F32), V((2, 8, D), F32),
    ]
    scratch += [V((n, 128), BF) for n in pn.sizes]
    scratch += [V((n, 128), BF) for n in pn.landing]
    scratch += [V((n, 128), BF) for n in pn.sizes]
    scratch += [
        dma((7,)), dma((2 + np_,)), dma((2,)), dma((2,)), dma((8,)), dma((8,)),
        dma((pn.n_subs, 8)), dma((pn.n_subs, 8)), dma((3,)), dma((3,)),
    ]
    shape = jax.ShapeDtypeStruct
    outs = pl.pallas_call(
        functools.partial(body, pn),
        out_shape=[shape((T, D), BF), shape((T, D), F32), shape((8, D), F32)]
        + [shape((n, 128), BF) for n in pn.sizes],
        in_specs=[anywhere, anywhere, vmem, vmem, anywhere, anywhere, vmem, vmem, anywhere, anywhere, anywhere],
        out_specs=[anywhere] * (3 + np_),
        scratch_shapes=scratch,
        compiler_params=pltpu.CompilerParams(
            collective_id=0, has_side_effects=True, vmem_limit_bytes=62 * 2**20
        ),
        name="block",
    )(
        patches.reshape(FD, TF, D), segment_ids, gain_attn, bias_attn, w_qkv, w_proj, gain_mlp, bias_mlp,
        w_hidden, w_output, cotangent.reshape(T, D),
    )
    layer, patch, vec = outs[:3]
    ags = outs[3:]
    wides = [(D, D + CHUNK)] * pn.chunks + [(D, D)] + [(D, 3 * WIDE)] * 2
    final = pl.pallas_call(
        functools.partial(widen, pn),
        out_shape=[
            shape((T, D), BF), shape((T, D), F32), shape((D,), F32), shape((D,), F32), shape((D, 3 * D), F32),
            shape((D, D), F32), shape((D,), F32), shape((D,), F32), shape((D, ff), F32), shape((ff, D), F32),
        ],
        in_specs=[anywhere] * np_ + [vmem, anywhere, anywhere],
        out_specs=[anywhere, anywhere, vmem, vmem, anywhere, anywhere, vmem, vmem, anywhere, anywhere],
        scratch_shapes=[V((n, 128), BF) for n in pn.sizes]
        + [V(s, F32) for s in wides]
        + [V((T, D), BF), V((T, D), F32), dma((np_,)), dma((2 * pn.chunks + 7,)), dma((4,))],
        compiler_params=pltpu.CompilerParams(vmem_limit_bytes=62 * 2**20),
        name="widen",
    )(*ags, vec, layer, patch)
    block = (FD, R, C, D)
    return (final[0].reshape(block), final[1].reshape(block)) + tuple(final[2:])


def solution(mesh):
    band = P("fld", "lat", None, None)
    return jax.shard_map(
        functools.partial(per_device, mesh),
        mesh=mesh,
        in_specs=(band, P("fld", None, None)) + (P(),) * 8 + (band,),
        out_specs=(band, band) + (P(),) * 8,
        check_vma=False,
    )
```

```python
import functools
import math

import jax
import jax.numpy as jnp
from jax import lax
from jax.experimental import pallas as pl
from jax.experimental.pallas import tpu as pltpu
from jax.sharding import PartitionSpec as P

HEAD_DIM = 32
GROUP = 8
WIDE = GROUP * HEAD_DIM
SCALE = HEAD_DIM ** -0.5
LOG2E = math.log2(math.e)
EPS = 1e-6
REACH = 4
NEG = -1e30
CHUNK = 512
BLOCK = 256
FIELDS_AT_ONCE = 2
SCHEDULE = {
    "J2": (0,), "J4": (0, 1), "J6": (2,), "J7": (1,), "J8": (3, 0),
    "E0": (2,), "E1": (1,), "E2": (3,), "E3": (), "P": (0,), "P1": (4, 2),
    "A0": (1,), "A1": (4, 3), "A2": (0,), "A3": (2, 1),
    "B0": (4, 3), "B1": (0,), "B2": (2, 1), "B3": (5, 3, 4),
    "C0": (0, 5, 2), "C1": (6, 1, 3, 4), "D0": (0, 6, 2), "D1": (5, 1), "D2": (3, 4), "D3": (0, 2),
}
BF = jnp.bfloat16
F32 = jnp.float32
MESH = pl.DeviceIdType.MESH

NT = (((1,), (1,)), ((), ()))
TN = (((0,), (0,)), ((), ()))


def dot(a, b, dims=None):
    if dims is None:
        return jnp.dot(a, b, preferred_element_type=F32)
    return lax.dot_general(a, b, dims, preferred_element_type=F32)


def normalize(x):
    center = jnp.mean(x, axis=-1, keepdims=True)
    off = x - center
    rstd = lax.rsqrt(jnp.mean(off * off, axis=-1, keepdims=True) + EPS)
    return off * rstd, rstd


def norm_pull(e, gain, n, rstd):
    ge = e * gain
    a = jnp.mean(ge, axis=-1, keepdims=True)
    b = jnp.mean(ge * n, axis=-1, keepdims=True)
    return (ge - a - n * b) * rstd


def gelu_both(u):
    cdf = 0.5 + 0.5 * lax.erf(u * (1.0 / math.sqrt(2.0)))
    density = jnp.exp2((u * u) * (-0.5 * LOG2E)) * (1.0 / math.sqrt(2.0 * math.pi))
    return u * cdf, cdf + u * density


def row_sums(x):
    return jnp.sum(x, axis=0, keepdims=True)


class Plan:
    def __init__(self, mesh, fields, rows, cols, width, ff):
        self.lats = mesh.shape["lat"]
        self.flds = mesh.shape["fld"]
        self.zs = self.flds // 2
        self.fields, self.rows, self.cols = fields, rows, cols
        self.tf = rows * cols
        self.tokens = fields * self.tf
        self.width, self.ff = width, ff
        self.chunks = ff // CHUNK
        self.size_of = {"core": 2, "x": 2, "y": self.lats // 2, "lat": self.lats, "z": self.zs}
        unit = 16 * self.lats * self.flds
        blocks = width // 128
        mlp = CHUNK * blocks + width * (CHUNK // 128)
        rows_needed = [mlp] * self.chunks + [width * blocks] + [width * (3 * WIDE // 128)] * 2
        self.sizes, self.subs = [], []
        for p, n in enumerate(rows_needed):
            n = -(-n // unit) * unit
            self.sizes.append(n)
            last = p >= len(rows_needed) - 1
            if last or n % (2 * unit):
                self.subs.append([(0, n, ("core", "lat", "z"))])
            else:
                self.subs.append([(0, n // 2, ("core", "x", "y", "z")), (n // 2, n // 2, ("core", "y", "x", "z"))])
        self.landing = []
        for subs in self.subs:
            total = 0
            for _, n, order in subs:
                for d in order:
                    n //= self.size_of[d]
                    total += n * (self.size_of[d] - 1)
            self.landing.append(total)
        self.n_subs = sum(len(s) for s in self.subs)


def body(plan, *refs):
    pn = plan
    np_ = len(pn.sizes)
    (patches, seg, gain_a, bias_a, w_qkv, w_proj, gain_m, bias_m, w_hid, w_out, cot) = refs[:11]
    out_layer, out_patch, out_vec = refs[11:14]
    out_ag = refs[14 : 14 + np_]
    sc = list(refs[14 + np_ :])

    def take(n):
        got = sc[:n]
        del sc[:n]
        return got

    wq, wp, wh, wo = take(4)
    pb, cb, segv, halo = take(4)
    normed, qb, kv, pt, ctx, res, nm, gres, act, gpre, gctx, edge = take(12)
    hq, hg, lse, hlse, dst, hdst = take(6)
    bm, biasb, vec, vrz, vrx, vrc = take(6)
    sb, rb, ag = take(np_), take(np_), take(np_)
    in_sem, out_sem, halo_s, halo_r, back_s, back_r, rs_s, rs_r, v_s, v_r = take(10)

    lat = lax.axis_index("lat")
    fld = lax.axis_index("fld")
    core = lax.rem(fld, 2)
    z = lax.div(fld, 2)
    x = lax.rem(lat, 2)
    y = lax.div(lat, 2)
    L, Z, Y = pn.lats, pn.zs, pn.lats // 2
    FD, R, C, TF, T, D, FF = pn.fields, pn.rows, pn.cols, pn.tf, pn.tokens, pn.width, pn.ff

    ins = [(patches, pb), (w_qkv, wq), (seg, segv), (w_proj, wp), (cot, cb), (w_hid, wh), (w_out, wo)]
    loads = [pltpu.make_async_copy(s, d, in_sem.at[i]) for i, (s, d) in enumerate(ins)]
    for c in loads:
        c.start()

    me = {"core": core, "x": x, "y": y, "lat": lat, "z": z}

    def device(d, i):
        if d == "core":
            return lat, z * 2 + i
        if d == "x":
            return y * 2 + i, fld
        if d == "y":
            return i * 2 + x, fld
        if d == "lat":
            return i, fld
        return lat, i * 2 + core

    def peers(d):
        n = pn.size_of[d]
        places = [lax.rem(me[d] + k, n) for k in range(1, n)]
        return [(i, device(d, i)) for i in places]

    barrier = pltpu.get_barrier_semaphore()
    everyone = peers("core") + peers("lat") + peers("z")
    for _, dev in everyone:
        pl.semaphore_signal(barrier, inc=1, device_id=dev, device_id_type=MESH)
    pl.semaphore_wait(barrier, len(everyone))

    up, down = (lat - 1, fld), (lat + 1, fld)
    has_up, has_down = lat > 0, lat < L - 1

    def remote(src, dst, s, r, dev):
        return pltpu.make_async_remote_copy(
            src_ref=src, dst_ref=dst, send_sem=s, recv_sem=r, device_id=dev, device_id_type=MESH
        )

    def arrived(ref, sem):
        pltpu.make_async_copy(ref, ref, sem).wait()

    halo_up = remote(patches.at[:, pl.ds(0, C)], halo.at[1], halo_s.at[0], halo_r.at[1], up)
    halo_dn = remote(patches.at[:, pl.ds(TF - C, C)], halo.at[0], halo_s.at[1], halo_r.at[0], down)
    pl.when(has_up)(halo_up.start)
    pl.when(has_down)(halo_dn.start)

    def spot(off, n):
        return pl.ds(pl.multiple_of(off, 16), n)

    class Part:
        def __init__(self, p, number, start, n, order, land):
            self.p, self.number, self.order = p, number, order
            self.off, self.len, self.land = [start], [n], []
            for d in order:
                g = pn.size_of[d]
                n = n // g
                self.land.append(land)
                land += n * (g - 1)
                self.off.append(self.off[-1] + me[d] * n)
                self.len.append(n)
            self.end = land

        def moved(self, i):
            return self.len[i + 1] * (pn.size_of[self.order[i]] - 1)

        def scatter(self, i):
            n = self.len[i + 1]
            for k, (j, dev) in enumerate(peers(self.order[i])):
                src = sb[self.p].at[spot(self.off[i] + j * n, n)]
                dst = rb[self.p].at[pl.ds(self.land[i] + k * n, n)]
                remote(src, dst, rs_s.at[self.number, i], rs_r.at[self.number, i], dev).start()

        def add(self, i):
            n = self.len[i + 1]
            d = self.order[i]
            arrived(rb[self.p].at[pl.ds(self.land[i], self.moved(i))], rs_r.at[self.number, i])
            mine = spot(self.off[i + 1], n)
            total = sb[self.p][mine, :].astype(F32)
            for k in range(pn.size_of[d] - 1):
                total = total + rb[self.p][self.land[i] + k * n : self.land[i] + (k + 1) * n, :].astype(F32)
            to = ag if i == len(self.order) - 1 else sb
            to[self.p][mine, :] = total.astype(BF)

        def gather(self, i):
            s = 4 + i
            mine = ag[self.p].at[spot(self.off[i + 1], self.len[i + 1])]
            for _, dev in peers(self.order[i]):
                remote(mine, mine, rs_s.at[self.number, s], rs_r.at[self.number, s], dev).start()

        def gathered(self, i):
            arrived(ag[self.p].at[pl.ds(0, self.moved(i))], rs_r.at[self.number, 4 + i])

        def step(self, s):
            nd = len(self.order)
            if s < nd:
                if s > 0:
                    self.add(s - 1)
                self.scatter(s)
            elif s == nd:
                self.add(nd - 1)
                self.gather(nd - 1)
            else:
                self.gathered(2 * nd - s)
                if s < 2 * nd:
                    self.gather(2 * nd - 1 - s)

        def finish(self):
            for i in range(len(self.order)):
                for s in (i, 4 + i):
                    arrived(sb[self.p].at[pl.ds(0, self.moved(i))], rs_s.at[self.number, s])

    parts, number = [], 0
    for p in range(np_):
        mine, land = [], 0
        for start, n, order in pn.subs[p]:
            mine.append(Part(p, number, start, n, order, land))
            land = mine[-1].end
            number += 1
        parts.append(mine)
    reached = [0] * np_
    last_step = [2 * len(m[0].order) for m in parts]

    def hook(*pieces):
        steps = []
        for p in pieces:
            if reached[p] <= last_step[p]:
                steps.append((p, reached[p]))
                reached[p] += 1

        def run():
            for p, s in steps:
                for part in parts[p]:
                    part.step(s)
                if s == last_step[p]:
                    pltpu.make_async_copy(ag[p], out_ag[p], out_sem.at[2 + p]).start()

        return run

    def place(name):
        return hook(*SCHEDULE.get(name, ()))

    def finish(p):
        for part in parts[p]:
            part.finish()
        pltpu.make_async_copy(ag[p], out_ag[p], out_sem.at[2 + p]).wait()

    def put(p, start, stride, value):
        rows, lanes = value.shape
        low = value.astype(BF)
        for j in range(lanes // 128):
            at = start + j * stride
            sb[p][at : at + rows, :] = low[:, j * 128 : (j + 1) * 128]

    rid = lax.broadcasted_iota(jnp.int32, (WIDE, WIDE), 0) // HEAD_DIM
    cid = lax.broadcasted_iota(jnp.int32, (WIDE, WIDE), 1) // HEAD_DIM
    same = jnp.where(rid == cid, 1.0, 0.0)
    bm[...] = same.astype(BF)

    ga, ba = gain_a[...].reshape(1, D), bias_a[...].reshape(1, D)
    gm, bmlp = gain_m[...].reshape(1, D), bias_m[...].reshape(1, D)
    loads[0].wait()

    per = max(1, 256 // TF)
    tile = per * TF
    tiles = T // tile

    def rows_at(t):
        return slice(t * tile, (t + 1) * tile)

    def fields_at(t):
        return slice(t * per, (t + 1) * per)

    def norm_one(t):
        n, _ = normalize(pb[fields_at(t)].reshape(tile, D).astype(F32))
        normed[rows_at(t), :] = (n * ga + ba).astype(BF)

    norm_one(0)
    loads[1].wait()
    for t in range(tiles):
        if t + 1 < tiles:
            norm_one(t + 1)
        qb[rows_at(t), :] = dot(normed[rows_at(t), :], wq[:, :D]).astype(BF)
        part = dot(normed[rows_at(t), :], wq[:, D:]).astype(BF)
        kv[fields_at(t), C : C + TF, :] = part.reshape(per, TF, 2 * D)

    loads[2].wait()
    kcol = lax.broadcasted_iota(jnp.int32, (C, WIDE), 0)
    qcol = lax.rem(lax.broadcasted_iota(jnp.int32, (C, WIDE), 1), C)
    away = jnp.abs(kcol - qcol)
    near = jnp.minimum(away, C - away) <= REACH
    diag = lax.broadcasted_iota(jnp.int32, (C, C), 0) == lax.broadcasted_iota(jnp.int32, (C, C), 1)
    for f in range(FD):
        line = segv[f, 0:1, :].astype(F32)
        across = jnp.concatenate([line] * GROUP, axis=1)
        along = jnp.sum(jnp.where(diag, line, 0.0), axis=1, keepdims=True)
        biasb[f] = jnp.where(jnp.logical_and(near, along == across), 0.0, NEG)
    pole_top = jnp.where(has_up, 0.0, NEG)
    pole_bottom = jnp.where(has_down, 0.0, NEG)

    lane_head = lax.broadcasted_iota(jnp.int32, (HEAD_DIM, WIDE), 1) // HEAD_DIM

    def diagonal(o):
        total = o[0:HEAD_DIM]
        for h in range(1, GROUP):
            total = jnp.where(lane_head == h, o[h * HEAD_DIM : (h + 1) * HEAD_DIM], total)
        return total

    def widened(q):
        return jnp.concatenate([q] * GROUP, axis=0) * bm[...]

    fpi = min(FIELDS_AT_ONCE, FD)

    def span(f, row):
        return pl.ds(pl.multiple_of(f * TF + row * C, C), C)

    k_lanes = [slice(g * WIDE, (g + 1) * WIDE) for g in range(2)]
    v_lanes = [slice(D + g * WIDE, D + (g + 1) * WIDE) for g in range(2)]

    def attend(rows, i, carry):
        units = [(i * fpi + j, g, r) for j in range(fpi) for g in range(2) for r in rows]
        scores = []
        for f, g, r in units:
            k = kv[f, r * C : (r + 3) * C, k_lanes[g]]
            scores.append(dot(k, widened(qb[span(f, r), k_lanes[g]]), NT))
        low, logs = [], []
        for (f, g, r), s in zip(units, scores):
            bias = biasb[f]
            first = bias + pole_top if r == 0 else bias
            third = bias + pole_bottom if r == R - 1 else bias
            s = s + jnp.concatenate([first, bias, third], axis=0)
            m = jnp.max(s, axis=0, keepdims=True)
            p = jnp.exp2((s - m) * (SCALE * LOG2E))
            total = row_sums(p)
            logs.append(m * (SCALE * LOG2E) + jnp.log2(total) if r in (0, R - 1) else None)
            low.append((p * (1.0 / total)).astype(BF))
        outs = []
        for (f, g, r), p in zip(units, low):
            v = kv[f, r * C : (r + 3) * C, v_lanes[g]]
            outs.append(diagonal(dot(p, v, TN)).astype(BF))
        for (f, g, r), p, log, o in zip(units, low, logs, outs):
            pt[f, g * R + r] = p
            ctx[span(f, r), k_lanes[g]] = o
            if r in (0, R - 1):
                lse[0 if r == 0 else 1, pl.ds(f * 2 + g, 1), :] = log
        return carry

    if R > 2:
        lax.fori_loop(0, FD // fpi, functools.partial(attend, range(1, R - 1)), 0)

    for side, ok, copy in ((0, has_up, halo_dn), (1, has_down, halo_up)):
        pl.when(ok)(copy.wait_recv)

        @pl.when(jnp.logical_not(ok))
        def _():
            halo[side] = jnp.zeros((FD, C, D), BF)

        n, _unused = normalize(halo[side].reshape(FD * C, D).astype(F32))
        low = (n * ga + ba).astype(BF)
        hq[side] = dot(low, wq[:, :D]).astype(BF)
        edge_kv = dot(low, wq[:, D:]).astype(BF).reshape(FD, C, 2 * D)
        start = 0 if side == 0 else TF + C
        kv[:, start : start + C, :] = edge_kv

    lax.fori_loop(0, FD // fpi, functools.partial(attend, (0, R - 1)), 0)

    loads[3].wait()
    for t in range(tiles):
        r = pb[fields_at(t)].reshape(tile, D).astype(F32) + dot(ctx[rows_at(t), :], wp[...])
        res[rows_at(t), :] = r
        n, _ = normalize(r)
        nm[rows_at(t), :] = (n * gm + bmlp).astype(BF)

    for i in (4, 5, 6):
        loads[i].wait()
    blocks = FF // BLOCK
    in_chunk = CHUNK // BLOCK

    def hidden_block(j):
        return slice(j * BLOCK, (j + 1) * BLOCK)

    def kept(ref, j):
        return ref.at[pl.ds(0, T), pl.ds((j % 2) * BLOCK, BLOCK)]

    def mlp_in(j):
        kept(gres, j)[...] = dot(nm[...], wh[:, hidden_block(j)])
        kept(edge, j)[...] = dot(cb[...], wo[hidden_block(j), :], NT)

    def mlp_mid(j):
        a, da = gelu_both(kept(gres, j)[...])
        act[:, hidden_block(j)] = a.astype(BF)
        gpre[:, hidden_block(j)] = (da * kept(edge, j)[...]).astype(BF)

    def mlp_out(j):
        c, part = j // in_chunk, j % in_chunk
        put(c, part * BLOCK, CHUNK, dot(act[:, hidden_block(j)], cb[...], TN))
        start = CHUNK * (D // 128) + part * (BLOCK // 128) * D
        put(c, start, D, dot(nm[...], gpre[:, hidden_block(j)], TN))

    mlp_in(0)
    for j in range(blocks):
        if j + 1 < blocks:
            mlp_in(j + 1)
        mlp_mid(j)
        if j > 0:
            mlp_out(j - 1)
        place(f"J{j}")()
    mlp_out(blocks - 1)
    place(f"J{blocks}")()

    zero = jnp.zeros((1, D), F32)

    mlp_gain, mlp_bias = zero, zero
    grad_in = dot(gpre[rows_at(0), :], wh[...], NT)
    for t in range(tiles):
        e = grad_in
        if t + 1 < tiles:
            grad_in = dot(gpre[rows_at(t + 1), :], wh[...], NT)
        n, rstd = normalize(res[rows_at(t), :])
        gr = cb[rows_at(t), :].astype(F32) + norm_pull(e, gm, n, rstd)
        gres[rows_at(t), :] = gr
        low = gr.astype(BF)
        nm[rows_at(t), :] = low
        gctx[fields_at(t)] = dot(low, wp[...], NT).astype(BF).reshape(per, TF, D)
        mlp_gain, mlp_bias = mlp_gain + row_sums(e * n), mlp_bias + row_sums(e)
        place(f"E{t}")()

    pj = pn.chunks
    g_up = remote(gctx.at[:, pl.ds(0, C)], hg.at[1], back_s.at[0], back_r.at[1], up)
    g_dn = remote(gctx.at[:, pl.ds(TF - C, C)], hg.at[0], back_s.at[1], back_r.at[0], down)
    l_up = remote(lse.at[0], hlse.at[1], back_s.at[2], back_r.at[3], up)
    l_dn = remote(lse.at[1], hlse.at[0], back_s.at[3], back_r.at[2], down)
    for to_up, to_dn in ((g_up, g_dn), (l_up, l_dn)):
        pl.when(has_up)(to_up.start)
        pl.when(has_down)(to_dn.start)
    place("P")()
    put(pj, 0, D, dot(ctx[...], nm[...], TN))
    place("P1")()

    grad_joined = gpre

    def joined(g, j):
        return slice((3 * g + j) * WIDE, (3 * g + j + 1) * WIDE)

    def edge_rows(g, side, f):
        return pl.ds(pl.multiple_of(((g * 2 + side) * FD + f) * C, C), C)

    def back_group(g, hooks):
        def back_fields(i, carry):
            for when, do in hooks.items():
                pl.when(i == when)(do)
            units = [(i * fpi + j, r) for j in range(fpi) for r in range(R)]
            have = []
            for f, r in units:
                win = slice(r * C, (r + 3) * C)
                qd = widened(qb[span(f, r), k_lanes[g]])
                dod = widened(gctx[f, r * C : (r + 1) * C, k_lanes[g]])
                have.append((qd, dod, kv[f, win, k_lanes[g]], kv[f, win, v_lanes[g]], pt[f, g * R + r]))
            dps = [dot(v, dod, NT) for qd, dod, k, v, p in have]
            dss, totals = [], []
            for (qd, dod, k, v, p), dp in zip(have, dps):
                wide = p.astype(F32)
                pd = wide * dp
                total = row_sums(pd)
                totals.append(total)
                dss.append(((pd - wide * total) * SCALE).astype(BF))
            dqs = [diagonal(dot(ds, one[2], TN)).astype(BF) for ds, one in zip(dss, have)]
            dks, dvs = [], []
            for (f, r), ds, (qd, dod, k, v, p) in zip(units, dss, have):
                own = slice(C if r == 0 else 0, 2 * C if r == R - 1 else 3 * C)
                first = r + 1 if r == 0 else r
                dks.append((first, dot(ds[own], qd)))
                dvs.append((first, dot(p[own], dod)))
            for (f, r), o, total in zip(units, dqs, totals):
                grad_joined[span(f, r), joined(g, 0)] = o
                if r in (0, R - 1):
                    dst[g, 0 if r == 0 else 1, pl.ds(f, 1), :] = total
            for j in range(fpi):
                f = i * fpi + j
                for what, terms in enumerate((dks, dvs)):
                    for row in range(1, R + 1):
                        total = None
                        for first, term in terms[j * R : (j + 1) * R]:
                            if first <= row < first + term.shape[0] // C:
                                piece = term[(row - first) * C : (row - first + 1) * C]
                                total = piece if total is None else total + piece
                        if row in (1, R):
                            edge[edge_rows(g, 0 if row == 1 else 1, f), what * WIDE : (what + 1) * WIDE] = total
                        else:
                            grad_joined[span(f, row - 1), joined(g, what + 1)] = total.astype(BF)
            return carry

        lax.fori_loop(0, FD // fpi, back_fields, 0)
        to_up = remote(dst.at[g, 0], hdst.at[g, 1], back_s.at[4 + 2 * g], back_r.at[5 + 2 * g], up)
        to_dn = remote(dst.at[g, 1], hdst.at[g, 0], back_s.at[5 + 2 * g], back_r.at[4 + 2 * g], down)
        pl.when(has_up)(to_up.start)
        pl.when(has_down)(to_dn.start)
        return to_up, to_dn

    fpe = min(2 * FIELDS_AT_ONCE, FD)

    def back_edges(g, sent):
        for to_up, to_dn in sent:
            pl.when(has_up)(to_dn.wait_recv)
            pl.when(has_down)(to_up.wait_recv)

        def back_rims(i, carry):
            units = [(i * fpe + j, side) for j in range(fpe) for side in range(2)]
            oks, rows = (has_up, has_down), (0, R - 1)
            have = []
            for f, side in units:
                qd = widened(hq[side, pl.ds(pl.multiple_of(f * C, C), C), k_lanes[g]])
                dod = widened(hg[side, f, :, k_lanes[g]])
                keys = slice((rows[side] + 1) * C, (rows[side] + 2) * C)
                have.append((qd, dod, kv[f, keys, k_lanes[g]], kv[f, keys, v_lanes[g]]))
            scores = [dot(k, qd, NT) for qd, dod, k, v in have]
            dps = [dot(v, dod, NT) for qd, dod, k, v in have]
            ps, dss = [], []
            for (f, side), s, dp in zip(units, scores, dps):
                s = (s + biasb[f]) * (SCALE * LOG2E) - hlse[side, pl.ds(f * 2 + g, 1), :]
                p = jnp.where(oks[side], jnp.exp2(s), 0.0)
                ds = p * (dp - hdst[g, side, pl.ds(f, 1), :]) * SCALE
                ps.append(p.astype(BF))
                dss.append(jnp.where(oks[side], ds, 0.0).astype(BF))
            dks = [dot(ds, one[0]) for ds, one in zip(dss, have)]
            dvs = [dot(p, one[1]) for p, one in zip(ps, have)]
            held = [edge[edge_rows(g, side, f), :] for f, side in units]
            for (f, side), dk, dv, own in zip(units, dks, dvs, held):
                dk = own[:, :WIDE] + jnp.where(oks[side], dk, 0.0)
                dv = own[:, WIDE:] + jnp.where(oks[side], dv, 0.0)
                grad_joined[span(f, rows[side]), joined(g, 1)] = dk.astype(BF)
                grad_joined[span(f, rows[side]), joined(g, 2)] = dv.astype(BF)
            return carry

        lax.fori_loop(0, FD // fpe, back_rims, 0)
        put(pj + 1 + g, 0, D, dot(normed[...], grad_joined[:, 3 * g * WIDE : 3 * (g + 1) * WIDE], TN))

    sent0 = back_group(0, {i: place(f"A{i}") for i in range(4)})
    early = {i: place(f"B{i}") for i in range(2)}
    later = {i: place(f"B{i}") for i in range(2, 4)}
    about = later[3]

    def first_edges():
        later[2]()
        back_edges(0, ((g_up, g_dn), (l_up, l_dn), sent0))

    sent1 = back_group(1, early | {2: first_edges, 3: about})
    place("C0")()
    back_edges(1, (sent1,))
    place("C1")()

    for t in range(tiles):
        nm[rows_at(t), :] = (res[rows_at(t), :] + dot(act[rows_at(t), :], wo[...])).astype(BF)
    layer_copy = pltpu.make_async_copy(nm, out_layer, out_sem.at[0])
    layer_copy.start()
    place("D0")()
    attn_gain, attn_bias = zero, zero

    def grad_of(t):
        e = None
        for g in range(2):
            for j in range(3):
                w = wq[:, j * D + g * WIDE : j * D + (g + 1) * WIDE]
                term = dot(grad_joined[rows_at(t), joined(g, j)], w, NT)
                e = term if e is None else e + term
        return e

    grad_in = grad_of(0)
    for t in range(tiles):
        e = grad_in
        if t + 1 < tiles:
            grad_in = grad_of(t + 1)
        n, rstd = normalize(pb[fields_at(t)].reshape(tile, D).astype(F32))
        gres[rows_at(t), :] += norm_pull(e, ga, n, rstd)
        attn_gain, attn_bias = attn_gain + row_sums(e * n), attn_bias + row_sums(e)

    patch_copy = pltpu.make_async_copy(gres, out_patch, out_sem.at[1])
    patch_copy.start()
    vec[...] = jnp.concatenate([attn_gain, attn_bias, mlp_gain, mlp_bias, zero, zero, zero, zero], axis=0)

    def vec_send(buf, d, i):
        buf[me[d]] = vec[...]
        for _, dev in peers(d):
            remote(vec, buf.at[me[d]], v_s.at[i], v_r.at[i], dev).start()

    def vec_sum(buf, d, i):
        count = pn.size_of[d]
        arrived(buf.at[pl.ds(0, count - 1)], v_r.at[i])
        arrived(buf.at[pl.ds(0, count - 1)], v_s.at[i])
        total = buf[0]
        for k in range(1, count):
            total = total + buf[k]
        vec[...] = total

    vec_send(vrz, "z", 0)
    place("D1")()
    vec_sum(vrz, "z", 0)
    vec_send(vrx, "lat", 1)
    place("D2")()
    vec_sum(vrx, "lat", 1)
    vec_send(vrc, "core", 2)
    place("D3")()
    vec_sum(vrc, "core", 2)
    vec_copy = pltpu.make_async_copy(vec, out_vec, in_sem.at[0])
    vec_copy.start()
    while any(reached[p] <= last_step[p] for p in range(np_)):
        for p in sorted(range(np_), key=lambda p: reached[p] - last_step[p], reverse=True):
            hook(p)()

    pl.when(has_up)(halo_up.wait_send)
    pl.when(has_down)(halo_dn.wait_send)
    for to_up, to_dn in ((g_up, g_dn), (l_up, l_dn), sent0, sent1):
        pl.when(has_up)(to_up.wait_send)
        pl.when(has_down)(to_dn.wait_send)
    layer_copy.wait()
    patch_copy.wait()
    vec_copy.wait()
    for p in range(np_):
        finish(p)


def widen(plan, *refs):
    pn = plan
    np_ = len(pn.sizes)
    ag, vec, layer, patch = refs[:np_], refs[np_], refs[np_ + 1], refs[np_ + 2]
    o_layer, o_patch, o_ag, o_ab, o_qkv, o_proj, o_mg, o_mb, o_hid, o_out = refs[np_ + 3 : np_ + 13]
    sc = list(refs[np_ + 13 :])
    low, wide = sc[:np_], sc[np_ : 2 * np_]
    kept_layer, kept_patch, in_sem, out_sem, pass_sem = sc[2 * np_ :]
    D = pn.width
    loads = [pltpu.make_async_copy(ag[p], low[p], in_sem.at[p]) for p in range(np_)]
    for c in loads:
        c.start()
    through = [
        (pltpu.make_async_copy(a, b, pass_sem.at[2 * i]), pltpu.make_async_copy(b, c, pass_sem.at[2 * i + 1]))
        for i, (a, b, c) in enumerate(((layer, kept_layer, o_layer), (patch, kept_patch, o_patch)))
    ]
    for arrive, _ in through:
        arrive.start()
    for i, o in enumerate((o_ag, o_ab, o_mg, o_mb)):
        o[...] = vec[i : i + 1, :].reshape(D)
    stores = []

    def store(src, dst):
        c = pltpu.make_async_copy(src, dst, out_sem.at[len(stores)])
        c.start()
        stores.append(c)

    def spread(p, start, rows, blocks, col):
        for j in range(blocks):
            wide[p][:, col + j * 128 : col + (j + 1) * 128] = low[p][
                start + j * rows : start + (j + 1) * rows, :
            ].astype(F32)

    for p in range(np_):
        loads[p].wait()
        if p == np_ - 1:
            for arrive, leave in through:
                arrive.wait()
                leave.start()
        if p < pn.chunks:
            spread(p, 0, CHUNK, D // 128, 0)
            store(wide[p].at[:, pl.ds(0, D)], o_out.at[pl.ds(p * CHUNK, CHUNK)])
            spread(p, CHUNK * (D // 128), D, CHUNK // 128, D)
            store(wide[p].at[:, pl.ds(D, CHUNK)], o_hid.at[:, pl.ds(p * CHUNK, CHUNK)])
        elif p == pn.chunks:
            spread(p, 0, D, D // 128, 0)
            store(wide[p], o_proj)
        else:
            g = p - pn.chunks - 1
            spread(p, 0, D, 3 * WIDE // 128, 0)
            for j in range(3):
                store(
                    wide[p].at[:, pl.ds(j * WIDE, WIDE)],
                    o_qkv.at[:, pl.ds(j * D + g * WIDE, WIDE)],
                )
    for c in stores + [leave for _, leave in through]:
        c.wait()


def per_device(mesh, patches, segment_ids, gain_attn, bias_attn, w_qkv, w_proj, gain_mlp, bias_mlp, w_hidden, w_output, cotangent):
    fields, rows, cols, width = patches.shape
    ff = w_hidden.shape[1]
    pn = Plan(mesh, fields, rows, cols, width, ff)
    np_ = len(pn.sizes)
    T, TF, D, C, R, FD = pn.tokens, pn.tf, width, cols, rows, fields
    L, Z = pn.lats, pn.zs
    anywhere = pl.BlockSpec(memory_space=pl.ANY)
    vmem = pl.BlockSpec(memory_space=pltpu.VMEM)
    V = pltpu.VMEM
    dma = pltpu.SemaphoreType.DMA
    scratch = [
        V((D, 3 * D), BF), V((D, D), BF), V((D, ff), BF), V((ff, D), BF),
        V((FD, TF, D), BF), V((T, D), BF), V(segment_ids.shape, jnp.int32), V((2, FD, C, D), BF),
        V((T, D), BF), V((T, D), BF), V((FD, TF + 2 * C, 2 * D), BF), V((FD, 2 * R, 3 * C, WIDE), BF),
        V((T, D), BF), V((T, D), F32), V((T, D), BF), V((T, D), F32),
        V((T, ff), BF), V((T, ff), BF), V((FD, TF, D), BF),
        V((max(4 * FD * C, T), 2 * WIDE), F32),
        V((2, FD * C, D), BF), V((2, FD, C, D), BF),
        V((2, 2 * FD, WIDE), F32), V((2, 2 * FD, WIDE), F32), V((2, 2, FD, WIDE), F32), V((2, 2, FD, WIDE), F32),
        V((WIDE, WIDE), BF), V((FD, C, WIDE), F32),
        V((8, D), F32), V((Z, 8, D), F32), V((L, 8, D), F32), V((2, 8, D), F32),
    ]
    scratch += [V((n, 128), BF) for n in pn.sizes]
    scratch += [V((n, 128), BF) for n in pn.landing]
    scratch += [V((n, 128), BF) for n in pn.sizes]
    scratch += [
        dma((7,)), dma((2 + np_,)), dma((2,)), dma((2,)), dma((8,)), dma((8,)),
        dma((pn.n_subs, 8)), dma((pn.n_subs, 8)), dma((3,)), dma((3,)),
    ]
    shape = jax.ShapeDtypeStruct
    outs = pl.pallas_call(
        functools.partial(body, pn),
        out_shape=[shape((T, D), BF), shape((T, D), F32), shape((8, D), F32)]
        + [shape((n, 128), BF) for n in pn.sizes],
        in_specs=[anywhere, anywhere, vmem, vmem, anywhere, anywhere, vmem, vmem, anywhere, anywhere, anywhere],
        out_specs=[anywhere] * (3 + np_),
        scratch_shapes=scratch,
        compiler_params=pltpu.CompilerParams(
            collective_id=0, has_side_effects=True, vmem_limit_bytes=62 * 2**20
        ),
        name="block",
    )(
        patches.reshape(FD, TF, D), segment_ids, gain_attn, bias_attn, w_qkv, w_proj, gain_mlp, bias_mlp,
        w_hidden, w_output, cotangent.reshape(T, D),
    )
    layer, patch, vec = outs[:3]
    ags = outs[3:]
    wides = [(D, D + CHUNK)] * pn.chunks + [(D, D)] + [(D, 3 * WIDE)] * 2
    final = pl.pallas_call(
        functools.partial(widen, pn),
        out_shape=[
            shape((T, D), BF), shape((T, D), F32), shape((D,), F32), shape((D,), F32), shape((D, 3 * D), F32),
            shape((D, D), F32), shape((D,), F32), shape((D,), F32), shape((D, ff), F32), shape((ff, D), F32),
        ],
        in_specs=[anywhere] * np_ + [vmem, anywhere, anywhere],
        out_specs=[anywhere, anywhere, vmem, vmem, anywhere, anywhere, vmem, vmem, anywhere, anywhere],
        scratch_shapes=[V((n, 128), BF) for n in pn.sizes]
        + [V(s, F32) for s in wides]
        + [V((T, D), BF), V((T, D), F32), dma((np_,)), dma((2 * pn.chunks + 7,)), dma((4,))],
        compiler_params=pltpu.CompilerParams(vmem_limit_bytes=62 * 2**20),
        name="widen",
    )(*ags, vec, layer, patch)
    block = (FD, R, C, D)
    return (final[0].reshape(block), final[1].reshape(block)) + tuple(final[2:])


def solution(mesh):
    band = P("fld", "lat", None, None)
    return jax.shard_map(
        functools.partial(per_device, mesh),
        mesh=mesh,
        in_specs=(band, P("fld", None, None)) + (P(),) * 8 + (band,),
        out_specs=(band, band) + (P(),) * 8,
        check_vma=False,
    )
```

```python
import functools
import math

import jax
import jax.numpy as jnp
from jax import lax
from jax.experimental import pallas as pl
from jax.experimental.pallas import tpu as pltpu
from jax.sharding import PartitionSpec as P

HEAD_DIM = 32
GROUP = 8
WIDE = GROUP * HEAD_DIM
SCALE = HEAD_DIM ** -0.5
LOG2E = math.log2(math.e)
EPS = 1e-6
REACH = 4
NEG = -1e30
CHUNK = 512
BLOCK = 256
FIELDS_AT_ONCE = 2
DIRECT = (5, 6)
Z_FIRST = ()
SCHEDULE = {
    "J2": (0, 1),
    "J4": (0, 2, 3, 1),
    "J6": (2, 3, 4, 5),
    "J8": (4, 6, 7, 5, 0, 1),
    "E0": (6,),
    "E1": (7, 2, 3),
    "E3": (4, 5),
    "P1": (1, 8, 9, 0),
    "A1": (8, 9),
    "A3": (1, 6, 7),
    "B0": (0, 2),
    "B2": (3, 1),
    "B3": (4, 0, 9),
    "X": (2, 6),
    "X1": (3,),
    "X2": (5, 0, 4),
    "C0": (8, 10),
    "X3": (7, 2),
    "X4": (1, 10, 6, 9, 8, 3),
    "C1": (12, 5, 2, 0),
    "D0": (4,),
    "D1": (12, 0, 7, 1),
    "D2": (6,),
    "D3": (9, 1, 8),
    "F0": (3, 5),
    "F1": (10, 7, 4, 2, 9),
    "F2": (8,),
    "F3": (2,),
    "V0": (14,),
    "T": (12, 10, 6, 5, 12, 10, 12, 7, 3, 8, 4, 14, 9, 5, 6, 10, 10, 12, 12, 3, 4, 5, 6, 14, 8, 7, 9, 8, 7, 9, 14),
}
BF = jnp.bfloat16
F32 = jnp.float32
MESH = pl.DeviceIdType.MESH

NT = (((1,), (1,)), ((), ()))
TN = (((0,), (0,)), ((), ()))


def dot(a, b, dims=None):
    if dims is None:
        return jnp.dot(a, b, preferred_element_type=F32)
    return lax.dot_general(a, b, dims, preferred_element_type=F32)


def normalize(x):
    center = jnp.mean(x, axis=-1, keepdims=True)
    off = x - center
    rstd = lax.rsqrt(jnp.mean(off * off, axis=-1, keepdims=True) + EPS)
    return off * rstd, rstd


def norm_pull(e, gain, n, rstd):
    ge = e * gain
    a = jnp.mean(ge, axis=-1, keepdims=True)
    b = jnp.mean(ge * n, axis=-1, keepdims=True)
    return (ge - a - n * b) * rstd


def gelu_both(u):
    cdf = 0.5 + 0.5 * lax.erf(u * (1.0 / math.sqrt(2.0)))
    density = jnp.exp2((u * u) * (-0.5 * LOG2E)) * (1.0 / math.sqrt(2.0 * math.pi))
    return u * cdf, cdf + u * density


def row_sums(x):
    return jnp.sum(x, axis=0, keepdims=True)


class Plan:
    def __init__(self, mesh, fields, rows, cols, width, ff):
        self.lats = mesh.shape["lat"]
        self.flds = mesh.shape["fld"]
        self.zs = self.flds // 2
        self.fields, self.rows, self.cols = fields, rows, cols
        self.tf = rows * cols
        self.tokens = fields * self.tf
        self.width, self.ff = width, ff
        self.chunks = ff // CHUNK
        self.size_of = {"core": 2, "x": 2, "y": self.lats // 2, "lat": self.lats, "z": self.zs}
        unit = 16 * self.lats * self.flds
        blocks = width // 128
        mlp = CHUNK * blocks + width * (CHUNK // 128)
        rows_needed = [mlp] * self.chunks + [width * blocks] + [width * (3 * WIDE // 128)] * 2
        self.sizes, self.subs = [], []
        for p, n in enumerate(rows_needed):
            n = -(-n // unit) * unit
            self.sizes.append(n)
            if p in Z_FIRST:
                self.subs.append([(0, n, ("core", "z", "lat"))])
            elif p in DIRECT or n % (2 * unit):
                self.subs.append([(0, n, ("core", "lat", "z"))])
            else:
                self.subs.append([(0, n // 2, ("core", "x", "y", "z")), (n // 2, n // 2, ("core", "y", "x", "z"))])
        self.landing = []
        for subs in self.subs:
            total = 0
            for _, n, order in subs:
                for d in order:
                    n //= self.size_of[d]
                    total += n * (self.size_of[d] - 1)
            self.landing.append(total)
        self.n_subs = sum(len(s) for s in self.subs)


def body(plan, *refs):
    pn = plan
    np_ = len(pn.sizes)
    (patches, seg, gain_a, bias_a, w_qkv, w_proj, gain_m, bias_m, w_hid, w_out, cot) = refs[:11]
    out_layer, out_patch, out_vec = refs[11:14]
    out_ag = refs[14 : 14 + np_]
    sc = list(refs[14 + np_ :])

    def take(n):
        got = sc[:n]
        del sc[:n]
        return got

    wq, wp, wh, wo = take(4)
    pb, cb, segv, halo = take(4)
    normed, qb, kv, pt, ctx, res, nm, gres, act, gpre, gctx, edge = take(12)
    hq, hg, lse, hlse, dst, hdst = take(6)
    bm, biasb, vec, vrz, vrx, vrc = take(6)
    sb, rb, ag = take(np_), take(np_), take(np_)
    in_sem, out_sem, halo_s, halo_r, rim_s, rim_r, back_s, back_r, rs_s, rs_r, v_s, v_r = take(12)

    lat = lax.axis_index("lat")
    fld = lax.axis_index("fld")
    core = lax.rem(fld, 2)
    z = lax.div(fld, 2)
    x = lax.rem(lat, 2)
    y = lax.div(lat, 2)
    L, Z, Y = pn.lats, pn.zs, pn.lats // 2
    FD, R, C, TF, T, D, FF = pn.fields, pn.rows, pn.cols, pn.tf, pn.tokens, pn.width, pn.ff

    ins = [(patches, pb), (w_qkv, wq), (seg, segv), (cot, cb), (w_out, wo), (w_proj, wp), (w_hid, wh)]
    loads = [pltpu.make_async_copy(s, d, in_sem.at[i]) for i, (s, d) in enumerate(ins)]
    loads[0].start()
    loads[1].start()

    me = {"core": core, "x": x, "y": y, "lat": lat, "z": z}

    def device(d, i):
        if d == "core":
            return lat, z * 2 + i
        if d == "x":
            return y * 2 + i, fld
        if d == "y":
            return i * 2 + x, fld
        if d == "lat":
            return i, fld
        return lat, i * 2 + core

    def peers(d):
        n = pn.size_of[d]
        places = [lax.rem(me[d] + k, n) for k in range(1, n)]
        return [(i, device(d, i)) for i in places]

    barrier = pltpu.get_barrier_semaphore()
    everyone = peers("core") + peers("lat") + peers("z")
    for _, dev in everyone:
        pl.semaphore_signal(barrier, inc=1, device_id=dev, device_id_type=MESH)
    pl.semaphore_wait(barrier, len(everyone))

    up, down = (lat - 1, fld), (lat + 1, fld)
    has_up, has_down = lat > 0, lat < L - 1

    def remote(src, dst, s, r, dev):
        return pltpu.make_async_remote_copy(
            src_ref=src, dst_ref=dst, send_sem=s, recv_sem=r, device_id=dev, device_id_type=MESH
        )

    def arrived(ref, sem):
        pltpu.make_async_copy(ref, ref, sem).wait()

    half = FD // 2
    halo_copies = []
    for h in range(2):
        some = pl.ds(h * half, half)
        to_up = remote(patches.at[some, pl.ds(0, C)], halo.at[1, some], halo_s.at[0, h], halo_r.at[1, h], up)
        to_dn = remote(patches.at[some, pl.ds(TF - C, C)], halo.at[0, some], halo_s.at[1, h], halo_r.at[0, h], down)
        pl.when(has_up)(to_up.start)
        pl.when(has_down)(to_dn.start)
        halo_copies.append((to_up, to_dn))
    for c in loads[2:]:
        c.start()

    def spot(off, n):
        return pl.ds(pl.multiple_of(off, 16), n)

    class Part:
        def __init__(self, p, number, start, n, order, land):
            self.p, self.number, self.order = p, number, order
            self.off, self.len, self.land = [start], [n], []
            for d in order:
                g = pn.size_of[d]
                n = n // g
                self.land.append(land)
                land += n * (g - 1)
                self.off.append(self.off[-1] + me[d] * n)
                self.len.append(n)
            self.end = land

        def moved(self, i):
            return self.len[i + 1] * (pn.size_of[self.order[i]] - 1)

        def scatter(self, i):
            n = self.len[i + 1]
            for k, (j, dev) in enumerate(peers(self.order[i])):
                src = sb[self.p].at[spot(self.off[i] + j * n, n)]
                dst = rb[self.p].at[pl.ds(self.land[i] + k * n, n)]
                remote(src, dst, rs_s.at[self.number, i], rs_r.at[self.number, i], dev).start()

        def add(self, i):
            n = self.len[i + 1]
            d = self.order[i]
            arrived(rb[self.p].at[pl.ds(self.land[i], self.moved(i))], rs_r.at[self.number, i])
            mine = spot(self.off[i + 1], n)
            total = sb[self.p][mine, :].astype(F32)
            for k in range(pn.size_of[d] - 1):
                total = total + rb[self.p][self.land[i] + k * n : self.land[i] + (k + 1) * n, :].astype(F32)
            to = ag if i == len(self.order) - 1 else sb
            to[self.p][mine, :] = total.astype(BF)

        def gather(self, i):
            s = 4 + i
            mine = ag[self.p].at[spot(self.off[i + 1], self.len[i + 1])]
            for _, dev in peers(self.order[i]):
                remote(mine, mine, rs_s.at[self.number, s], rs_r.at[self.number, s], dev).start()

        def gathered(self, i):
            arrived(ag[self.p].at[pl.ds(0, self.moved(i))], rs_r.at[self.number, 4 + i])

        def step(self, s):
            nd = len(self.order)
            if s < nd:
                if s > 0:
                    self.add(s - 1)
                self.scatter(s)
            elif s == nd:
                self.add(nd - 1)
                self.gather(nd - 1)
            else:
                self.gathered(2 * nd - s)
                if s < 2 * nd:
                    self.gather(2 * nd - 1 - s)

        def finish(self):
            for i in range(len(self.order)):
                for s in (i, 4 + i):
                    arrived(sb[self.p].at[pl.ds(0, self.moved(i))], rs_s.at[self.number, s])

    parts, number = [], 0
    for p in range(np_):
        mine, land = [], 0
        for start, n, order in pn.subs[p]:
            mine.append(Part(p, number, start, n, order, land))
            land = mine[-1].end
            number += 1
        parts.append(mine)
    every = [part for mine in parts for part in mine]
    vec_at = len(every)
    reached = [0] * (vec_at + 1)
    last_step = [2 * len(part.order) for part in every] + [3]

    def out_copy(part):
        rows = pl.ds(part.off[0], part.len[0])
        return pltpu.make_async_copy(ag[part.p].at[rows], out_ag[part.p].at[rows], out_sem.at[2 + part.number])

    codes = [2 * p + i for p, mine in enumerate(parts) for i in range(len(mine))] + [2 * np_]
    number_of = {code: k for k, code in enumerate(codes)}

    def hook(*some):
        steps = []
        for code in some:
            k = number_of.get(code, vec_at + 1)
            if k <= vec_at and reached[k] <= last_step[k]:
                steps.append((k, reached[k]))
                reached[k] += 1

        def run():
            for k, s in steps:
                if k == vec_at:
                    vec_step(s)
                    continue
                every[k].step(s)
                if s == last_step[k]:
                    out_copy(every[k]).start()

        return run

    def place(name):
        return hook(*SCHEDULE.get(name, ()))

    rounds = ((vrz, "z"), (vrx, "lat"), (vrc, "core"))

    def vec_step(s):
        if s > 0:
            buf, d = rounds[s - 1]
            count = pn.size_of[d]
            arrived(buf.at[pl.ds(0, count - 1)], v_r.at[s - 1])
            arrived(buf.at[pl.ds(0, count - 1)], v_s.at[s - 1])
            total = buf[0]
            for k in range(1, count):
                total = total + buf[k]
            vec[...] = total
        if s < 3:
            buf, d = rounds[s]
            buf[me[d]] = vec[...]
            for _, dev in peers(d):
                remote(vec, buf.at[me[d]], v_s.at[s], v_r.at[s], dev).start()
        else:
            pltpu.make_async_copy(vec, out_vec, in_sem.at[0]).start()

    def finish(part):
        part.finish()
        out_copy(part).wait()

    def put(p, start, stride, value):
        rows, lanes = value.shape
        low = value.astype(BF)
        for j in range(lanes // 128):
            at = start + j * stride
            sb[p][at : at + rows, :] = low[:, j * 128 : (j + 1) * 128]

    rid = lax.broadcasted_iota(jnp.int32, (WIDE, WIDE), 0) // HEAD_DIM
    cid = lax.broadcasted_iota(jnp.int32, (WIDE, WIDE), 1) // HEAD_DIM
    same = jnp.where(rid == cid, 1.0, 0.0)
    bm[...] = same.astype(BF)

    ga, ba = gain_a[...].reshape(1, D), bias_a[...].reshape(1, D)
    gm, bmlp = gain_m[...].reshape(1, D), bias_m[...].reshape(1, D)
    loads[0].wait()

    per = max(1, 256 // TF)
    tile = per * TF
    tiles = T // tile

    def rows_at(t):
        return slice(t * tile, (t + 1) * tile)

    def fields_at(t):
        return slice(t * per, (t + 1) * per)

    def norm_one(t):
        n, _ = normalize(pb[fields_at(t)].reshape(tile, D).astype(F32))
        normed[rows_at(t), :] = (n * ga + ba).astype(BF)

    norm_one(0)
    loads[1].wait()
    for t in range(tiles):
        if t + 1 < tiles:
            norm_one(t + 1)
        qb[rows_at(t), :] = dot(normed[rows_at(t), :], wq[:, :D]).astype(BF)
        part = dot(normed[rows_at(t), :], wq[:, D:]).astype(BF)
        kv[fields_at(t), C : C + TF, :] = part.reshape(per, TF, 2 * D)

    loads[2].wait()
    kcol = lax.broadcasted_iota(jnp.int32, (C, WIDE), 0)
    qcol = lax.rem(lax.broadcasted_iota(jnp.int32, (C, WIDE), 1), C)
    away = jnp.abs(kcol - qcol)
    near = jnp.minimum(away, C - away) <= REACH
    diag = lax.broadcasted_iota(jnp.int32, (C, C), 0) == lax.broadcasted_iota(jnp.int32, (C, C), 1)
    for f in range(FD):
        line = segv[f, 0:1, :].astype(F32)
        across = jnp.concatenate([line] * GROUP, axis=1)
        along = jnp.sum(jnp.where(diag, line, 0.0), axis=1, keepdims=True)
        biasb[f] = jnp.where(jnp.logical_and(near, along == across), 0.0, NEG)
    pole_top = jnp.where(has_up, 0.0, NEG)
    pole_bottom = jnp.where(has_down, 0.0, NEG)

    lane_head = lax.broadcasted_iota(jnp.int32, (HEAD_DIM, WIDE), 1) // HEAD_DIM

    def diagonal(o):
        total = o[0:HEAD_DIM]
        for h in range(1, GROUP):
            total = jnp.where(lane_head == h, o[h * HEAD_DIM : (h + 1) * HEAD_DIM], total)
        return total

    def widened(q):
        return jnp.concatenate([q] * GROUP, axis=0) * bm[...]

    fpi = min(FIELDS_AT_ONCE, FD)

    def span(f, row):
        return pl.ds(pl.multiple_of(f * TF + row * C, C), C)

    k_lanes = [slice(g * WIDE, (g + 1) * WIDE) for g in range(2)]
    v_lanes = [slice(D + g * WIDE, D + (g + 1) * WIDE) for g in range(2)]

    def attend(rows, i, carry):
        units = [(i * fpi + j, g, r) for j in range(fpi) for g in range(2) for r in rows]
        scores = []
        for f, g, r in units:
            k = kv[f, r * C : (r + 3) * C, k_lanes[g]]
            scores.append(dot(k, widened(qb[span(f, r), k_lanes[g]]), NT))
        low, logs = [], []
        for (f, g, r), s in zip(units, scores):
            bias = biasb[f]
            first = bias + pole_top if r == 0 else bias
            third = bias + pole_bottom if r == R - 1 else bias
            s = s + jnp.concatenate([first, bias, third], axis=0)
            m = jnp.max(s, axis=0, keepdims=True)
            p = jnp.exp2((s - m) * (SCALE * LOG2E))
            total = row_sums(p)
            logs.append(m * (SCALE * LOG2E) + jnp.log2(total) if r in (0, R - 1) else None)
            low.append((p * (1.0 / total)).astype(BF))
        outs = []
        for (f, g, r), p in zip(units, low):
            v = kv[f, r * C : (r + 3) * C, v_lanes[g]]
            outs.append(diagonal(dot(p, v, TN)).astype(BF))
        for (f, g, r), p, log, o in zip(units, low, logs, outs):
            pt[f, g * R + r] = p
            ctx[span(f, r), k_lanes[g]] = o
            if r in (0, R - 1):
                lse[0 if r == 0 else 1, pl.ds(f * 2 + g, 1), :] = log
        return carry

    if R > 2:
        lax.fori_loop(0, FD // fpi, functools.partial(attend, range(1, R - 1)), 0)

    loads[3].wait()
    loads[4].wait()
    for j in range(FF // BLOCK):
        some = slice(j * BLOCK, (j + 1) * BLOCK)
        gpre[:, some] = dot(cb[...], wo[some, :], NT).astype(BF)

    for h in range(2):
        some = slice(h * half, (h + 1) * half)
        flat = slice(h * half * C, (h + 1) * half * C)
        for side, ok, copy in ((0, has_up, halo_copies[h][1]), (1, has_down, halo_copies[h][0])):
            pl.when(ok)(copy.wait_recv)

            @pl.when(jnp.logical_not(ok))
            def _():
                halo[side, some] = jnp.zeros((half, C, D), BF)

            n, _unused = normalize(halo[side, some].reshape(half * C, D).astype(F32))
            low = (n * ga + ba).astype(BF)
            hq[side, flat, :] = dot(low, wq[:, :D]).astype(BF)
            start = 0 if side == 0 else TF + C
            kv[some, start : start + C, :] = dot(low, wq[:, D:]).astype(BF).reshape(half, C, 2 * D)
        turns = half // fpi
        lax.fori_loop(h * turns, (h + 1) * turns, functools.partial(attend, (0, R - 1)), 0)

    loads[5].wait()
    for t in range(tiles):
        r = pb[fields_at(t)].reshape(tile, D).astype(F32) + dot(ctx[rows_at(t), :], wp[...])
        res[rows_at(t), :] = r
        n, _ = normalize(r)
        nm[rows_at(t), :] = (n * gm + bmlp).astype(BF)

    loads[6].wait()
    blocks = FF // BLOCK
    in_chunk = CHUNK // BLOCK

    def hidden_block(j):
        return slice(j * BLOCK, (j + 1) * BLOCK)

    def kept(ref, j):
        return ref.at[pl.ds(0, T), pl.ds((j % 2) * BLOCK, BLOCK)]

    def mlp_in(j):
        kept(gres, j)[...] = dot(nm[...], wh[:, hidden_block(j)])

    def mlp_mid(j):
        a, da = gelu_both(kept(gres, j)[...])
        act[:, hidden_block(j)] = a.astype(BF)
        gpre[:, hidden_block(j)] = (da * gpre[:, hidden_block(j)].astype(F32)).astype(BF)

    def mlp_out(j):
        c, part = j // in_chunk, j % in_chunk
        put(c, part * BLOCK, CHUNK, dot(act[:, hidden_block(j)], cb[...], TN))
        start = CHUNK * (D // 128) + part * (BLOCK // 128) * D
        put(c, start, D, dot(nm[...], gpre[:, hidden_block(j)], TN))

    mlp_in(0)
    for j in range(blocks):
        if j + 1 < blocks:
            mlp_in(j + 1)
        mlp_mid(j)
        if j > 0:
            mlp_out(j - 1)
        place(f"J{j}")()
    mlp_out(blocks - 1)
    place(f"J{blocks}")()

    zero = jnp.zeros((1, D), F32)

    mlp_gain, mlp_bias = zero, zero

    l_up = remote(lse.at[0], hlse.at[1], back_s.at[2], back_r.at[3], up)
    l_dn = remote(lse.at[1], hlse.at[0], back_s.at[3], back_r.at[2], down)
    pl.when(has_up)(l_up.start)
    pl.when(has_down)(l_dn.start)

    def send_rims(some):
        some = pl.ds(some.start, some.stop - some.start)
        h = some.start // half
        to_up = remote(gctx.at[some, pl.ds(0, C)], hg.at[1, some], rim_s.at[0, h], rim_r.at[1, h], up)
        to_dn = remote(gctx.at[some, pl.ds(TF - C, C)], hg.at[0, some], rim_s.at[1, h], rim_r.at[0, h], down)
        pl.when(has_up)(to_up.start)
        pl.when(has_down)(to_dn.start)

    grad_in = dot(gpre[rows_at(0), :], wh[...], NT)
    for t in range(tiles):
        e = grad_in
        if t + 1 < tiles:
            grad_in = dot(gpre[rows_at(t + 1), :], wh[...], NT)
        n, rstd = normalize(res[rows_at(t), :])
        gr = cb[rows_at(t), :].astype(F32) + norm_pull(e, gm, n, rstd)
        gres[rows_at(t), :] = gr
        low = gr.astype(BF)
        nm[rows_at(t), :] = low
        gctx[fields_at(t)] = dot(low, wp[...], NT).astype(BF).reshape(per, TF, D)
        mlp_gain, mlp_bias = mlp_gain + row_sums(e * n), mlp_bias + row_sums(e)
        send_rims(fields_at(t))
        place(f"E{t}")()

    pj = pn.chunks
    place("P")()
    put(pj, 0, D, dot(ctx[...], nm[...], TN))
    place("P1")()

    grad_joined = gpre

    def joined(g, j):
        return slice((3 * g + j) * WIDE, (3 * g + j + 1) * WIDE)

    def edge_rows(g, side, f):
        return pl.ds(pl.multiple_of(((g * 2 + side) * FD + f) * C, C), C)

    def back_group(g, hooks):
        def back_fields(i, carry):
            for when, do in hooks.items():
                pl.when(i == when)(do)
            units = [(i * fpi + j, r) for j in range(fpi) for r in range(R)]
            have = []
            for f, r in units:
                win = slice(r * C, (r + 3) * C)
                qd = widened(qb[span(f, r), k_lanes[g]])
                dod = widened(gctx[f, r * C : (r + 1) * C, k_lanes[g]])
                have.append((qd, dod, kv[f, win, k_lanes[g]], kv[f, win, v_lanes[g]], pt[f, g * R + r]))
            dps = [dot(v, dod, NT) for qd, dod, k, v, p in have]
            dss, totals = [], []
            for (qd, dod, k, v, p), dp in zip(have, dps):
                wide = p.astype(F32)
                pd = wide * dp
                total = row_sums(pd)
                totals.append(total)
                dss.append(((pd - wide * total) * SCALE).astype(BF))
            dqs = [diagonal(dot(ds, one[2], TN)).astype(BF) for ds, one in zip(dss, have)]
            dks, dvs = [], []
            for (f, r), ds, (qd, dod, k, v, p) in zip(units, dss, have):
                own = slice(C if r == 0 else 0, 2 * C if r == R - 1 else 3 * C)
                first = r + 1 if r == 0 else r
                dks.append((first, dot(ds[own], qd)))
                dvs.append((first, dot(p[own], dod)))
            for (f, r), o, total in zip(units, dqs, totals):
                grad_joined[span(f, r), joined(g, 0)] = o
                if r in (0, R - 1):
                    dst[g, 0 if r == 0 else 1, pl.ds(f, 1), :] = total
            for j in range(fpi):
                f = i * fpi + j
                for what, terms in enumerate((dks, dvs)):
                    for row in range(1, R + 1):
                        total = None
                        for first, term in terms[j * R : (j + 1) * R]:
                            if first <= row < first + term.shape[0] // C:
                                piece = term[(row - first) * C : (row - first + 1) * C]
                                total = piece if total is None else total + piece
                        if row in (1, R):
                            edge[edge_rows(g, 0 if row == 1 else 1, f), what * WIDE : (what + 1) * WIDE] = total
                        else:
                            grad_joined[span(f, row - 1), joined(g, what + 1)] = total.astype(BF)
            return carry

        lax.fori_loop(0, FD // fpi, back_fields, 0)
        to_up = remote(dst.at[g, 0], hdst.at[g, 1], back_s.at[4 + 2 * g], back_r.at[5 + 2 * g], up)
        to_dn = remote(dst.at[g, 1], hdst.at[g, 0], back_s.at[5 + 2 * g], back_r.at[4 + 2 * g], down)
        pl.when(has_up)(to_up.start)
        pl.when(has_down)(to_dn.start)
        return to_up, to_dn

    def rim_part(h):
        return pl.ds(h * half, half)

    def back_edges(g, sent):
        for to_up, to_dn in sent:
            pl.when(has_up)(to_dn.wait_recv)
            pl.when(has_down)(to_up.wait_recv)

        def back_rims(h):
            units = [(h * half + j, side) for j in range(half) for side in range(2)]
            oks, rows = (has_up, has_down), (0, R - 1)
            have = []
            for f, side in units:
                qd = widened(hq[side, f * C : (f + 1) * C, k_lanes[g]])
                dod = widened(hg[side, f, :, k_lanes[g]])
                keys = slice((rows[side] + 1) * C, (rows[side] + 2) * C)
                have.append((qd, dod, kv[f, keys, k_lanes[g]], kv[f, keys, v_lanes[g]]))
            scores = [dot(k, qd, NT) for qd, dod, k, v in have]
            dps = [dot(v, dod, NT) for qd, dod, k, v in have]
            ps, dss = [], []
            for (f, side), s, dp in zip(units, scores, dps):
                s = (s + biasb[f]) * (SCALE * LOG2E) - hlse[side, pl.ds(f * 2 + g, 1), :]
                p = jnp.where(oks[side], jnp.exp2(s), 0.0)
                ds = p * (dp - hdst[g, side, pl.ds(f, 1), :]) * SCALE
                ps.append(p.astype(BF))
                dss.append(jnp.where(oks[side], ds, 0.0).astype(BF))
            dks = [dot(ds, one[0]) for ds, one in zip(dss, have)]
            dvs = [dot(p, one[1]) for p, one in zip(ps, have)]
            held = [edge[edge_rows(g, side, f), :] for f, side in units]
            for (f, side), dk, dv, own in zip(units, dks, dvs, held):
                dk = own[:, :WIDE] + jnp.where(oks[side], dk, 0.0)
                dv = own[:, WIDE:] + jnp.where(oks[side], dv, 0.0)
                grad_joined[span(f, rows[side]), joined(g, 1)] = dk.astype(BF)
                grad_joined[span(f, rows[side]), joined(g, 2)] = dv.astype(BF)

        for h in range(2):
            if g == 0:
                pl.when(has_up)(lambda: arrived(hg.at[0, rim_part(h)], rim_r.at[0, h]))
                pl.when(has_down)(lambda: arrived(hg.at[1, rim_part(h)], rim_r.at[1, h]))
            back_rims(h)
            place(f"X{2 * g + h + 1}")()
        put(pj + 1 + g, 0, D, dot(normed[...], grad_joined[:, 3 * g * WIDE : 3 * (g + 1) * WIDE], TN))
        place(f"C{g}")()

    sent0 = back_group(0, {i: place(f"A{i}") for i in range(4)})
    sent1 = back_group(1, {i: place(f"B{i}") for i in range(4)})
    place("X")()
    back_edges(0, ((l_up, l_dn), sent0))
    back_edges(1, (sent1,))

    for t in range(tiles):
        nm[rows_at(t), :] = (res[rows_at(t), :] + dot(act[rows_at(t), :], wo[...])).astype(BF)
        place(f"D{t}")()
    layer_copy = pltpu.make_async_copy(nm, out_layer, out_sem.at[0])
    layer_copy.start()
    attn_gain, attn_bias = zero, zero

    def grad_of(t):
        e = None
        for g in range(2):
            for j in range(3):
                w = wq[:, j * D + g * WIDE : j * D + (g + 1) * WIDE]
                term = dot(grad_joined[rows_at(t), joined(g, j)], w, NT)
                e = term if e is None else e + term
        return e

    grad_in = grad_of(0)
    for t in range(tiles):
        e = grad_in
        if t + 1 < tiles:
            grad_in = grad_of(t + 1)
        n, rstd = normalize(pb[fields_at(t)].reshape(tile, D).astype(F32))
        gres[rows_at(t), :] += norm_pull(e, ga, n, rstd)
        attn_gain, attn_bias = attn_gain + row_sums(e * n), attn_bias + row_sums(e)
        place(f"F{t}")()

    patch_copy = pltpu.make_async_copy(gres, out_patch, out_sem.at[1])
    patch_copy.start()
    vec[...] = jnp.concatenate([attn_gain, attn_bias, mlp_gain, mlp_bias, zero, zero, zero, zero], axis=0)

    for name in ("V0", "V1", "V2", "T"):
        place(name)()
    while any(a <= b for a, b in zip(reached, last_step)):
        for k in sorted(range(vec_at + 1), key=lambda k: reached[k] - last_step[k], reverse=True):
            hook(codes[k])()

    for to_up, to_dn in halo_copies:
        pl.when(has_up)(to_up.wait_send)
        pl.when(has_down)(to_dn.wait_send)
    for h in range(2):
        pl.when(has_up)(lambda: arrived(hg.at[1, rim_part(h)], rim_s.at[0, h]))
        pl.when(has_down)(lambda: arrived(hg.at[0, rim_part(h)], rim_s.at[1, h]))
    for to_up, to_dn in ((l_up, l_dn), sent0, sent1):
        pl.when(has_up)(to_up.wait_send)
        pl.when(has_down)(to_dn.wait_send)
    layer_copy.wait()
    patch_copy.wait()
    pltpu.make_async_copy(vec, out_vec, in_sem.at[0]).wait()
    for part in every:
        finish(part)


def widen(plan, *refs):
    pn = plan
    np_ = len(pn.sizes)
    ag, vec, layer, patch = refs[:np_], refs[np_], refs[np_ + 1], refs[np_ + 2]
    o_layer, o_patch, o_ag, o_ab, o_qkv, o_proj, o_mg, o_mb, o_hid, o_out = refs[np_ + 3 : np_ + 13]
    sc = list(refs[np_ + 13 :])
    low, wide = sc[:np_], sc[np_ : 2 * np_]
    kept_layer, kept_patch, in_sem, out_sem, pass_sem = sc[2 * np_ :]
    D = pn.width
    loads = [pltpu.make_async_copy(ag[p], low[p], in_sem.at[p]) for p in range(np_)]
    for c in loads:
        c.start()
    through = [
        (pltpu.make_async_copy(a, b, pass_sem.at[2 * i]), pltpu.make_async_copy(b, c, pass_sem.at[2 * i + 1]))
        for i, (a, b, c) in enumerate(((layer, kept_layer, o_layer), (patch, kept_patch, o_patch)))
    ]
    for arrive, _ in through:
        arrive.start()
    for i, o in enumerate((o_ag, o_ab, o_mg, o_mb)):
        o[...] = vec[i : i + 1, :].reshape(D)
    stores = []

    def store(src, dst):
        c = pltpu.make_async_copy(src, dst, out_sem.at[len(stores)])
        c.start()
        stores.append(c)

    def spread(p, start, rows, blocks, col):
        for j in range(blocks):
            wide[p][:, col + j * 128 : col + (j + 1) * 128] = low[p][
                start + j * rows : start + (j + 1) * rows, :
            ].astype(F32)

    for p in range(np_):
        loads[p].wait()
        if p == np_ - 1:
            for arrive, leave in through:
                arrive.wait()
                leave.start()
        if p < pn.chunks:
            spread(p, 0, CHUNK, D // 128, 0)
            store(wide[p].at[:, pl.ds(0, D)], o_out.at[pl.ds(p * CHUNK, CHUNK)])
            spread(p, CHUNK * (D // 128), D, CHUNK // 128, D)
            store(wide[p].at[:, pl.ds(D, CHUNK)], o_hid.at[:, pl.ds(p * CHUNK, CHUNK)])
        elif p == pn.chunks:
            spread(p, 0, D, D // 128, 0)
            store(wide[p], o_proj)
        else:
            g = p - pn.chunks - 1
            spread(p, 0, D, 3 * WIDE // 128, 0)
            for j in range(3):
                store(
                    wide[p].at[:, pl.ds(j * WIDE, WIDE)],
                    o_qkv.at[:, pl.ds(j * D + g * WIDE, WIDE)],
                )
    for c in stores + [leave for _, leave in through]:
        c.wait()


def per_device(mesh, patches, segment_ids, gain_attn, bias_attn, w_qkv, w_proj, gain_mlp, bias_mlp, w_hidden, w_output, cotangent):
    fields, rows, cols, width = patches.shape
    ff = w_hidden.shape[1]
    pn = Plan(mesh, fields, rows, cols, width, ff)
    np_ = len(pn.sizes)
    T, TF, D, C, R, FD = pn.tokens, pn.tf, width, cols, rows, fields
    L, Z = pn.lats, pn.zs
    anywhere = pl.BlockSpec(memory_space=pl.ANY)
    vmem = pl.BlockSpec(memory_space=pltpu.VMEM)
    V = pltpu.VMEM
    dma = pltpu.SemaphoreType.DMA
    scratch = [
        V((D, 3 * D), BF), V((D, D), BF), V((D, ff), BF), V((ff, D), BF),
        V((FD, TF, D), BF), V((T, D), BF), V(segment_ids.shape, jnp.int32), V((2, FD, C, D), BF),
        V((T, D), BF), V((T, D), BF), V((FD, TF + 2 * C, 2 * D), BF), V((FD, 2 * R, 3 * C, WIDE), BF),
        V((T, D), BF), V((T, D), F32), V((T, D), BF), V((T, D), F32),
        V((T, ff), BF), V((T, ff), BF), V((FD, TF, D), BF),
        V((max(4 * FD * C, T), 2 * WIDE), F32),
        V((2, FD * C, D), BF), V((2, FD, C, D), BF),
        V((2, 2 * FD, WIDE), F32), V((2, 2 * FD, WIDE), F32), V((2, 2, FD, WIDE), F32), V((2, 2, FD, WIDE), F32),
        V((WIDE, WIDE), BF), V((FD, C, WIDE), F32),
        V((8, D), F32), V((Z, 8, D), F32), V((L, 8, D), F32), V((2, 8, D), F32),
    ]
    scratch += [V((n, 128), BF) for n in pn.sizes]
    scratch += [V((n, 128), BF) for n in pn.landing]
    scratch += [V((n, 128), BF) for n in pn.sizes]
    scratch += [
        dma((7,)), dma((2 + pn.n_subs,)), dma((2, 2)), dma((2, 2)), dma((2, 2)), dma((2, 2)), dma((8,)), dma((8,)),
        dma((pn.n_subs, 8)), dma((pn.n_subs, 8)), dma((3,)), dma((3,)),
    ]
    shape = jax.ShapeDtypeStruct
    outs = pl.pallas_call(
        functools.partial(body, pn),
        out_shape=[shape((T, D), BF), shape((T, D), F32), shape((8, D), F32)]
        + [shape((n, 128), BF) for n in pn.sizes],
        in_specs=[anywhere, anywhere, vmem, vmem, anywhere, anywhere, vmem, vmem, anywhere, anywhere, anywhere],
        out_specs=[anywhere] * (3 + np_),
        scratch_shapes=scratch,
        compiler_params=pltpu.CompilerParams(
            collective_id=0, has_side_effects=True, vmem_limit_bytes=62 * 2**20
        ),
        name="block",
    )(
        patches.reshape(FD, TF, D), segment_ids, gain_attn, bias_attn, w_qkv, w_proj, gain_mlp, bias_mlp,
        w_hidden, w_output, cotangent.reshape(T, D),
    )
    layer, patch, vec = outs[:3]
    ags = outs[3:]
    wides = [(D, D + CHUNK)] * pn.chunks + [(D, D)] + [(D, 3 * WIDE)] * 2
    final = pl.pallas_call(
        functools.partial(widen, pn),
        out_shape=[
            shape((T, D), BF), shape((T, D), F32), shape((D,), F32), shape((D,), F32), shape((D, 3 * D), F32),
            shape((D, D), F32), shape((D,), F32), shape((D,), F32), shape((D, ff), F32), shape((ff, D), F32),
        ],
        in_specs=[anywhere] * np_ + [vmem, anywhere, anywhere],
        out_specs=[anywhere, anywhere, vmem, vmem, anywhere, anywhere, vmem, vmem, anywhere, anywhere],
        scratch_shapes=[V((n, 128), BF) for n in pn.sizes]
        + [V(s, F32) for s in wides]
        + [V((T, D), BF), V((T, D), F32), dma((np_,)), dma((2 * pn.chunks + 7,)), dma((4,))],
        compiler_params=pltpu.CompilerParams(vmem_limit_bytes=62 * 2**20),
        name="widen",
    )(*ags, vec, layer, patch)
    block = (FD, R, C, D)
    return (final[0].reshape(block), final[1].reshape(block)) + tuple(final[2:])


def solution(mesh):
    band = P("fld", "lat", None, None)
    return jax.shard_map(
        functools.partial(per_device, mesh),
        mesh=mesh,
        in_specs=(band, P("fld", None, None)) + (P(),) * 8 + (band,),
        out_specs=(band, band) + (P(),) * 8,
        check_vma=False,
    )
```

```python
import functools
import math

import jax
import jax.numpy as jnp
from jax import lax
from jax.experimental import pallas as pl
from jax.experimental.pallas import tpu as pltpu
from jax.sharding import PartitionSpec as P

HEAD_DIM = 32
GROUP = 8
WIDE = GROUP * HEAD_DIM
SCALE = HEAD_DIM ** -0.5
LOG2E = math.log2(math.e)
EPS = 1e-6
REACH = 4
NEG = -1e30
CHUNK = 512
BLOCK = 256
FIELDS_AT_ONCE = 2
DIRECT = (5, 6)
Z_FIRST = ()
SCHEDULE = {
    "J2": (0, 1),
    "J4": (0, 2, 3, 1),
    "J6": (2, 3, 4, 5),
    "J8": (4, 6, 7, 5),
    "E0": (0, 1),
    "E1": (6, 7),
    "E2": (2, 3),
    "P1": (4, 5, 8, 9),
    "A1": (8,),
    "A2": (9, 0),
    "A3": (1,),
    "B1": (7,),
    "B2": (0, 6),
    "B3": (2, 1),
    "D0": (4,),
    "D1": (3, 9),
    "D2": (0,),
    "D3": (6,),
    "X": (2,),
    "X1": (1, 5, 4, 0, 8),
    "X2": (3, 7),
    "C0": (9, 6, 10),
    "X3": (8, 1, 2),
    "X4": (10, 5),
    "C1": (0, 4, 12),
    "F1": (3, 0),
    "F2": (1, 7, 12),
    "F3": (9, 2),
    "V0": (14,),
    "T": (6, 1, 8, 3, 5, 10, 14, 7, 9, 4, 8, 12, 10, 14, 2, 6, 5, 7, 9, 3, 12, 14, 2, 8, 3, 4, 10, 5, 6, 4, 12, 5, 8, 7, 6, 9, 8, 7, 9, 10, 10, 12, 12),
}
BF = jnp.bfloat16
F32 = jnp.float32
MESH = pl.DeviceIdType.MESH

NT = (((1,), (1,)), ((), ()))
TN = (((0,), (0,)), ((), ()))


def dot(a, b, dims=None):
    if dims is None:
        return jnp.dot(a, b, preferred_element_type=F32)
    return lax.dot_general(a, b, dims, preferred_element_type=F32)


def normalize(x):
    center = jnp.mean(x, axis=-1, keepdims=True)
    off = x - center
    rstd = lax.rsqrt(jnp.mean(off * off, axis=-1, keepdims=True) + EPS)
    return off * rstd, rstd


def norm_pull(e, gain, n, rstd):
    ge = e * gain
    a = jnp.mean(ge, axis=-1, keepdims=True)
    b = jnp.mean(ge * n, axis=-1, keepdims=True)
    return (ge - a - n * b) * rstd


def gelu_both(u):
    cdf = 0.5 + 0.5 * lax.erf(u * (1.0 / math.sqrt(2.0)))
    density = jnp.exp2((u * u) * (-0.5 * LOG2E)) * (1.0 / math.sqrt(2.0 * math.pi))
    return u * cdf, cdf + u * density


def row_sums(x):
    return jnp.sum(x, axis=0, keepdims=True)


class Plan:
    def __init__(self, mesh, fields, rows, cols, width, ff):
        self.lats = mesh.shape["lat"]
        self.flds = mesh.shape["fld"]
        self.zs = self.flds // 2
        self.fields, self.rows, self.cols = fields, rows, cols
        self.tf = rows * cols
        self.tokens = fields * self.tf
        self.width, self.ff = width, ff
        self.chunks = ff // CHUNK
        self.size_of = {"core": 2, "x": 2, "y": self.lats // 2, "lat": self.lats, "z": self.zs}
        unit = 16 * self.lats * self.flds
        blocks = width // 128
        mlp = CHUNK * blocks + width * (CHUNK // 128)
        rows_needed = [mlp] * self.chunks + [width * blocks] + [width * (3 * WIDE // 128)] * 2
        self.sizes, self.subs = [], []
        for p, n in enumerate(rows_needed):
            n = -(-n // unit) * unit
            self.sizes.append(n)
            if p in Z_FIRST:
                self.subs.append([(0, n, ("core", "z", "lat"))])
            elif p in DIRECT or n % (2 * unit):
                self.subs.append([(0, n, ("core", "lat", "z"))])
            else:
                self.subs.append([(0, n // 2, ("core", "x", "y", "z")), (n // 2, n // 2, ("core", "y", "x", "z"))])
        self.landing = []
        for subs in self.subs:
            total = 0
            for _, n, order in subs:
                for d in order:
                    n //= self.size_of[d]
                    total += n * (self.size_of[d] - 1)
            self.landing.append(total)
        self.n_subs = sum(len(s) for s in self.subs)


def body(plan, *refs):
    pn = plan
    np_ = len(pn.sizes)
    (patches, seg, gain_a, bias_a, w_qkv, w_proj, gain_m, bias_m, w_hid, w_out, cot) = refs[:11]
    out_layer, out_patch, out_vec = refs[11:14]
    out_ag = refs[14 : 14 + np_]
    sc = list(refs[14 + np_ :])

    def take(n):
        got = sc[:n]
        del sc[:n]
        return got

    wq, wp, wh, wo = take(4)
    pb, cb, segv, halo = take(4)
    normed, qb, kv, pt, ctx, res, nm, gres, act, gpre, gctx, edge = take(12)
    hq, hg, lse, hlse, dst, hdst = take(6)
    bm, biasb, vec, vrz, vrx, vrc = take(6)
    sb, rb, ag = take(np_), take(np_), take(np_)
    in_sem, out_sem, halo_s, halo_r, rim_s, rim_r, back_s, back_r, rs_s, rs_r, v_s, v_r = take(12)

    lat = lax.axis_index("lat")
    fld = lax.axis_index("fld")
    core = lax.rem(fld, 2)
    z = lax.div(fld, 2)
    x = lax.rem(lat, 2)
    y = lax.div(lat, 2)
    L, Z, Y = pn.lats, pn.zs, pn.lats // 2
    FD, R, C, TF, T, D, FF = pn.fields, pn.rows, pn.cols, pn.tf, pn.tokens, pn.width, pn.ff

    ins = [(patches, pb), (w_qkv, wq), (seg, segv), (cot, cb), (w_out, wo), (w_proj, wp), (w_hid, wh)]
    loads = [pltpu.make_async_copy(s, d, in_sem.at[i]) for i, (s, d) in enumerate(ins)]
    loads[0].start()
    loads[1].start()

    me = {"core": core, "x": x, "y": y, "lat": lat, "z": z}

    def device(d, i):
        if d == "core":
            return lat, z * 2 + i
        if d == "x":
            return y * 2 + i, fld
        if d == "y":
            return i * 2 + x, fld
        if d == "lat":
            return i, fld
        return lat, i * 2 + core

    def peers(d):
        n = pn.size_of[d]
        places = [lax.rem(me[d] + k, n) for k in range(1, n)]
        return [(i, device(d, i)) for i in places]

    barrier = pltpu.get_barrier_semaphore()
    everyone = peers("core") + peers("lat") + peers("z")
    for _, dev in everyone:
        pl.semaphore_signal(barrier, inc=1, device_id=dev, device_id_type=MESH)
    pl.semaphore_wait(barrier, len(everyone))

    up, down = (lat - 1, fld), (lat + 1, fld)
    has_up, has_down = lat > 0, lat < L - 1

    def remote(src, dst, s, r, dev):
        return pltpu.make_async_remote_copy(
            src_ref=src, dst_ref=dst, send_sem=s, recv_sem=r, device_id=dev, device_id_type=MESH
        )

    def arrived(ref, sem):
        pltpu.make_async_copy(ref, ref, sem).wait()

    half = FD // 2
    halo_copies = []
    for h in range(2):
        some = pl.ds(h * half, half)
        to_up = remote(patches.at[some, pl.ds(0, C)], halo.at[1, some], halo_s.at[0, h], halo_r.at[1, h], up)
        to_dn = remote(patches.at[some, pl.ds(TF - C, C)], halo.at[0, some], halo_s.at[1, h], halo_r.at[0, h], down)
        pl.when(has_up)(to_up.start)
        pl.when(has_down)(to_dn.start)
        halo_copies.append((to_up, to_dn))
    for c in loads[2:]:
        c.start()

    def spot(off, n):
        return pl.ds(pl.multiple_of(off, 16), n)

    class Part:
        def __init__(self, p, number, start, n, order, land):
            self.p, self.number, self.order = p, number, order
            self.off, self.len, self.land = [start], [n], []
            for d in order:
                g = pn.size_of[d]
                n = n // g
                self.land.append(land)
                land += n * (g - 1)
                self.off.append(self.off[-1] + me[d] * n)
                self.len.append(n)
            self.end = land

        def moved(self, i):
            return self.len[i + 1] * (pn.size_of[self.order[i]] - 1)

        def scatter(self, i):
            n = self.len[i + 1]
            for k, (j, dev) in enumerate(peers(self.order[i])):
                src = sb[self.p].at[spot(self.off[i] + j * n, n)]
                dst = rb[self.p].at[pl.ds(self.land[i] + k * n, n)]
                remote(src, dst, rs_s.at[self.number, i], rs_r.at[self.number, i], dev).start()

        def add(self, i):
            n = self.len[i + 1]
            d = self.order[i]
            arrived(rb[self.p].at[pl.ds(self.land[i], self.moved(i))], rs_r.at[self.number, i])
            mine = spot(self.off[i + 1], n)
            total = sb[self.p][mine, :].astype(F32)
            for k in range(pn.size_of[d] - 1):
                total = total + rb[self.p][self.land[i] + k * n : self.land[i] + (k + 1) * n, :].astype(F32)
            to = ag if i == len(self.order) - 1 else sb
            to[self.p][mine, :] = total.astype(BF)

        def gather(self, i):
            s = 4 + i
            mine = ag[self.p].at[spot(self.off[i + 1], self.len[i + 1])]
            for _, dev in peers(self.order[i]):
                remote(mine, mine, rs_s.at[self.number, s], rs_r.at[self.number, s], dev).start()

        def gathered(self, i):
            arrived(ag[self.p].at[pl.ds(0, self.moved(i))], rs_r.at[self.number, 4 + i])

        def step(self, s):
            nd = len(self.order)
            if s < nd:
                if s > 0:
                    self.add(s - 1)
                self.scatter(s)
            elif s == nd:
                self.add(nd - 1)
                self.gather(nd - 1)
            else:
                self.gathered(2 * nd - s)
                if s < 2 * nd:
                    self.gather(2 * nd - 1 - s)

        def finish(self):
            for i in range(len(self.order)):
                for s in (i, 4 + i):
                    arrived(sb[self.p].at[pl.ds(0, self.moved(i))], rs_s.at[self.number, s])

    parts, number = [], 0
    for p in range(np_):
        mine, land = [], 0
        for start, n, order in pn.subs[p]:
            mine.append(Part(p, number, start, n, order, land))
            land = mine[-1].end
            number += 1
        parts.append(mine)
    every = [part for mine in parts for part in mine]
    vec_at = len(every)
    reached = [0] * (vec_at + 1)
    last_step = [2 * len(part.order) for part in every] + [3]

    def out_copy(part):
        rows = pl.ds(part.off[0], part.len[0])
        return pltpu.make_async_copy(ag[part.p].at[rows], out_ag[part.p].at[rows], out_sem.at[2 + part.number])

    codes = [2 * p + i for p, mine in enumerate(parts) for i in range(len(mine))] + [2 * np_]
    number_of = {code: k for k, code in enumerate(codes)}

    def hook(*some):
        steps = []
        for code in some:
            k = number_of.get(code, vec_at + 1)
            if k <= vec_at and reached[k] <= last_step[k]:
                steps.append((k, reached[k]))
                reached[k] += 1

        def run():
            for k, s in steps:
                if k == vec_at:
                    vec_step(s)
                    continue
                every[k].step(s)
                if s == last_step[k]:
                    out_copy(every[k]).start()

        return run

    def place(name):
        return hook(*SCHEDULE.get(name, ()))

    rounds = ((vrz, "z"), (vrx, "lat"), (vrc, "core"))

    def vec_step(s):
        if s > 0:
            buf, d = rounds[s - 1]
            count = pn.size_of[d]
            arrived(buf.at[pl.ds(0, count - 1)], v_r.at[s - 1])
            arrived(buf.at[pl.ds(0, count - 1)], v_s.at[s - 1])
            total = buf[0]
            for k in range(1, count):
                total = total + buf[k]
            vec[...] = total
        if s < 3:
            buf, d = rounds[s]
            buf[me[d]] = vec[...]
            for _, dev in peers(d):
                remote(vec, buf.at[me[d]], v_s.at[s], v_r.at[s], dev).start()
        else:
            pltpu.make_async_copy(vec, out_vec, in_sem.at[0]).start()

    def finish(part):
        part.finish()
        out_copy(part).wait()

    def put(p, start, stride, value):
        rows, lanes = value.shape
        low = value.astype(BF)
        for j in range(lanes // 128):
            at = start + j * stride
            sb[p][at : at + rows, :] = low[:, j * 128 : (j + 1) * 128]

    rid = lax.broadcasted_iota(jnp.int32, (WIDE, WIDE), 0) // HEAD_DIM
    cid = lax.broadcasted_iota(jnp.int32, (WIDE, WIDE), 1) // HEAD_DIM
    same = jnp.where(rid == cid, 1.0, 0.0)
    bm[...] = same.astype(BF)

    ga, ba = gain_a[...].reshape(1, D), bias_a[...].reshape(1, D)
    gm, bmlp = gain_m[...].reshape(1, D), bias_m[...].reshape(1, D)
    loads[0].wait()

    per = max(1, 256 // TF)
    tile = per * TF
    tiles = T // tile

    def rows_at(t):
        return slice(t * tile, (t + 1) * tile)

    def fields_at(t):
        return slice(t * per, (t + 1) * per)

    def norm_one(t):
        n, _ = normalize(pb[fields_at(t)].reshape(tile, D).astype(F32))
        normed[rows_at(t), :] = (n * ga + ba).astype(BF)

    norm_one(0)
    loads[1].wait()
    for t in range(tiles):
        if t + 1 < tiles:
            norm_one(t + 1)
        qb[rows_at(t), :] = dot(normed[rows_at(t), :], wq[:, :D]).astype(BF)
        part = dot(normed[rows_at(t), :], wq[:, D:]).astype(BF)
        kv[fields_at(t), C : C + TF, :] = part.reshape(per, TF, 2 * D)

    loads[2].wait()
    kcol = lax.broadcasted_iota(jnp.int32, (C, WIDE), 0)
    qcol = lax.rem(lax.broadcasted_iota(jnp.int32, (C, WIDE), 1), C)
    away = jnp.abs(kcol - qcol)
    near = jnp.minimum(away, C - away) <= REACH
    diag = lax.broadcasted_iota(jnp.int32, (C, C), 0) == lax.broadcasted_iota(jnp.int32, (C, C), 1)
    for f in range(FD):
        line = segv[f, 0:1, :].astype(F32)
        across = jnp.concatenate([line] * GROUP, axis=1)
        along = jnp.sum(jnp.where(diag, line, 0.0), axis=1, keepdims=True)
        biasb[f] = jnp.where(jnp.logical_and(near, along == across), 0.0, NEG)
    pole_top = jnp.where(has_up, 0.0, NEG)
    pole_bottom = jnp.where(has_down, 0.0, NEG)

    lane_head = lax.broadcasted_iota(jnp.int32, (HEAD_DIM, WIDE), 1) // HEAD_DIM

    def diagonal(o):
        total = o[0:HEAD_DIM]
        for h in range(1, GROUP):
            total = jnp.where(lane_head == h, o[h * HEAD_DIM : (h + 1) * HEAD_DIM], total)
        return total

    def widened(q):
        return jnp.concatenate([q] * GROUP, axis=0) * bm[...]

    fpi = min(FIELDS_AT_ONCE, FD)

    def span(f, row):
        return pl.ds(pl.multiple_of(f * TF + row * C, C), C)

    k_lanes = [slice(g * WIDE, (g + 1) * WIDE) for g in range(2)]
    v_lanes = [slice(D + g * WIDE, D + (g + 1) * WIDE) for g in range(2)]

    def attend(rows, i, carry):
        units = [(i * fpi + j, g, r) for j in range(fpi) for g in range(2) for r in rows]
        scores = []
        for f, g, r in units:
            k = kv[f, r * C : (r + 3) * C, k_lanes[g]]
            scores.append(dot(k, widened(qb[span(f, r), k_lanes[g]]), NT))
        low, logs = [], []
        for (f, g, r), s in zip(units, scores):
            bias = biasb[f]
            first = bias + pole_top if r == 0 else bias
            third = bias + pole_bottom if r == R - 1 else bias
            s = s + jnp.concatenate([first, bias, third], axis=0)
            m = jnp.max(s, axis=0, keepdims=True)
            p = jnp.exp2((s - m) * (SCALE * LOG2E))
            total = row_sums(p)
            logs.append(m * (SCALE * LOG2E) + jnp.log2(total) if r in (0, R - 1) else None)
            low.append((p * (1.0 / total)).astype(BF))
        outs = []
        for (f, g, r), p in zip(units, low):
            v = kv[f, r * C : (r + 3) * C, v_lanes[g]]
            outs.append(diagonal(dot(p, v, TN)).astype(BF))
        for (f, g, r), p, log, o in zip(units, low, logs, outs):
            pt[f, g * R + r] = p
            ctx[span(f, r), k_lanes[g]] = o
            if r in (0, R - 1):
                lse[0 if r == 0 else 1, pl.ds(f * 2 + g, 1), :] = log
        return carry

    if R > 2:
        lax.fori_loop(0, FD // fpi, functools.partial(attend, range(1, R - 1)), 0)

    loads[3].wait()
    loads[4].wait()
    for j in range(FF // BLOCK):
        some = slice(j * BLOCK, (j + 1) * BLOCK)
        gpre[:, some] = dot(cb[...], wo[some, :], NT).astype(BF)

    for h in range(2):
        some = slice(h * half, (h + 1) * half)
        flat = slice(h * half * C, (h + 1) * half * C)
        for side, ok, copy in ((0, has_up, halo_copies[h][1]), (1, has_down, halo_copies[h][0])):
            pl.when(ok)(copy.wait_recv)

            @pl.when(jnp.logical_not(ok))
            def _():
                halo[side, some] = jnp.zeros((half, C, D), BF)

            n, _unused = normalize(halo[side, some].reshape(half * C, D).astype(F32))
            low = (n * ga + ba).astype(BF)
            hq[side, flat, :] = dot(low, wq[:, :D]).astype(BF)
            start = 0 if side == 0 else TF + C
            kv[some, start : start + C, :] = dot(low, wq[:, D:]).astype(BF).reshape(half, C, 2 * D)
        turns = half // fpi
        lax.fori_loop(h * turns, (h + 1) * turns, functools.partial(attend, (0, R - 1)), 0)

    loads[5].wait()
    for t in range(tiles):
        r = pb[fields_at(t)].reshape(tile, D).astype(F32) + dot(ctx[rows_at(t), :], wp[...])
        res[rows_at(t), :] = r
        n, _ = normalize(r)
        nm[rows_at(t), :] = (n * gm + bmlp).astype(BF)

    loads[6].wait()
    blocks = FF // BLOCK
    in_chunk = CHUNK // BLOCK

    def hidden_block(j):
        return slice(j * BLOCK, (j + 1) * BLOCK)

    def kept(ref, j):
        return ref.at[pl.ds(0, T), pl.ds((j % 2) * BLOCK, BLOCK)]

    def mlp_in(j):
        kept(gres, j)[...] = dot(nm[...], wh[:, hidden_block(j)])

    def mlp_mid(j):
        a, da = gelu_both(kept(gres, j)[...])
        act[:, hidden_block(j)] = a.astype(BF)
        gpre[:, hidden_block(j)] = (da * gpre[:, hidden_block(j)].astype(F32)).astype(BF)

    def mlp_out(j):
        c, part = j // in_chunk, j % in_chunk
        put(c, part * BLOCK, CHUNK, dot(act[:, hidden_block(j)], cb[...], TN))
        start = CHUNK * (D // 128) + part * (BLOCK // 128) * D
        put(c, start, D, dot(nm[...], gpre[:, hidden_block(j)], TN))

    mlp_in(0)
    for j in range(blocks):
        if j + 1 < blocks:
            mlp_in(j + 1)
        mlp_mid(j)
        if j > 0:
            mlp_out(j - 1)
        place(f"J{j}")()
    mlp_out(blocks - 1)
    place(f"J{blocks}")()

    zero = jnp.zeros((1, D), F32)

    mlp_gain, mlp_bias = zero, zero

    l_up = remote(lse.at[0], hlse.at[1], back_s.at[2], back_r.at[3], up)
    l_dn = remote(lse.at[1], hlse.at[0], back_s.at[3], back_r.at[2], down)
    pl.when(has_up)(l_up.start)
    pl.when(has_down)(l_dn.start)

    head_rows = lax.broadcasted_iota(jnp.int32, (2 * GROUP, D), 0) == lax.broadcasted_iota(
        jnp.int32, (2 * GROUP, D), 1
    ) // HEAD_DIM
    head_rows = jnp.where(head_rows, 1.0, 0.0).astype(BF)
    own_head = lax.broadcasted_iota(jnp.int32, (GROUP, WIDE), 0) == lax.broadcasted_iota(
        jnp.int32, (GROUP, WIDE), 1
    ) // HEAD_DIM

    def rim_totals(some):
        spots = [(f, side) for f in range(some.start, some.stop) for side in range(2)]
        terms = []
        for f, side in spots:
            row = 0 if side == 0 else R - 1
            mine = ctx[f * TF + row * C : f * TF + (row + 1) * C, :].astype(F32)
            terms.append(mine * gctx[f, row * C : (row + 1) * C, :].astype(F32))
        terms = jnp.concatenate(terms, axis=0)
        high = terms.astype(BF)
        rest = (terms - high.astype(F32)).astype(BF)
        sums = dot(head_rows, high, NT) + dot(head_rows, rest, NT)
        for i, (f, side) in enumerate(spots):
            across = jnp.concatenate([sums[:, i * C : (i + 1) * C]] * GROUP, axis=1)
            for g in range(2):
                own = jnp.where(own_head, across[g * GROUP : (g + 1) * GROUP], 0.0)
                dst[side, 2 * f + g : 2 * f + g + 1, :] = row_sums(own)

    def send_rims(some):
        some = pl.ds(some.start, some.stop - some.start)
        h = some.start // half
        to_up = remote(gctx.at[some, pl.ds(0, C)], hg.at[1, some], rim_s.at[0, h], rim_r.at[1, h], up)
        to_dn = remote(gctx.at[some, pl.ds(TF - C, C)], hg.at[0, some], rim_s.at[1, h], rim_r.at[0, h], down)
        pl.when(has_up)(to_up.start)
        pl.when(has_down)(to_dn.start)

    grad_in = dot(gpre[rows_at(0), :], wh[...], NT)
    for t in range(tiles):
        e = grad_in
        if t + 1 < tiles:
            grad_in = dot(gpre[rows_at(t + 1), :], wh[...], NT)
        n, rstd = normalize(res[rows_at(t), :])
        gr = cb[rows_at(t), :].astype(F32) + norm_pull(e, gm, n, rstd)
        gres[rows_at(t), :] = gr
        low = gr.astype(BF)
        nm[rows_at(t), :] = low
        gctx[fields_at(t)] = dot(low, wp[...], NT).astype(BF).reshape(per, TF, D)
        mlp_gain, mlp_bias = mlp_gain + row_sums(e * n), mlp_bias + row_sums(e)
        rim_totals(fields_at(t))
        send_rims(fields_at(t))
        place(f"E{t}")()

    d_up = remote(dst.at[0], hdst.at[1], back_s.at[4], back_r.at[5], up)
    d_dn = remote(dst.at[1], hdst.at[0], back_s.at[5], back_r.at[4], down)
    pl.when(has_up)(d_up.start)
    pl.when(has_down)(d_dn.start)
    pj = pn.chunks
    place("P")()
    put(pj, 0, D, dot(ctx[...], nm[...], TN))
    place("P1")()

    grad_joined = gpre

    def joined(g, j):
        return slice((3 * g + j) * WIDE, (3 * g + j + 1) * WIDE)

    def edge_rows(g, side, f):
        return pl.ds(pl.multiple_of(((g * 2 + side) * FD + f) * C, C), C)

    def back_group(g, hooks):
        def back_fields(i, carry):
            for when, do in hooks.items():
                pl.when(i == when)(do)
            units = [(i * fpi + j, r) for j in range(fpi) for r in range(R)]
            have = []
            for f, r in units:
                win = slice(r * C, (r + 3) * C)
                qd = widened(qb[span(f, r), k_lanes[g]])
                dod = widened(gctx[f, r * C : (r + 1) * C, k_lanes[g]])
                have.append((qd, dod, kv[f, win, k_lanes[g]], kv[f, win, v_lanes[g]], pt[f, g * R + r]))
            dps = [dot(v, dod, NT) for qd, dod, k, v, p in have]
            dss = []
            for (qd, dod, k, v, p), dp in zip(have, dps):
                wide = p.astype(F32)
                pd = wide * dp
                total = row_sums(pd)
                dss.append(((pd - wide * total) * SCALE).astype(BF))
            dqs = [diagonal(dot(ds, one[2], TN)).astype(BF) for ds, one in zip(dss, have)]
            dks, dvs = [], []
            for (f, r), ds, (qd, dod, k, v, p) in zip(units, dss, have):
                own = slice(C if r == 0 else 0, 2 * C if r == R - 1 else 3 * C)
                first = r + 1 if r == 0 else r
                dks.append((first, dot(ds[own], qd)))
                dvs.append((first, dot(p[own], dod)))
            for (f, r), o in zip(units, dqs):
                grad_joined[span(f, r), joined(g, 0)] = o
            for j in range(fpi):
                f = i * fpi + j
                for what, terms in enumerate((dks, dvs)):
                    for row in range(1, R + 1):
                        total = None
                        for first, term in terms[j * R : (j + 1) * R]:
                            if first <= row < first + term.shape[0] // C:
                                piece = term[(row - first) * C : (row - first + 1) * C]
                                total = piece if total is None else total + piece
                        if row in (1, R):
                            edge[edge_rows(g, 0 if row == 1 else 1, f), what * WIDE : (what + 1) * WIDE] = total
                        else:
                            grad_joined[span(f, row - 1), joined(g, what + 1)] = total.astype(BF)
            return carry

        lax.fori_loop(0, FD // fpi, back_fields, 0)
    def rim_part(h):
        return pl.ds(h * half, half)

    def back_edges(g, sent):
        for to_up, to_dn in sent:
            pl.when(has_up)(to_dn.wait_recv)
            pl.when(has_down)(to_up.wait_recv)

        def back_rims(h):
            units = [(h * half + j, side) for j in range(half) for side in range(2)]
            oks, rows = (has_up, has_down), (0, R - 1)
            have = []
            for f, side in units:
                qd = widened(hq[side, f * C : (f + 1) * C, k_lanes[g]])
                dod = widened(hg[side, f, :, k_lanes[g]])
                keys = slice((rows[side] + 1) * C, (rows[side] + 2) * C)
                have.append((qd, dod, kv[f, keys, k_lanes[g]], kv[f, keys, v_lanes[g]]))
            scores = [dot(k, qd, NT) for qd, dod, k, v in have]
            dps = [dot(v, dod, NT) for qd, dod, k, v in have]
            ps, dss = [], []
            for (f, side), s, dp in zip(units, scores, dps):
                s = (s + biasb[f]) * (SCALE * LOG2E) - hlse[side, pl.ds(f * 2 + g, 1), :]
                p = jnp.where(oks[side], jnp.exp2(s), 0.0)
                ds = p * (dp - hdst[side, pl.ds(f * 2 + g, 1), :]) * SCALE
                ps.append(p.astype(BF))
                dss.append(jnp.where(oks[side], ds, 0.0).astype(BF))
            dks = [dot(ds, one[0]) for ds, one in zip(dss, have)]
            dvs = [dot(p, one[1]) for p, one in zip(ps, have)]
            held = [edge[edge_rows(g, side, f), :] for f, side in units]
            for (f, side), dk, dv, own in zip(units, dks, dvs, held):
                dk = own[:, :WIDE] + jnp.where(oks[side], dk, 0.0)
                dv = own[:, WIDE:] + jnp.where(oks[side], dv, 0.0)
                grad_joined[span(f, rows[side]), joined(g, 1)] = dk.astype(BF)
                grad_joined[span(f, rows[side]), joined(g, 2)] = dv.astype(BF)

        for h in range(2):
            if g == 0:
                pl.when(has_up)(lambda: arrived(hg.at[0, rim_part(h)], rim_r.at[0, h]))
                pl.when(has_down)(lambda: arrived(hg.at[1, rim_part(h)], rim_r.at[1, h]))
            back_rims(h)
            place(f"X{2 * g + h + 1}")()
        put(pj + 1 + g, 0, D, dot(normed[...], grad_joined[:, 3 * g * WIDE : 3 * (g + 1) * WIDE], TN))
        place(f"C{g}")()

    back_group(0, {i: place(f"A{i}") for i in range(4)})
    back_group(1, {i: place(f"B{i}") for i in range(4)})
    for t in range(tiles):
        nm[rows_at(t), :] = (res[rows_at(t), :] + dot(act[rows_at(t), :], wo[...])).astype(BF)
        place(f"D{t}")()
    layer_copy = pltpu.make_async_copy(nm, out_layer, out_sem.at[0])
    layer_copy.start()

    place("X")()
    back_edges(0, ((l_up, l_dn), (d_up, d_dn)))
    back_edges(1, ())

    attn_gain, attn_bias = zero, zero

    def grad_of(t):
        e = None
        for g in range(2):
            for j in range(3):
                w = wq[:, j * D + g * WIDE : j * D + (g + 1) * WIDE]
                term = dot(grad_joined[rows_at(t), joined(g, j)], w, NT)
                e = term if e is None else e + term
        return e

    grad_in = grad_of(0)
    for t in range(tiles):
        e = grad_in
        if t + 1 < tiles:
            grad_in = grad_of(t + 1)
        n, rstd = normalize(pb[fields_at(t)].reshape(tile, D).astype(F32))
        gres[rows_at(t), :] += norm_pull(e, ga, n, rstd)
        attn_gain, attn_bias = attn_gain + row_sums(e * n), attn_bias + row_sums(e)
        place(f"F{t}")()

    patch_copy = pltpu.make_async_copy(gres, out_patch, out_sem.at[1])
    patch_copy.start()
    vec[...] = jnp.concatenate([attn_gain, attn_bias, mlp_gain, mlp_bias, zero, zero, zero, zero], axis=0)
    place("V0")()

    place("T")()
    while any(a <= b for a, b in zip(reached, last_step)):
        for k in sorted(range(vec_at + 1), key=lambda k: reached[k] - last_step[k], reverse=True):
            hook(codes[k])()

    for to_up, to_dn in halo_copies:
        pl.when(has_up)(to_up.wait_send)
        pl.when(has_down)(to_dn.wait_send)
    for h in range(2):
        pl.when(has_up)(lambda: arrived(hg.at[1, rim_part(h)], rim_s.at[0, h]))
        pl.when(has_down)(lambda: arrived(hg.at[0, rim_part(h)], rim_s.at[1, h]))
    for to_up, to_dn in ((l_up, l_dn), (d_up, d_dn)):
        pl.when(has_up)(to_up.wait_send)
        pl.when(has_down)(to_dn.wait_send)
    layer_copy.wait()
    patch_copy.wait()
    pltpu.make_async_copy(vec, out_vec, in_sem.at[0]).wait()
    for part in every:
        finish(part)


def widen(plan, *refs):
    pn = plan
    np_ = len(pn.sizes)
    ag, vec, layer, patch = refs[:np_], refs[np_], refs[np_ + 1], refs[np_ + 2]
    o_layer, o_patch, o_ag, o_ab, o_qkv, o_proj, o_mg, o_mb, o_hid, o_out = refs[np_ + 3 : np_ + 13]
    sc = list(refs[np_ + 13 :])
    low, wide = sc[:np_], sc[np_ : 2 * np_]
    kept_layer, kept_patch, in_sem, out_sem, pass_sem = sc[2 * np_ :]
    D = pn.width
    loads = [pltpu.make_async_copy(ag[p], low[p], in_sem.at[p]) for p in range(np_)]
    for c in loads:
        c.start()
    through = [
        (pltpu.make_async_copy(a, b, pass_sem.at[2 * i]), pltpu.make_async_copy(b, c, pass_sem.at[2 * i + 1]))
        for i, (a, b, c) in enumerate(((layer, kept_layer, o_layer), (patch, kept_patch, o_patch)))
    ]
    for arrive, _ in through:
        arrive.start()
    for i, o in enumerate((o_ag, o_ab, o_mg, o_mb)):
        o[...] = vec[i : i + 1, :].reshape(D)
    stores = []

    def store(src, dst):
        c = pltpu.make_async_copy(src, dst, out_sem.at[len(stores)])
        c.start()
        stores.append(c)

    def spread(p, start, rows, blocks, col):
        for j in range(blocks):
            wide[p][:, col + j * 128 : col + (j + 1) * 128] = low[p][
                start + j * rows : start + (j + 1) * rows, :
            ].astype(F32)

    for p in range(np_):
        loads[p].wait()
        if p == np_ - 1:
            for arrive, leave in through:
                arrive.wait()
                leave.start()
        if p < pn.chunks:
            spread(p, 0, CHUNK, D // 128, 0)
            store(wide[p].at[:, pl.ds(0, D)], o_out.at[pl.ds(p * CHUNK, CHUNK)])
            spread(p, CHUNK * (D // 128), D, CHUNK // 128, D)
            store(wide[p].at[:, pl.ds(D, CHUNK)], o_hid.at[:, pl.ds(p * CHUNK, CHUNK)])
        elif p == pn.chunks:
            spread(p, 0, D, D // 128, 0)
            store(wide[p], o_proj)
        else:
            g = p - pn.chunks - 1
            spread(p, 0, D, 3 * WIDE // 128, 0)
            for j in range(3):
                store(
                    wide[p].at[:, pl.ds(j * WIDE, WIDE)],
                    o_qkv.at[:, pl.ds(j * D + g * WIDE, WIDE)],
                )
    for c in stores + [leave for _, leave in through]:
        c.wait()


def per_device(mesh, patches, segment_ids, gain_attn, bias_attn, w_qkv, w_proj, gain_mlp, bias_mlp, w_hidden, w_output, cotangent):
    fields, rows, cols, width = patches.shape
    ff = w_hidden.shape[1]
    pn = Plan(mesh, fields, rows, cols, width, ff)
    np_ = len(pn.sizes)
    T, TF, D, C, R, FD = pn.tokens, pn.tf, width, cols, rows, fields
    L, Z = pn.lats, pn.zs
    anywhere = pl.BlockSpec(memory_space=pl.ANY)
    vmem = pl.BlockSpec(memory_space=pltpu.VMEM)
    V = pltpu.VMEM
    dma = pltpu.SemaphoreType.DMA
    scratch = [
        V((D, 3 * D), BF), V((D, D), BF), V((D, ff), BF), V((ff, D), BF),
        V((FD, TF, D), BF), V((T, D), BF), V(segment_ids.shape, jnp.int32), V((2, FD, C, D), BF),
        V((T, D), BF), V((T, D), BF), V((FD, TF + 2 * C, 2 * D), BF), V((FD, 2 * R, 3 * C, WIDE), BF),
        V((T, D), BF), V((T, D), F32), V((T, D), BF), V((T, D), F32),
        V((T, ff), BF), V((T, ff), BF), V((FD, TF, D), BF),
        V((max(4 * FD * C, T), 2 * WIDE), F32),
        V((2, FD * C, D), BF), V((2, FD, C, D), BF),
        V((2, 2 * FD, WIDE), F32), V((2, 2 * FD, WIDE), F32), V((2, 2 * FD, WIDE), F32), V((2, 2 * FD, WIDE), F32),
        V((WIDE, WIDE), BF), V((FD, C, WIDE), F32),
        V((8, D), F32), V((Z, 8, D), F32), V((L, 8, D), F32), V((2, 8, D), F32),
    ]
    scratch += [V((n, 128), BF) for n in pn.sizes]
    scratch += [V((n, 128), BF) for n in pn.landing]
    scratch += [V((n, 128), BF) for n in pn.sizes]
    scratch += [
        dma((7,)), dma((2 + pn.n_subs,)), dma((2, 2)), dma((2, 2)), dma((2, 2)), dma((2, 2)), dma((8,)), dma((8,)),
        dma((pn.n_subs, 8)), dma((pn.n_subs, 8)), dma((3,)), dma((3,)),
    ]
    shape = jax.ShapeDtypeStruct
    outs = pl.pallas_call(
        functools.partial(body, pn),
        out_shape=[shape((T, D), BF), shape((T, D), F32), shape((8, D), F32)]
        + [shape((n, 128), BF) for n in pn.sizes],
        in_specs=[anywhere, anywhere, vmem, vmem, anywhere, anywhere, vmem, vmem, anywhere, anywhere, anywhere],
        out_specs=[anywhere] * (3 + np_),
        scratch_shapes=scratch,
        compiler_params=pltpu.CompilerParams(
            collective_id=0, has_side_effects=True, vmem_limit_bytes=62 * 2**20
        ),
        name="block",
    )(
        patches.reshape(FD, TF, D), segment_ids, gain_attn, bias_attn, w_qkv, w_proj, gain_mlp, bias_mlp,
        w_hidden, w_output, cotangent.reshape(T, D),
    )
    layer, patch, vec = outs[:3]
    ags = outs[3:]
    wides = [(D, D + CHUNK)] * pn.chunks + [(D, D)] + [(D, 3 * WIDE)] * 2
    final = pl.pallas_call(
        functools.partial(widen, pn),
        out_shape=[
            shape((T, D), BF), shape((T, D), F32), shape((D,), F32), shape((D,), F32), shape((D, 3 * D), F32),
            shape((D, D), F32), shape((D,), F32), shape((D,), F32), shape((D, ff), F32), shape((ff, D), F32),
        ],
        in_specs=[anywhere] * np_ + [vmem, anywhere, anywhere],
        out_specs=[anywhere, anywhere, vmem, vmem, anywhere, anywhere, vmem, vmem, anywhere, anywhere],
        scratch_shapes=[V((n, 128), BF) for n in pn.sizes]
        + [V(s, F32) for s in wides]
        + [V((T, D), BF), V((T, D), F32), dma((np_,)), dma((2 * pn.chunks + 7,)), dma((4,))],
        compiler_params=pltpu.CompilerParams(vmem_limit_bytes=62 * 2**20),
        name="widen",
    )(*ags, vec, layer, patch)
    block = (FD, R, C, D)
    return (final[0].reshape(block), final[1].reshape(block)) + tuple(final[2:])


def solution(mesh):
    band = P("fld", "lat", None, None)
    return jax.shard_map(
        functools.partial(per_device, mesh),
        mesh=mesh,
        in_specs=(band, P("fld", None, None)) + (P(),) * 8 + (band,),
        out_specs=(band, band) + (P(),) * 8,
        check_vma=False,
    )
```

```python
import functools
import math

import jax
import jax.numpy as jnp
from jax import lax
from jax.experimental import pallas as pl
from jax.experimental.pallas import tpu as pltpu
from jax.sharding import PartitionSpec as P

HEAD_DIM = 32
GROUP = 8
WIDE = GROUP * HEAD_DIM
SCALE = HEAD_DIM ** -0.5
LOG2E = math.log2(math.e)
EPS = 1e-6
REACH = 4
NEG = -1e30
CHUNK = 512
BLOCK = 256
FIELDS_AT_ONCE = 2
DIRECT = (5, 6)
Z_FIRST = ()
SCHEDULE = {
    "J2": (0, 1),
    "J4": (0, 2, 3, 1),
    "J6": (2, 3, 4, 5),
    "J8": (4, 6, 7, 5),
    "E0": (0, 1),
    "E1": (6, 7),
    "E2": (2, 3),
    "P1": (4, 5, 8, 9),
    "A1": (8,),
    "A2": (9, 0),
    "A3": (1,),
    "B1": (7,),
    "B2": (0, 6),
    "B3": (2, 1),
    "D0": (4,),
    "D1": (3, 9),
    "D2": (0,),
    "D3": (6,),
    "X": (2,),
    "X1": (1, 5, 4, 0, 8),
    "X2": (3, 7),
    "C0": (9, 6, 10),
    "X3": (8, 1, 2),
    "X4": (10, 5),
    "C1": (0, 4, 12),
    "F1": (3, 0),
    "F2": (1, 7, 12),
    "F3": (9, 2),
    "V0": (14,),
    "T": (6, 1, 8, 3, 5, 10, 7, 9, 4, 8, 14, 12, 10, 2, 6, 5, 7, 2, 9, 3, 12, 8, 3, 4, 10, 14, 5, 12, 14, 4, 6, 7, 8, 9, 5, 10, 6, 7, 8, 9, 10, 12, 12),
}
BF = jnp.bfloat16
F32 = jnp.float32
MESH = pl.DeviceIdType.MESH

NT = (((1,), (1,)), ((), ()))
TN = (((0,), (0,)), ((), ()))


def dot(a, b, dims=None):
    if dims is None:
        return jnp.dot(a, b, preferred_element_type=F32)
    return lax.dot_general(a, b, dims, preferred_element_type=F32)


def normalize(x):
    center = jnp.mean(x, axis=-1, keepdims=True)
    off = x - center
    rstd = lax.rsqrt(jnp.mean(off * off, axis=-1, keepdims=True) + EPS)
    return off * rstd, rstd


def norm_pull(e, gain, n, rstd):
    ge = e * gain
    a = jnp.mean(ge, axis=-1, keepdims=True)
    b = jnp.mean(ge * n, axis=-1, keepdims=True)
    return (ge - a - n * b) * rstd


def gelu_both(u):
    cdf = 0.5 + 0.5 * lax.erf(u * (1.0 / math.sqrt(2.0)))
    density = jnp.exp2((u * u) * (-0.5 * LOG2E)) * (1.0 / math.sqrt(2.0 * math.pi))
    return u * cdf, cdf + u * density


def row_sums(x):
    return jnp.sum(x, axis=0, keepdims=True)


class Plan:
    def __init__(self, mesh, fields, rows, cols, width, ff):
        self.lats = mesh.shape["lat"]
        self.flds = mesh.shape["fld"]
        self.zs = self.flds // 2
        self.fields, self.rows, self.cols = fields, rows, cols
        self.tf = rows * cols
        self.tokens = fields * self.tf
        self.width, self.ff = width, ff
        self.chunks = ff // CHUNK
        self.size_of = {"core": 2, "x": 2, "y": self.lats // 2, "lat": self.lats, "z": self.zs}
        unit = 16 * self.lats * self.flds
        blocks = width // 128
        mlp = CHUNK * blocks + width * (CHUNK // 128)
        rows_needed = [mlp] * self.chunks + [width * blocks] + [width * (3 * WIDE // 128)] * 2
        self.sizes, self.subs = [], []
        for p, n in enumerate(rows_needed):
            n = -(-n // unit) * unit
            self.sizes.append(n)
            if p in Z_FIRST:
                self.subs.append([(0, n, ("core", "z", "lat"))])
            elif p in DIRECT or n % (2 * unit):
                self.subs.append([(0, n, ("core", "lat", "z"))])
            else:
                self.subs.append([(0, n // 2, ("core", "x", "y", "z")), (n // 2, n // 2, ("core", "y", "x", "z"))])
        self.landing = []
        for subs in self.subs:
            total = 0
            for _, n, order in subs:
                for d in order:
                    n //= self.size_of[d]
                    total += n * (self.size_of[d] - 1)
            self.landing.append(total)
        self.n_subs = sum(len(s) for s in self.subs)


def body(plan, *refs):
    pn = plan
    np_ = len(pn.sizes)
    (patches, seg, gain_a, bias_a, w_qkv, w_proj, gain_m, bias_m, w_hid, w_out, cot) = refs[:11]
    out_layer, out_patch, out_vec = refs[11:14]
    out_ag = refs[14 : 14 + np_]
    sc = list(refs[14 + np_ :])

    def take(n):
        got = sc[:n]
        del sc[:n]
        return got

    wq, wp, wh, wo = take(4)
    pb, cb, segv, halo = take(4)
    normed, qb, kv, pt, ctx, res, nm, gres, act, gpre, gctx, edge = take(12)
    hq, hg, lse, hlse, dst, hdst = take(6)
    bm, biasb, vec, vrz, vrx, vrc = take(6)
    sb, rb, ag = take(np_), take(np_), take(np_)
    in_sem, out_sem, halo_s, halo_r, rim_s, rim_r, back_s, back_r, rs_s, rs_r, v_s, v_r = take(12)

    lat = lax.axis_index("lat")
    fld = lax.axis_index("fld")
    core = lax.rem(fld, 2)
    z = lax.div(fld, 2)
    x = lax.rem(lat, 2)
    y = lax.div(lat, 2)
    L, Z, Y = pn.lats, pn.zs, pn.lats // 2
    FD, R, C, TF, T, D, FF = pn.fields, pn.rows, pn.cols, pn.tf, pn.tokens, pn.width, pn.ff

    ins = [(patches, pb), (w_qkv, wq), (seg, segv), (cot, cb), (w_out, wo), (w_proj, wp), (w_hid, wh)]
    loads = [pltpu.make_async_copy(s, d, in_sem.at[i]) for i, (s, d) in enumerate(ins)]
    loads[0].start()
    loads[1].start()

    me = {"core": core, "x": x, "y": y, "lat": lat, "z": z}

    def device(d, i):
        if d == "core":
            return lat, z * 2 + i
        if d == "x":
            return y * 2 + i, fld
        if d == "y":
            return i * 2 + x, fld
        if d == "lat":
            return i, fld
        return lat, i * 2 + core

    def peers(d):
        n = pn.size_of[d]
        places = [lax.rem(me[d] + k, n) for k in range(1, n)]
        return [(i, device(d, i)) for i in places]

    barrier = pltpu.get_barrier_semaphore()
    everyone = peers("core") + peers("lat") + peers("z")
    for _, dev in everyone:
        pl.semaphore_signal(barrier, inc=1, device_id=dev, device_id_type=MESH)
    pl.semaphore_wait(barrier, len(everyone))

    up, down = (lat - 1, fld), (lat + 1, fld)
    has_up, has_down = lat > 0, lat < L - 1

    def remote(src, dst, s, r, dev):
        return pltpu.make_async_remote_copy(
            src_ref=src, dst_ref=dst, send_sem=s, recv_sem=r, device_id=dev, device_id_type=MESH
        )

    def arrived(ref, sem):
        pltpu.make_async_copy(ref, ref, sem).wait()

    half = FD // 2
    halo_copies = []
    for h in range(2):
        some = pl.ds(h * half, half)
        to_up = remote(patches.at[some, pl.ds(0, C)], halo.at[1, some], halo_s.at[0, h], halo_r.at[1, h], up)
        to_dn = remote(patches.at[some, pl.ds(TF - C, C)], halo.at[0, some], halo_s.at[1, h], halo_r.at[0, h], down)
        pl.when(has_up)(to_up.start)
        pl.when(has_down)(to_dn.start)
        halo_copies.append((to_up, to_dn))
    for c in loads[2:]:
        c.start()

    def spot(off, n):
        return pl.ds(pl.multiple_of(off, 16), n)

    class Part:
        def __init__(self, p, number, start, n, order, land):
            self.p, self.number, self.order = p, number, order
            self.off, self.len, self.land = [start], [n], []
            for d in order:
                g = pn.size_of[d]
                n = n // g
                self.land.append(land)
                land += n * (g - 1)
                self.off.append(self.off[-1] + me[d] * n)
                self.len.append(n)
            self.end = land

        def moved(self, i):
            return self.len[i + 1] * (pn.size_of[self.order[i]] - 1)

        def scatter(self, i):
            n = self.len[i + 1]
            for k, (j, dev) in enumerate(peers(self.order[i])):
                src = sb[self.p].at[spot(self.off[i] + j * n, n)]
                dst = rb[self.p].at[pl.ds(self.land[i] + k * n, n)]
                remote(src, dst, rs_s.at[self.number, i], rs_r.at[self.number, i], dev).start()

        def add(self, i):
            n = self.len[i + 1]
            d = self.order[i]
            arrived(rb[self.p].at[pl.ds(self.land[i], self.moved(i))], rs_r.at[self.number, i])
            mine = spot(self.off[i + 1], n)
            total = sb[self.p][mine, :].astype(F32)
            for k in range(pn.size_of[d] - 1):
                total = total + rb[self.p][self.land[i] + k * n : self.land[i] + (k + 1) * n, :].astype(F32)
            to = ag if i == len(self.order) - 1 else sb
            to[self.p][mine, :] = total.astype(BF)

        def gather(self, i):
            s = 4 + i
            mine = ag[self.p].at[spot(self.off[i + 1], self.len[i + 1])]
            for _, dev in peers(self.order[i]):
                remote(mine, mine, rs_s.at[self.number, s], rs_r.at[self.number, s], dev).start()

        def gathered(self, i):
            arrived(ag[self.p].at[pl.ds(0, self.moved(i))], rs_r.at[self.number, 4 + i])

        def step(self, s):
            nd = len(self.order)
            if s < nd:
                if s > 0:
                    self.add(s - 1)
                self.scatter(s)
            elif s == nd:
                self.add(nd - 1)
                self.gather(nd - 1)
            else:
                self.gathered(2 * nd - s)
                if s < 2 * nd:
                    self.gather(2 * nd - 1 - s)

        def finish(self):
            for i in range(len(self.order)):
                for s in (i, 4 + i):
                    arrived(sb[self.p].at[pl.ds(0, self.moved(i))], rs_s.at[self.number, s])

    parts, number = [], 0
    for p in range(np_):
        mine, land = [], 0
        for start, n, order in pn.subs[p]:
            mine.append(Part(p, number, start, n, order, land))
            land = mine[-1].end
            number += 1
        parts.append(mine)
    every = [part for mine in parts for part in mine]
    vec_at = len(every)
    reached = [0] * (vec_at + 1)
    last_step = [2 * len(part.order) for part in every] + [3]

    def out_copy(part):
        rows = pl.ds(part.off[0], part.len[0])
        return pltpu.make_async_copy(ag[part.p].at[rows], out_ag[part.p].at[rows], out_sem.at[2 + part.number])

    codes = [2 * p + i for p, mine in enumerate(parts) for i in range(len(mine))] + [2 * np_]
    number_of = {code: k for k, code in enumerate(codes)}

    def hook(*some):
        steps = []
        for code in some:
            k = number_of.get(code, vec_at + 1)
            if k <= vec_at and reached[k] <= last_step[k]:
                steps.append((k, reached[k]))
                reached[k] += 1

        def run():
            for k, s in steps:
                if k == vec_at:
                    vec_step(s)
                    continue
                every[k].step(s)
                if s == last_step[k]:
                    out_copy(every[k]).start()

        return run

    def place(name):
        return hook(*SCHEDULE.get(name, ()))

    rounds = ((vrz, "z"), (vrx, "lat"), (vrc, "core"))

    def vec_step(s):
        if s > 0:
            buf, d = rounds[s - 1]
            count = pn.size_of[d]
            arrived(buf.at[pl.ds(0, count - 1)], v_r.at[s - 1])
            arrived(buf.at[pl.ds(0, count - 1)], v_s.at[s - 1])
            total = buf[0]
            for k in range(1, count):
                total = total + buf[k]
            vec[...] = total
        if s < 3:
            buf, d = rounds[s]
            buf[me[d]] = vec[...]
            for _, dev in peers(d):
                remote(vec, buf.at[me[d]], v_s.at[s], v_r.at[s], dev).start()
        else:
            pltpu.make_async_copy(vec, out_vec, in_sem.at[0]).start()

    def finish(part):
        part.finish()
        out_copy(part).wait()

    def put(p, start, stride, value):
        rows, lanes = value.shape
        low = value.astype(BF)
        for j in range(lanes // 128):
            at = start + j * stride
            sb[p][at : at + rows, :] = low[:, j * 128 : (j + 1) * 128]

    rid = lax.broadcasted_iota(jnp.int32, (WIDE, WIDE), 0) // HEAD_DIM
    cid = lax.broadcasted_iota(jnp.int32, (WIDE, WIDE), 1) // HEAD_DIM
    same = jnp.where(rid == cid, 1.0, 0.0)
    bm[...] = same.astype(BF)

    ga, ba = gain_a[...].reshape(1, D), bias_a[...].reshape(1, D)
    gm, bmlp = gain_m[...].reshape(1, D), bias_m[...].reshape(1, D)
    loads[0].wait()

    per = max(1, 256 // TF)
    tile = per * TF
    tiles = T // tile

    def rows_at(t):
        return slice(t * tile, (t + 1) * tile)

    def fields_at(t):
        return slice(t * per, (t + 1) * per)

    def norm_one(t):
        n, _ = normalize(pb[fields_at(t)].reshape(tile, D).astype(F32))
        normed[rows_at(t), :] = (n * ga + ba).astype(BF)

    norm_one(0)
    loads[1].wait()
    for t in range(tiles):
        if t + 1 < tiles:
            norm_one(t + 1)
        qb[rows_at(t), :] = dot(normed[rows_at(t), :], wq[:, :D]).astype(BF)
        part = dot(normed[rows_at(t), :], wq[:, D:]).astype(BF)
        kv[fields_at(t), C : C + TF, :] = part.reshape(per, TF, 2 * D)

    loads[2].wait()
    kcol = lax.broadcasted_iota(jnp.int32, (C, WIDE), 0)
    qcol = lax.rem(lax.broadcasted_iota(jnp.int32, (C, WIDE), 1), C)
    away = jnp.abs(kcol - qcol)
    near = jnp.minimum(away, C - away) <= REACH
    diag = lax.broadcasted_iota(jnp.int32, (C, C), 0) == lax.broadcasted_iota(jnp.int32, (C, C), 1)
    for f in range(FD):
        line = segv[f, 0:1, :].astype(F32)
        across = jnp.concatenate([line] * GROUP, axis=1)
        along = jnp.sum(jnp.where(diag, line, 0.0), axis=1, keepdims=True)
        biasb[f] = jnp.where(jnp.logical_and(near, along == across), 0.0, NEG)
    pole_top = jnp.where(has_up, 0.0, NEG)
    pole_bottom = jnp.where(has_down, 0.0, NEG)

    lane_head = lax.broadcasted_iota(jnp.int32, (HEAD_DIM, WIDE), 1) // HEAD_DIM

    def diagonal(o):
        total = o[0:HEAD_DIM]
        for h in range(1, GROUP):
            total = jnp.where(lane_head == h, o[h * HEAD_DIM : (h + 1) * HEAD_DIM], total)
        return total

    def widened(q):
        return jnp.concatenate([q] * GROUP, axis=0) * bm[...]

    fpi = min(FIELDS_AT_ONCE, FD)

    def span(f, row):
        return pl.ds(pl.multiple_of(f * TF + row * C, C), C)

    k_lanes = [slice(g * WIDE, (g + 1) * WIDE) for g in range(2)]
    v_lanes = [slice(D + g * WIDE, D + (g + 1) * WIDE) for g in range(2)]

    def attend(rows, i, carry):
        units = [(i * fpi + j, g, r) for j in range(fpi) for g in range(2) for r in rows]
        scores = []
        for f, g, r in units:
            k = kv[f, r * C : (r + 3) * C, k_lanes[g]]
            scores.append(dot(k, widened(qb[span(f, r), k_lanes[g]]), NT))
        low, logs = [], []
        for (f, g, r), s in zip(units, scores):
            bias = biasb[f]
            first = bias + pole_top if r == 0 else bias
            third = bias + pole_bottom if r == R - 1 else bias
            s = s + jnp.concatenate([first, bias, third], axis=0)
            m = jnp.max(s, axis=0, keepdims=True)
            p = jnp.exp2((s - m) * (SCALE * LOG2E))
            total = row_sums(p)
            logs.append(m * (SCALE * LOG2E) + jnp.log2(total) if r in (0, R - 1) else None)
            low.append((p * (1.0 / total)).astype(BF))
        outs = []
        for (f, g, r), p in zip(units, low):
            v = kv[f, r * C : (r + 3) * C, v_lanes[g]]
            outs.append(diagonal(dot(p, v, TN)).astype(BF))
        for (f, g, r), p, log, o in zip(units, low, logs, outs):
            pt[f, g * R + r] = p
            ctx[span(f, r), k_lanes[g]] = o
            if r in (0, R - 1):
                lse[0 if r == 0 else 1, pl.ds(f * 2 + g, 1), :] = log
        return carry

    if R > 2:
        lax.fori_loop(0, FD // fpi, functools.partial(attend, range(1, R - 1)), 0)

    loads[3].wait()
    loads[4].wait()
    for j in range(FF // BLOCK):
        some = slice(j * BLOCK, (j + 1) * BLOCK)
        gpre[:, some] = dot(cb[...], wo[some, :], NT).astype(BF)

    for h in range(2):
        some = slice(h * half, (h + 1) * half)
        flat = slice(h * half * C, (h + 1) * half * C)
        for side, ok, copy in ((0, has_up, halo_copies[h][1]), (1, has_down, halo_copies[h][0])):
            pl.when(ok)(copy.wait_recv)

            @pl.when(jnp.logical_not(ok))
            def _():
                halo[side, some] = jnp.zeros((half, C, D), BF)

            n, _unused = normalize(halo[side, some].reshape(half * C, D).astype(F32))
            low = (n * ga + ba).astype(BF)
            hq[side, flat, :] = dot(low, wq[:, :D]).astype(BF)
            start = 0 if side == 0 else TF + C
            kv[some, start : start + C, :] = dot(low, wq[:, D:]).astype(BF).reshape(half, C, 2 * D)
        turns = half // fpi
        lax.fori_loop(h * turns, (h + 1) * turns, functools.partial(attend, (0, R - 1)), 0)

    loads[5].wait()
    for t in range(tiles):
        r = pb[fields_at(t)].reshape(tile, D).astype(F32) + dot(ctx[rows_at(t), :], wp[...])
        res[rows_at(t), :] = r
        n, _ = normalize(r)
        nm[rows_at(t), :] = (n * gm + bmlp).astype(BF)

    loads[6].wait()
    blocks = FF // BLOCK
    in_chunk = CHUNK // BLOCK

    def hidden_block(j):
        return slice(j * BLOCK, (j + 1) * BLOCK)

    def kept(ref, j):
        return ref.at[pl.ds(0, T), pl.ds((j % 2) * BLOCK, BLOCK)]

    def mlp_in(j):
        kept(gres, j)[...] = dot(nm[...], wh[:, hidden_block(j)])

    def mlp_mid(j):
        a, da = gelu_both(kept(gres, j)[...])
        act[:, hidden_block(j)] = a.astype(BF)
        gpre[:, hidden_block(j)] = (da * gpre[:, hidden_block(j)].astype(F32)).astype(BF)

    def mlp_out(j):
        c, part = j // in_chunk, j % in_chunk
        put(c, part * BLOCK, CHUNK, dot(act[:, hidden_block(j)], cb[...], TN))
        start = CHUNK * (D // 128) + part * (BLOCK // 128) * D
        put(c, start, D, dot(nm[...], gpre[:, hidden_block(j)], TN))

    mlp_in(0)
    for j in range(blocks):
        if j + 1 < blocks:
            mlp_in(j + 1)
        mlp_mid(j)
        if j > 0:
            mlp_out(j - 1)
        place(f"J{j}")()
    mlp_out(blocks - 1)
    place(f"J{blocks}")()

    zero = jnp.zeros((1, D), F32)

    mlp_gain, mlp_bias = zero, zero

    l_up = remote(lse.at[0], hlse.at[1], back_s.at[2], back_r.at[3], up)
    l_dn = remote(lse.at[1], hlse.at[0], back_s.at[3], back_r.at[2], down)
    pl.when(has_up)(l_up.start)
    pl.when(has_down)(l_dn.start)

    head_rows = lax.broadcasted_iota(jnp.int32, (2 * GROUP, D), 0) == lax.broadcasted_iota(
        jnp.int32, (2 * GROUP, D), 1
    ) // HEAD_DIM
    head_rows = jnp.where(head_rows, 1.0, 0.0).astype(BF)
    own_head = lax.broadcasted_iota(jnp.int32, (GROUP, WIDE), 0) == lax.broadcasted_iota(
        jnp.int32, (GROUP, WIDE), 1
    ) // HEAD_DIM

    def rim_totals(some):
        spots = [(f, side) for f in range(some.start, some.stop) for side in range(2)]
        terms = []
        for f, side in spots:
            row = 0 if side == 0 else R - 1
            mine = ctx[f * TF + row * C : f * TF + (row + 1) * C, :].astype(F32)
            terms.append(mine * gctx[f, row * C : (row + 1) * C, :].astype(F32))
        terms = jnp.concatenate(terms, axis=0)
        high = terms.astype(BF)
        rest = (terms - high.astype(F32)).astype(BF)
        sums = dot(head_rows, high, NT) + dot(head_rows, rest, NT)
        for i, (f, side) in enumerate(spots):
            across = jnp.concatenate([sums[:, i * C : (i + 1) * C]] * GROUP, axis=1)
            for g in range(2):
                own = jnp.where(own_head, across[g * GROUP : (g + 1) * GROUP], 0.0)
                dst[side, 2 * f + g : 2 * f + g + 1, :] = row_sums(own)

    def send_rims(some):
        some = pl.ds(some.start, some.stop - some.start)
        h = some.start // half
        to_up = remote(gctx.at[some, pl.ds(0, C)], hg.at[1, some], rim_s.at[0, h], rim_r.at[1, h], up)
        to_dn = remote(gctx.at[some, pl.ds(TF - C, C)], hg.at[0, some], rim_s.at[1, h], rim_r.at[0, h], down)
        pl.when(has_up)(to_up.start)
        pl.when(has_down)(to_dn.start)

    grad_in = dot(gpre[rows_at(0), :], wh[...], NT)
    for t in range(tiles):
        e = grad_in
        if t + 1 < tiles:
            grad_in = dot(gpre[rows_at(t + 1), :], wh[...], NT)
        n, rstd = normalize(res[rows_at(t), :])
        gr = cb[rows_at(t), :].astype(F32) + norm_pull(e, gm, n, rstd)
        gres[rows_at(t), :] = gr
        low = gr.astype(BF)
        nm[rows_at(t), :] = low
        gctx[fields_at(t)] = dot(low, wp[...], NT).astype(BF).reshape(per, TF, D)
        mlp_gain, mlp_bias = mlp_gain + row_sums(e * n), mlp_bias + row_sums(e)
        rim_totals(fields_at(t))
        send_rims(fields_at(t))
        place(f"E{t}")()

    d_up = remote(dst.at[0], hdst.at[1], back_s.at[4], back_r.at[5], up)
    d_dn = remote(dst.at[1], hdst.at[0], back_s.at[5], back_r.at[4], down)
    pl.when(has_up)(d_up.start)
    pl.when(has_down)(d_dn.start)
    pj = pn.chunks
    place("P")()
    put(pj, 0, D, dot(ctx[...], nm[...], TN))
    place("P1")()

    grad_joined = gpre

    def joined(g, j):
        return slice((3 * g + j) * WIDE, (3 * g + j + 1) * WIDE)

    def edge_rows(g, side, f):
        return pl.ds(pl.multiple_of(((g * 2 + side) * FD + f) * C, C), C)

    def back_group(g, hooks):
        def back_fields(i, carry):
            for when, do in hooks.items():
                pl.when(i == when)(do)
            units = [(i * fpi + j, r) for j in range(fpi) for r in range(R)]
            have = []
            for f, r in units:
                win = slice(r * C, (r + 3) * C)
                qd = widened(qb[span(f, r), k_lanes[g]])
                dod = widened(gctx[f, r * C : (r + 1) * C, k_lanes[g]])
                have.append((qd, dod, kv[f, win, k_lanes[g]], kv[f, win, v_lanes[g]], pt[f, g * R + r]))
            dps = [dot(v, dod, NT) for qd, dod, k, v, p in have]
            dss = []
            for (qd, dod, k, v, p), dp in zip(have, dps):
                wide = p.astype(F32)
                pd = wide * dp
                total = row_sums(pd)
                dss.append(((pd - wide * total) * SCALE).astype(BF))
            dqs = [diagonal(dot(ds, one[2], TN)).astype(BF) for ds, one in zip(dss, have)]
            dks, dvs = [], []
            for (f, r), ds, (qd, dod, k, v, p) in zip(units, dss, have):
                own = slice(C if r == 0 else 0, 2 * C if r == R - 1 else 3 * C)
                first = r + 1 if r == 0 else r
                dks.append((first, dot(ds[own], qd)))
                dvs.append((first, dot(p[own], dod)))
            for (f, r), o in zip(units, dqs):
                grad_joined[span(f, r), joined(g, 0)] = o
            for j in range(fpi):
                f = i * fpi + j
                for what, terms in enumerate((dks, dvs)):
                    for row in range(1, R + 1):
                        total = None
                        for first, term in terms[j * R : (j + 1) * R]:
                            if first <= row < first + term.shape[0] // C:
                                piece = term[(row - first) * C : (row - first + 1) * C]
                                total = piece if total is None else total + piece
                        if row in (1, R):
                            edge[edge_rows(g, 0 if row == 1 else 1, f), what * WIDE : (what + 1) * WIDE] = total
                        else:
                            grad_joined[span(f, row - 1), joined(g, what + 1)] = total.astype(BF)
            return carry

        lax.fori_loop(0, FD // fpi, back_fields, 0)
    def rim_part(h):
        return pl.ds(h * half, half)

    def back_edges(g, sent):
        for to_up, to_dn in sent:
            pl.when(has_up)(to_dn.wait_recv)
            pl.when(has_down)(to_up.wait_recv)

        def back_rims(h):
            units = [(h * half + j, side) for j in range(half) for side in range(2)]
            oks, rows = (has_up, has_down), (0, R - 1)
            have = []
            for f, side in units:
                qd = widened(hq[side, f * C : (f + 1) * C, k_lanes[g]])
                dod = widened(hg[side, f, :, k_lanes[g]])
                keys = slice((rows[side] + 1) * C, (rows[side] + 2) * C)
                have.append((qd, dod, kv[f, keys, k_lanes[g]], kv[f, keys, v_lanes[g]]))
            scores = [dot(k, qd, NT) for qd, dod, k, v in have]
            dps = [dot(v, dod, NT) for qd, dod, k, v in have]
            ps, dss = [], []
            for (f, side), s, dp in zip(units, scores, dps):
                s = (s + biasb[f]) * (SCALE * LOG2E) - hlse[side, pl.ds(f * 2 + g, 1), :]
                p = jnp.where(oks[side], jnp.exp2(s), 0.0)
                ds = p * (dp - hdst[side, pl.ds(f * 2 + g, 1), :]) * SCALE
                ps.append(p.astype(BF))
                dss.append(jnp.where(oks[side], ds, 0.0).astype(BF))
            dks = [dot(ds, one[0]) for ds, one in zip(dss, have)]
            dvs = [dot(p, one[1]) for p, one in zip(ps, have)]
            held = [edge[edge_rows(g, side, f), :] for f, side in units]
            for (f, side), dk, dv, own in zip(units, dks, dvs, held):
                dk = own[:, :WIDE] + jnp.where(oks[side], dk, 0.0)
                dv = own[:, WIDE:] + jnp.where(oks[side], dv, 0.0)
                grad_joined[span(f, rows[side]), joined(g, 1)] = dk.astype(BF)
                grad_joined[span(f, rows[side]), joined(g, 2)] = dv.astype(BF)

        for h in range(2):
            if g == 0:
                pl.when(has_up)(lambda: arrived(hg.at[0, rim_part(h)], rim_r.at[0, h]))
                pl.when(has_down)(lambda: arrived(hg.at[1, rim_part(h)], rim_r.at[1, h]))
            back_rims(h)
            place(f"X{2 * g + h + 1}")()
        put(pj + 1 + g, 0, D, dot(normed[...], grad_joined[:, 3 * g * WIDE : 3 * (g + 1) * WIDE], TN))
        place(f"C{g}")()

    back_group(0, {i: place(f"A{i}") for i in range(4)})
    back_group(1, {i: place(f"B{i}") for i in range(4)})
    for t in range(tiles):
        nm[rows_at(t), :] = (res[rows_at(t), :] + dot(act[rows_at(t), :], wo[...])).astype(BF)
        place(f"D{t}")()
    layer_copy = pltpu.make_async_copy(nm, out_layer, out_sem.at[0])
    layer_copy.start()

    place("X")()
    back_edges(0, ((l_up, l_dn), (d_up, d_dn)))
    back_edges(1, ())

    attn_gain, attn_bias = zero, zero

    def grad_of(t):
        e = None
        for g in range(2):
            for j in range(3):
                w = wq[:, j * D + g * WIDE : j * D + (g + 1) * WIDE]
                term = dot(grad_joined[rows_at(t), joined(g, j)], w, NT)
                e = term if e is None else e + term
        return e

    grad_in = grad_of(0)
    for t in range(tiles):
        e = grad_in
        if t + 1 < tiles:
            grad_in = grad_of(t + 1)
        n, rstd = normalize(pb[fields_at(t)].reshape(tile, D).astype(F32))
        gres[rows_at(t), :] += norm_pull(e, ga, n, rstd)
        attn_gain, attn_bias = attn_gain + row_sums(e * n), attn_bias + row_sums(e)
        place(f"F{t}")()

    patch_copy = pltpu.make_async_copy(gres, out_patch, out_sem.at[1])
    patch_copy.start()
    vec[...] = jnp.concatenate([attn_gain, attn_bias, mlp_gain, mlp_bias, zero, zero, zero, zero], axis=0)
    place("V0")()

    place("T")()
    while any(a <= b for a, b in zip(reached, last_step)):
        for k in sorted(range(vec_at + 1), key=lambda k: reached[k] - last_step[k], reverse=True):
            hook(codes[k])()

    for to_up, to_dn in halo_copies:
        pl.when(has_up)(to_up.wait_send)
        pl.when(has_down)(to_dn.wait_send)
    for h in range(2):
        pl.when(has_up)(lambda: arrived(hg.at[1, rim_part(h)], rim_s.at[0, h]))
        pl.when(has_down)(lambda: arrived(hg.at[0, rim_part(h)], rim_s.at[1, h]))
    for to_up, to_dn in ((l_up, l_dn), (d_up, d_dn)):
        pl.when(has_up)(to_up.wait_send)
        pl.when(has_down)(to_dn.wait_send)
    layer_copy.wait()
    patch_copy.wait()
    pltpu.make_async_copy(vec, out_vec, in_sem.at[0]).wait()
    for part in every:
        finish(part)


def widen(plan, *refs):
    pn = plan
    np_ = len(pn.sizes)
    ag, vec, layer, patch = refs[:np_], refs[np_], refs[np_ + 1], refs[np_ + 2]
    o_layer, o_patch, o_ag, o_ab, o_qkv, o_proj, o_mg, o_mb, o_hid, o_out = refs[np_ + 3 : np_ + 13]
    sc = list(refs[np_ + 13 :])
    low, wide = sc[:np_], sc[np_ : 2 * np_]
    kept_layer, kept_patch, in_sem, out_sem, pass_sem = sc[2 * np_ :]
    D = pn.width
    loads = [pltpu.make_async_copy(ag[p], low[p], in_sem.at[p]) for p in range(np_)]
    for c in loads:
        c.start()
    through = [
        (pltpu.make_async_copy(a, b, pass_sem.at[2 * i]), pltpu.make_async_copy(b, c, pass_sem.at[2 * i + 1]))
        for i, (a, b, c) in enumerate(((layer, kept_layer, o_layer), (patch, kept_patch, o_patch)))
    ]
    for arrive, _ in through:
        arrive.start()
    for i, o in enumerate((o_ag, o_ab, o_mg, o_mb)):
        o[...] = vec[i : i + 1, :].reshape(D)
    stores = []

    def store(src, dst):
        c = pltpu.make_async_copy(src, dst, out_sem.at[len(stores)])
        c.start()
        stores.append(c)

    def spread(p, start, rows, blocks, col):
        for j in range(blocks):
            wide[p][:, col + j * 128 : col + (j + 1) * 128] = low[p][
                start + j * rows : start + (j + 1) * rows, :
            ].astype(F32)

    for p in range(np_):
        loads[p].wait()
        if p == np_ - 1:
            for arrive, leave in through:
                arrive.wait()
                leave.start()
        if p < pn.chunks:
            spread(p, 0, CHUNK, D // 128, 0)
            store(wide[p].at[:, pl.ds(0, D)], o_out.at[pl.ds(p * CHUNK, CHUNK)])
            spread(p, CHUNK * (D // 128), D, CHUNK // 128, D)
            store(wide[p].at[:, pl.ds(D, CHUNK)], o_hid.at[:, pl.ds(p * CHUNK, CHUNK)])
        elif p == pn.chunks:
            spread(p, 0, D, D // 128, 0)
            store(wide[p], o_proj)
        else:
            g = p - pn.chunks - 1
            spread(p, 0, D, 3 * WIDE // 128, 0)
            for j in range(3):
                store(
                    wide[p].at[:, pl.ds(j * WIDE, WIDE)],
                    o_qkv.at[:, pl.ds(j * D + g * WIDE, WIDE)],
                )
    for c in stores + [leave for _, leave in through]:
        c.wait()


def per_device(mesh, patches, segment_ids, gain_attn, bias_attn, w_qkv, w_proj, gain_mlp, bias_mlp, w_hidden, w_output, cotangent):
    fields, rows, cols, width = patches.shape
    ff = w_hidden.shape[1]
    pn = Plan(mesh, fields, rows, cols, width, ff)
    np_ = len(pn.sizes)
    T, TF, D, C, R, FD = pn.tokens, pn.tf, width, cols, rows, fields
    L, Z = pn.lats, pn.zs
    anywhere = pl.BlockSpec(memory_space=pl.ANY)
    vmem = pl.BlockSpec(memory_space=pltpu.VMEM)
    V = pltpu.VMEM
    dma = pltpu.SemaphoreType.DMA
    scratch = [
        V((D, 3 * D), BF), V((D, D), BF), V((D, ff), BF), V((ff, D), BF),
        V((FD, TF, D), BF), V((T, D), BF), V(segment_ids.shape, jnp.int32), V((2, FD, C, D), BF),
        V((T, D), BF), V((T, D), BF), V((FD, TF + 2 * C, 2 * D), BF), V((FD, 2 * R, 3 * C, WIDE), BF),
        V((T, D), BF), V((T, D), F32), V((T, D), BF), V((T, D), F32),
        V((T, ff), BF), V((T, ff), BF), V((FD, TF, D), BF),
        V((max(4 * FD * C, T), 2 * WIDE), F32),
        V((2, FD * C, D), BF), V((2, FD, C, D), BF),
        V((2, 2 * FD, WIDE), F32), V((2, 2 * FD, WIDE), F32), V((2, 2 * FD, WIDE), F32), V((2, 2 * FD, WIDE), F32),
        V((WIDE, WIDE), BF), V((FD, C, WIDE), F32),
        V((8, D), F32), V((Z, 8, D), F32), V((L, 8, D), F32), V((2, 8, D), F32),
    ]
    scratch += [V((n, 128), BF) for n in pn.sizes]
    scratch += [V((n, 128), BF) for n in pn.landing]
    scratch += [V((n, 128), BF) for n in pn.sizes]
    scratch += [
        dma((7,)), dma((2 + pn.n_subs,)), dma((2, 2)), dma((2, 2)), dma((2, 2)), dma((2, 2)), dma((8,)), dma((8,)),
        dma((pn.n_subs, 8)), dma((pn.n_subs, 8)), dma((3,)), dma((3,)),
    ]
    shape = jax.ShapeDtypeStruct
    outs = pl.pallas_call(
        functools.partial(body, pn),
        out_shape=[shape((T, D), BF), shape((T, D), F32), shape((8, D), F32)]
        + [shape((n, 128), BF) for n in pn.sizes],
        in_specs=[anywhere, anywhere, vmem, vmem, anywhere, anywhere, vmem, vmem, anywhere, anywhere, anywhere],
        out_specs=[anywhere] * (3 + np_),
        scratch_shapes=scratch,
        compiler_params=pltpu.CompilerParams(
            collective_id=0, has_side_effects=True, vmem_limit_bytes=62 * 2**20
        ),
        name="block",
    )(
        patches.reshape(FD, TF, D), segment_ids, gain_attn, bias_attn, w_qkv, w_proj, gain_mlp, bias_mlp,
        w_hidden, w_output, cotangent.reshape(T, D),
    )
    layer, patch, vec = outs[:3]
    ags = outs[3:]
    wides = [(D, D + CHUNK)] * pn.chunks + [(D, D)] + [(D, 3 * WIDE)] * 2
    final = pl.pallas_call(
        functools.partial(widen, pn),
        out_shape=[
            shape((T, D), BF), shape((T, D), F32), shape((D,), F32), shape((D,), F32), shape((D, 3 * D), F32),
            shape((D, D), F32), shape((D,), F32), shape((D,), F32), shape((D, ff), F32), shape((ff, D), F32),
        ],
        in_specs=[anywhere] * np_ + [vmem, anywhere, anywhere],
        out_specs=[anywhere, anywhere, vmem, vmem, anywhere, anywhere, vmem, vmem, anywhere, anywhere],
        scratch_shapes=[V((n, 128), BF) for n in pn.sizes]
        + [V(s, F32) for s in wides]
        + [V((T, D), BF), V((T, D), F32), dma((np_,)), dma((2 * pn.chunks + 7,)), dma((4,))],
        compiler_params=pltpu.CompilerParams(vmem_limit_bytes=62 * 2**20),
        name="widen",
    )(*ags, vec, layer, patch)
    block = (FD, R, C, D)
    return (final[0].reshape(block), final[1].reshape(block)) + tuple(final[2:])


def solution(mesh):
    band = P("fld", "lat", None, None)
    return jax.shard_map(
        functools.partial(per_device, mesh),
        mesh=mesh,
        in_specs=(band, P("fld", None, None)) + (P(),) * 8 + (band,),
        out_specs=(band, band) + (P(),) * 8,
        check_vma=False,
    )
```

```python
import functools
import math

import jax
import jax.numpy as jnp
from jax import lax
from jax.experimental import pallas as pl
from jax.experimental.pallas import tpu as pltpu
from jax.sharding import PartitionSpec as P

HEAD_DIM = 32
GROUP = 8
WIDE = GROUP * HEAD_DIM
SCALE = HEAD_DIM ** -0.5
LOG2E = math.log2(math.e)
EPS = 1e-6
REACH = 4
NEG = -1e30
CHUNK = 512
BLOCK = 256
FIELDS_AT_ONCE = 2
DIRECT = ()
Z_FIRST = ()
SCHEDULE = {
    "J2": (0, 1),
    "J4": (0, 2, 3, 1),
    "J6": (2, 3, 4, 5),
    "J8": (4, 6, 7, 5),
    "E0": (0, 1),
    "E1": (6, 7),
    "E2": (2, 3),
    "P1": (4, 5, 8, 9),
    "A1": (8,),
    "A2": (9, 0),
    "A3": (1,),
    "B1": (7,),
    "B2": (0, 6),
    "B3": (2, 1),
    "D0": (4,),
    "D1": (3, 9),
    "D2": (0,),
    "D3": (6,),
    "X": (2,),
    "X1": (1, 5, 4, 0, 8),
    "X2": (3, 7),
    "C0": (9, 6, 10, 11),
    "X3": (8, 1, 2),
    "X4": (10, 11, 5),
    "C1": (0, 4, 12, 13),
    "F1": (3, 0),
    "F2": (12, 1, 7, 13),
    "F3": (10, 9, 2),
    "V0": (14,),
    "T": (6, 1, 8, 3, 11, 5, 12, 13, 4, 7, 9, 8, 10, 2, 11, 6, 14, 13, 2, 5, 12, 3, 10, 8, 11, 4, 13, 3, 7, 12, 9, 4, 5, 10, 13, 14, 6, 12, 11, 5, 13, 14, 12, 8, 7, 9, 6, 10, 11, 13, 13, 12, 8, 7, 9, 11, 12, 10, 11, 10),
}
BF = jnp.bfloat16
F32 = jnp.float32
MESH = pl.DeviceIdType.MESH

NT = (((1,), (1,)), ((), ()))
TN = (((0,), (0,)), ((), ()))


def dot(a, b, dims=None):
    if dims is None:
        return jnp.dot(a, b, preferred_element_type=F32)
    return lax.dot_general(a, b, dims, preferred_element_type=F32)


def normalize(x):
    center = jnp.mean(x, axis=-1, keepdims=True)
    off = x - center
    rstd = lax.rsqrt(jnp.mean(off * off, axis=-1, keepdims=True) + EPS)
    return off * rstd, rstd


def norm_pull(e, gain, n, rstd):
    ge = e * gain
    a = jnp.mean(ge, axis=-1, keepdims=True)
    b = jnp.mean(ge * n, axis=-1, keepdims=True)
    return (ge - a - n * b) * rstd


def gelu_both(u):
    cdf = 0.5 + 0.5 * lax.erf(u * (1.0 / math.sqrt(2.0)))
    density = jnp.exp2((u * u) * (-0.5 * LOG2E)) * (1.0 / math.sqrt(2.0 * math.pi))
    return u * cdf, cdf + u * density


def row_sums(x):
    return jnp.sum(x, axis=0, keepdims=True)


class Plan:
    def __init__(self, mesh, fields, rows, cols, width, ff):
        self.lats = mesh.shape["lat"]
        self.flds = mesh.shape["fld"]
        self.zs = self.flds // 2
        self.fields, self.rows, self.cols = fields, rows, cols
        self.tf = rows * cols
        self.tokens = fields * self.tf
        self.width, self.ff = width, ff
        self.chunks = ff // CHUNK
        self.size_of = {"core": 2, "x": 2, "y": self.lats // 2, "lat": self.lats, "z": self.zs}
        unit = 16 * self.lats * self.flds
        blocks = width // 128
        mlp = CHUNK * blocks + width * (CHUNK // 128)
        rows_needed = [mlp] * self.chunks + [width * blocks] + [width * (3 * WIDE // 128)] * 2
        self.sizes, self.subs = [], []
        for p, n in enumerate(rows_needed):
            n = -(-n // unit) * unit
            self.sizes.append(n)
            if p in Z_FIRST:
                self.subs.append([(0, n, ("core", "z", "lat"))])
            elif p in DIRECT or n % (2 * unit):
                self.subs.append([(0, n, ("core", "lat", "z"))])
            else:
                self.subs.append([(0, n // 2, ("core", "x", "y", "z")), (n // 2, n // 2, ("core", "y", "x", "z"))])
        self.landing = []
        for subs in self.subs:
            total = 0
            for _, n, order in subs:
                for d in order:
                    n //= self.size_of[d]
                    total += n * (self.size_of[d] - 1)
            self.landing.append(total)
        self.n_subs = sum(len(s) for s in self.subs)


def body(plan, *refs):
    pn = plan
    np_ = len(pn.sizes)
    (patches, seg, gain_a, bias_a, w_qkv, w_proj, gain_m, bias_m, w_hid, w_out, cot) = refs[:11]
    out_layer, out_patch, out_vec = refs[11:14]
    out_ag = refs[14 : 14 + np_]
    sc = list(refs[14 + np_ :])

    def take(n):
        got = sc[:n]
        del sc[:n]
        return got

    wq, wp, wh, wo = take(4)
    pb, cb, segv, halo = take(4)
    normed, qb, kv, pt, ctx, res, nm, gres, act, gpre, gctx, edge = take(12)
    hq, hg, lse, hlse, dst, hdst = take(6)
    bm, biasb, vec, vrz, vrx, vrc = take(6)
    sb, rb, ag = take(np_), take(np_), take(np_)
    in_sem, out_sem, halo_s, halo_r, rim_s, rim_r, back_s, back_r, rs_s, rs_r, v_s, v_r = take(12)

    lat = lax.axis_index("lat")
    fld = lax.axis_index("fld")
    core = lax.rem(fld, 2)
    z = lax.div(fld, 2)
    x = lax.rem(lat, 2)
    y = lax.div(lat, 2)
    L, Z, Y = pn.lats, pn.zs, pn.lats // 2
    FD, R, C, TF, T, D, FF = pn.fields, pn.rows, pn.cols, pn.tf, pn.tokens, pn.width, pn.ff

    ins = [(patches, pb), (w_qkv, wq), (seg, segv), (cot, cb), (w_out, wo), (w_proj, wp), (w_hid, wh)]
    loads = [pltpu.make_async_copy(s, d, in_sem.at[i]) for i, (s, d) in enumerate(ins)]
    loads[0].start()
    loads[1].start()

    me = {"core": core, "x": x, "y": y, "lat": lat, "z": z}

    def device(d, i):
        if d == "core":
            return lat, z * 2 + i
        if d == "x":
            return y * 2 + i, fld
        if d == "y":
            return i * 2 + x, fld
        if d == "lat":
            return i, fld
        return lat, i * 2 + core

    def peers(d):
        n = pn.size_of[d]
        places = [lax.rem(me[d] + k, n) for k in range(1, n)]
        return [(i, device(d, i)) for i in places]

    barrier = pltpu.get_barrier_semaphore()
    everyone = peers("core") + peers("lat") + peers("z")
    for _, dev in everyone:
        pl.semaphore_signal(barrier, inc=1, device_id=dev, device_id_type=MESH)
    pl.semaphore_wait(barrier, len(everyone))

    up, down = (lat - 1, fld), (lat + 1, fld)
    has_up, has_down = lat > 0, lat < L - 1

    def remote(src, dst, s, r, dev):
        return pltpu.make_async_remote_copy(
            src_ref=src, dst_ref=dst, send_sem=s, recv_sem=r, device_id=dev, device_id_type=MESH
        )

    def arrived(ref, sem):
        pltpu.make_async_copy(ref, ref, sem).wait()

    half = FD // 2
    halo_copies = []
    for h in range(2):
        some = pl.ds(h * half, half)
        to_up = remote(patches.at[some, pl.ds(0, C)], halo.at[1, some], halo_s.at[0, h], halo_r.at[1, h], up)
        to_dn = remote(patches.at[some, pl.ds(TF - C, C)], halo.at[0, some], halo_s.at[1, h], halo_r.at[0, h], down)
        pl.when(has_up)(to_up.start)
        pl.when(has_down)(to_dn.start)
        halo_copies.append((to_up, to_dn))
    for c in loads[2:]:
        c.start()

    def spot(off, n):
        return pl.ds(pl.multiple_of(off, 16), n)

    class Part:
        def __init__(self, p, number, start, n, order, land):
            self.p, self.number, self.order = p, number, order
            self.off, self.len, self.land = [start], [n], []
            for d in order:
                g = pn.size_of[d]
                n = n // g
                self.land.append(land)
                land += n * (g - 1)
                self.off.append(self.off[-1] + me[d] * n)
                self.len.append(n)
            self.end = land

        def moved(self, i):
            return self.len[i + 1] * (pn.size_of[self.order[i]] - 1)

        def scatter(self, i):
            n = self.len[i + 1]
            for k, (j, dev) in enumerate(peers(self.order[i])):
                src = sb[self.p].at[spot(self.off[i] + j * n, n)]
                dst = rb[self.p].at[pl.ds(self.land[i] + k * n, n)]
                remote(src, dst, rs_s.at[self.number, i], rs_r.at[self.number, i], dev).start()

        def add(self, i):
            n = self.len[i + 1]
            d = self.order[i]
            arrived(rb[self.p].at[pl.ds(self.land[i], self.moved(i))], rs_r.at[self.number, i])
            mine = spot(self.off[i + 1], n)
            total = sb[self.p][mine, :].astype(F32)
            for k in range(pn.size_of[d] - 1):
                total = total + rb[self.p][self.land[i] + k * n : self.land[i] + (k + 1) * n, :].astype(F32)
            to = ag if i == len(self.order) - 1 else sb
            to[self.p][mine, :] = total.astype(BF)

        def gather(self, i):
            s = 4 + i
            mine = ag[self.p].at[spot(self.off[i + 1], self.len[i + 1])]
            for _, dev in peers(self.order[i]):
                remote(mine, mine, rs_s.at[self.number, s], rs_r.at[self.number, s], dev).start()

        def gathered(self, i):
            arrived(ag[self.p].at[pl.ds(0, self.moved(i))], rs_r.at[self.number, 4 + i])

        def step(self, s):
            nd = len(self.order)
            if s < nd:
                if s > 0:
                    self.add(s - 1)
                self.scatter(s)
            elif s == nd:
                self.add(nd - 1)
                self.gather(nd - 1)
            else:
                self.gathered(2 * nd - s)
                if s < 2 * nd:
                    self.gather(2 * nd - 1 - s)

        def finish(self):
            for i in range(len(self.order)):
                for s in (i, 4 + i):
                    arrived(sb[self.p].at[pl.ds(0, self.moved(i))], rs_s.at[self.number, s])

    parts, number = [], 0
    for p in range(np_):
        mine, land = [], 0
        for start, n, order in pn.subs[p]:
            mine.append(Part(p, number, start, n, order, land))
            land = mine[-1].end
            number += 1
        parts.append(mine)
    every = [part for mine in parts for part in mine]
    vec_at = len(every)
    reached = [0] * (vec_at + 1)
    last_step = [2 * len(part.order) for part in every] + [3]

    def out_copy(part):
        rows = pl.ds(part.off[0], part.len[0])
        return pltpu.make_async_copy(ag[part.p].at[rows], out_ag[part.p].at[rows], out_sem.at[2 + part.number])

    codes = [2 * p + i for p, mine in enumerate(parts) for i in range(len(mine))] + [2 * np_]
    number_of = {code: k for k, code in enumerate(codes)}

    def hook(*some):
        steps = []
        for code in some:
            k = number_of.get(code, vec_at + 1)
            if k <= vec_at and reached[k] <= last_step[k]:
                steps.append((k, reached[k]))
                reached[k] += 1

        def run():
            for k, s in steps:
                if k == vec_at:
                    vec_step(s)
                    continue
                every[k].step(s)
                if s == last_step[k]:
                    out_copy(every[k]).start()

        return run

    def place(name):
        return hook(*SCHEDULE.get(name, ()))

    rounds = ((vrz, "z"), (vrx, "lat"), (vrc, "core"))

    def vec_step(s):
        if s > 0:
            buf, d = rounds[s - 1]
            count = pn.size_of[d]
            arrived(buf.at[pl.ds(0, count - 1)], v_r.at[s - 1])
            arrived(buf.at[pl.ds(0, count - 1)], v_s.at[s - 1])
            total = buf[0]
            for k in range(1, count):
                total = total + buf[k]
            vec[...] = total
        if s < 3:
            buf, d = rounds[s]
            buf[me[d]] = vec[...]
            for _, dev in peers(d):
                remote(vec, buf.at[me[d]], v_s.at[s], v_r.at[s], dev).start()
        else:
            pltpu.make_async_copy(vec, out_vec, in_sem.at[0]).start()

    def finish(part):
        part.finish()
        out_copy(part).wait()

    def put(p, start, stride, value):
        rows, lanes = value.shape
        low = value.astype(BF)
        for j in range(lanes // 128):
            at = start + j * stride
            sb[p][at : at + rows, :] = low[:, j * 128 : (j + 1) * 128]

    rid = lax.broadcasted_iota(jnp.int32, (WIDE, WIDE), 0) // HEAD_DIM
    cid = lax.broadcasted_iota(jnp.int32, (WIDE, WIDE), 1) // HEAD_DIM
    same = jnp.where(rid == cid, 1.0, 0.0)
    bm[...] = same.astype(BF)

    ga, ba = gain_a[...].reshape(1, D), bias_a[...].reshape(1, D)
    gm, bmlp = gain_m[...].reshape(1, D), bias_m[...].reshape(1, D)
    loads[0].wait()

    per = max(1, 256 // TF)
    tile = per * TF
    tiles = T // tile

    def rows_at(t):
        return slice(t * tile, (t + 1) * tile)

    def fields_at(t):
        return slice(t * per, (t + 1) * per)

    def norm_one(t):
        n, _ = normalize(pb[fields_at(t)].reshape(tile, D).astype(F32))
        normed[rows_at(t), :] = (n * ga + ba).astype(BF)

    norm_one(0)
    loads[1].wait()
    for t in range(tiles):
        if t + 1 < tiles:
            norm_one(t + 1)
        qb[rows_at(t), :] = dot(normed[rows_at(t), :], wq[:, :D]).astype(BF)
        part = dot(normed[rows_at(t), :], wq[:, D:]).astype(BF)
        kv[fields_at(t), C : C + TF, :] = part.reshape(per, TF, 2 * D)

    loads[2].wait()
    kcol = lax.broadcasted_iota(jnp.int32, (C, WIDE), 0)
    qcol = lax.rem(lax.broadcasted_iota(jnp.int32, (C, WIDE), 1), C)
    away = jnp.abs(kcol - qcol)
    near = jnp.minimum(away, C - away) <= REACH
    diag = lax.broadcasted_iota(jnp.int32, (C, C), 0) == lax.broadcasted_iota(jnp.int32, (C, C), 1)
    for f in range(FD):
        line = segv[f, 0:1, :].astype(F32)
        across = jnp.concatenate([line] * GROUP, axis=1)
        along = jnp.sum(jnp.where(diag, line, 0.0), axis=1, keepdims=True)
        biasb[f] = jnp.where(jnp.logical_and(near, along == across), 0.0, NEG)
    pole_top = jnp.where(has_up, 0.0, NEG)
    pole_bottom = jnp.where(has_down, 0.0, NEG)

    lane_head = lax.broadcasted_iota(jnp.int32, (HEAD_DIM, WIDE), 1) // HEAD_DIM

    def diagonal(o):
        total = o[0:HEAD_DIM]
        for h in range(1, GROUP):
            total = jnp.where(lane_head == h, o[h * HEAD_DIM : (h + 1) * HEAD_DIM], total)
        return total

    def widened(q):
        return jnp.concatenate([q] * GROUP, axis=0) * bm[...]

    fpi = min(FIELDS_AT_ONCE, FD)

    def span(f, row):
        return pl.ds(pl.multiple_of(f * TF + row * C, C), C)

    k_lanes = [slice(g * WIDE, (g + 1) * WIDE) for g in range(2)]
    v_lanes = [slice(D + g * WIDE, D + (g + 1) * WIDE) for g in range(2)]

    def attend(rows, i, carry):
        units = [(i * fpi + j, g, r) for j in range(fpi) for g in range(2) for r in rows]
        scores = []
        for f, g, r in units:
            k = kv[f, r * C : (r + 3) * C, k_lanes[g]]
            scores.append(dot(k, widened(qb[span(f, r), k_lanes[g]]), NT))
        low, logs = [], []
        for (f, g, r), s in zip(units, scores):
            bias = biasb[f]
            first = bias + pole_top if r == 0 else bias
            third = bias + pole_bottom if r == R - 1 else bias
            s = s + jnp.concatenate([first, bias, third], axis=0)
            m = jnp.max(s, axis=0, keepdims=True)
            p = jnp.exp2((s - m) * (SCALE * LOG2E))
            total = row_sums(p)
            logs.append(m * (SCALE * LOG2E) + jnp.log2(total) if r in (0, R - 1) else None)
            low.append((p * (1.0 / total)).astype(BF))
        outs = []
        for (f, g, r), p in zip(units, low):
            v = kv[f, r * C : (r + 3) * C, v_lanes[g]]
            outs.append(diagonal(dot(p, v, TN)).astype(BF))
        for (f, g, r), p, log, o in zip(units, low, logs, outs):
            pt[f, g * R + r] = p
            ctx[span(f, r), k_lanes[g]] = o
            if r in (0, R - 1):
                lse[0 if r == 0 else 1, pl.ds(f * 2 + g, 1), :] = log
        return carry

    if R > 2:
        lax.fori_loop(0, FD // fpi, functools.partial(attend, range(1, R - 1)), 0)

    loads[3].wait()
    loads[4].wait()
    for j in range(FF // BLOCK):
        some = slice(j * BLOCK, (j + 1) * BLOCK)
        gpre[:, some] = dot(cb[...], wo[some, :], NT).astype(BF)

    for h in range(2):
        some = slice(h * half, (h + 1) * half)
        flat = slice(h * half * C, (h + 1) * half * C)
        for side, ok, copy in ((0, has_up, halo_copies[h][1]), (1, has_down, halo_copies[h][0])):
            pl.when(ok)(copy.wait_recv)

            @pl.when(jnp.logical_not(ok))
            def _():
                halo[side, some] = jnp.zeros((half, C, D), BF)

            n, _unused = normalize(halo[side, some].reshape(half * C, D).astype(F32))
            low = (n * ga + ba).astype(BF)
            hq[side, flat, :] = dot(low, wq[:, :D]).astype(BF)
            start = 0 if side == 0 else TF + C
            kv[some, start : start + C, :] = dot(low, wq[:, D:]).astype(BF).reshape(half, C, 2 * D)
        turns = half // fpi
        lax.fori_loop(h * turns, (h + 1) * turns, functools.partial(attend, (0, R - 1)), 0)

    loads[5].wait()
    for t in range(tiles):
        r = pb[fields_at(t)].reshape(tile, D).astype(F32) + dot(ctx[rows_at(t), :], wp[...])
        res[rows_at(t), :] = r
        n, _ = normalize(r)
        nm[rows_at(t), :] = (n * gm + bmlp).astype(BF)

    loads[6].wait()
    blocks = FF // BLOCK
    in_chunk = CHUNK // BLOCK

    def hidden_block(j):
        return slice(j * BLOCK, (j + 1) * BLOCK)

    def kept(ref, j):
        return ref.at[pl.ds(0, T), pl.ds((j % 2) * BLOCK, BLOCK)]

    def mlp_in(j):
        kept(gres, j)[...] = dot(nm[...], wh[:, hidden_block(j)])

    def mlp_mid(j):
        a, da = gelu_both(kept(gres, j)[...])
        act[:, hidden_block(j)] = a.astype(BF)
        gpre[:, hidden_block(j)] = (da * gpre[:, hidden_block(j)].astype(F32)).astype(BF)

    def mlp_out(j):
        c, part = j // in_chunk, j % in_chunk
        put(c, part * BLOCK, CHUNK, dot(act[:, hidden_block(j)], cb[...], TN))
        start = CHUNK * (D // 128) + part * (BLOCK // 128) * D
        put(c, start, D, dot(nm[...], gpre[:, hidden_block(j)], TN))

    mlp_in(0)
    for j in range(blocks):
        if j + 1 < blocks:
            mlp_in(j + 1)
        mlp_mid(j)
        if j > 0:
            mlp_out(j - 1)
        place(f"J{j}")()
    mlp_out(blocks - 1)
    place(f"J{blocks}")()

    zero = jnp.zeros((1, D), F32)

    mlp_gain, mlp_bias = zero, zero

    l_up = remote(lse.at[0], hlse.at[1], back_s.at[2], back_r.at[3], up)
    l_dn = remote(lse.at[1], hlse.at[0], back_s.at[3], back_r.at[2], down)
    pl.when(has_up)(l_up.start)
    pl.when(has_down)(l_dn.start)

    head_rows = lax.broadcasted_iota(jnp.int32, (2 * GROUP, D), 0) == lax.broadcasted_iota(
        jnp.int32, (2 * GROUP, D), 1
    ) // HEAD_DIM
    head_rows = jnp.where(head_rows, 1.0, 0.0).astype(BF)
    own_head = lax.broadcasted_iota(jnp.int32, (GROUP, WIDE), 0) == lax.broadcasted_iota(
        jnp.int32, (GROUP, WIDE), 1
    ) // HEAD_DIM

    def rim_totals(some):
        spots = [(f, side) for f in range(some.start, some.stop) for side in range(2)]
        terms = []
        for f, side in spots:
            row = 0 if side == 0 else R - 1
            mine = ctx[f * TF + row * C : f * TF + (row + 1) * C, :].astype(F32)
            terms.append(mine * gctx[f, row * C : (row + 1) * C, :].astype(F32))
        terms = jnp.concatenate(terms, axis=0)
        high = terms.astype(BF)
        rest = (terms - high.astype(F32)).astype(BF)
        sums = dot(head_rows, high, NT) + dot(head_rows, rest, NT)
        for i, (f, side) in enumerate(spots):
            across = jnp.concatenate([sums[:, i * C : (i + 1) * C]] * GROUP, axis=1)
            for g in range(2):
                own = jnp.where(own_head, across[g * GROUP : (g + 1) * GROUP], 0.0)
                dst[side, 2 * f + g : 2 * f + g + 1, :] = row_sums(own)

    def send_rims(some):
        some = pl.ds(some.start, some.stop - some.start)
        h = some.start // half
        to_up = remote(gctx.at[some, pl.ds(0, C)], hg.at[1, some], rim_s.at[0, h], rim_r.at[1, h], up)
        to_dn = remote(gctx.at[some, pl.ds(TF - C, C)], hg.at[0, some], rim_s.at[1, h], rim_r.at[0, h], down)
        pl.when(has_up)(to_up.start)
        pl.when(has_down)(to_dn.start)

    grad_in = dot(gpre[rows_at(0), :], wh[...], NT)
    for t in range(tiles):
        e = grad_in
        if t + 1 < tiles:
            grad_in = dot(gpre[rows_at(t + 1), :], wh[...], NT)
        n, rstd = normalize(res[rows_at(t), :])
        gr = cb[rows_at(t), :].astype(F32) + norm_pull(e, gm, n, rstd)
        gres[rows_at(t), :] = gr
        low = gr.astype(BF)
        nm[rows_at(t), :] = low
        gctx[fields_at(t)] = dot(low, wp[...], NT).astype(BF).reshape(per, TF, D)
        mlp_gain, mlp_bias = mlp_gain + row_sums(e * n), mlp_bias + row_sums(e)
        rim_totals(fields_at(t))
        send_rims(fields_at(t))
        place(f"E{t}")()

    d_up = remote(dst.at[0], hdst.at[1], back_s.at[4], back_r.at[5], up)
    d_dn = remote(dst.at[1], hdst.at[0], back_s.at[5], back_r.at[4], down)
    pl.when(has_up)(d_up.start)
    pl.when(has_down)(d_dn.start)
    pj = pn.chunks
    place("P")()
    put(pj, 0, D, dot(ctx[...], nm[...], TN))
    place("P1")()

    grad_joined = gpre

    def joined(g, j):
        return slice((3 * g + j) * WIDE, (3 * g + j + 1) * WIDE)

    def edge_rows(g, side, f):
        return pl.ds(pl.multiple_of(((g * 2 + side) * FD + f) * C, C), C)

    def back_group(g, hooks):
        def back_fields(i, carry):
            for when, do in hooks.items():
                pl.when(i == when)(do)
            units = [(i * fpi + j, r) for j in range(fpi) for r in range(R)]
            have = []
            for f, r in units:
                win = slice(r * C, (r + 3) * C)
                qd = widened(qb[span(f, r), k_lanes[g]])
                dod = widened(gctx[f, r * C : (r + 1) * C, k_lanes[g]])
                have.append((qd, dod, kv[f, win, k_lanes[g]], kv[f, win, v_lanes[g]], pt[f, g * R + r]))
            dps = [dot(v, dod, NT) for qd, dod, k, v, p in have]
            dss = []
            for (qd, dod, k, v, p), dp in zip(have, dps):
                wide = p.astype(F32)
                pd = wide * dp
                total = row_sums(pd)
                dss.append(((pd - wide * total) * SCALE).astype(BF))
            dqs = [diagonal(dot(ds, one[2], TN)).astype(BF) for ds, one in zip(dss, have)]
            dks, dvs = [], []
            for (f, r), ds, (qd, dod, k, v, p) in zip(units, dss, have):
                own = slice(C if r == 0 else 0, 2 * C if r == R - 1 else 3 * C)
                first = r + 1 if r == 0 else r
                dks.append((first, dot(ds[own], qd)))
                dvs.append((first, dot(p[own], dod)))
            for (f, r), o in zip(units, dqs):
                grad_joined[span(f, r), joined(g, 0)] = o
            for j in range(fpi):
                f = i * fpi + j
                for what, terms in enumerate((dks, dvs)):
                    for row in range(1, R + 1):
                        total = None
                        for first, term in terms[j * R : (j + 1) * R]:
                            if first <= row < first + term.shape[0] // C:
                                piece = term[(row - first) * C : (row - first + 1) * C]
                                total = piece if total is None else total + piece
                        if row in (1, R):
                            edge[edge_rows(g, 0 if row == 1 else 1, f), what * WIDE : (what + 1) * WIDE] = total
                        else:
                            grad_joined[span(f, row - 1), joined(g, what + 1)] = total.astype(BF)
            return carry

        lax.fori_loop(0, FD // fpi, back_fields, 0)
    def rim_part(h):
        return pl.ds(h * half, half)

    def back_edges(g, sent):
        for to_up, to_dn in sent:
            pl.when(has_up)(to_dn.wait_recv)
            pl.when(has_down)(to_up.wait_recv)

        def back_rims(h):
            units = [(h * half + j, side) for j in range(half) for side in range(2)]
            oks, rows = (has_up, has_down), (0, R - 1)
            have = []
            for f, side in units:
                qd = widened(hq[side, f * C : (f + 1) * C, k_lanes[g]])
                dod = widened(hg[side, f, :, k_lanes[g]])
                keys = slice((rows[side] + 1) * C, (rows[side] + 2) * C)
                have.append((qd, dod, kv[f, keys, k_lanes[g]], kv[f, keys, v_lanes[g]]))
            scores = [dot(k, qd, NT) for qd, dod, k, v in have]
            dps = [dot(v, dod, NT) for qd, dod, k, v in have]
            ps, dss = [], []
            for (f, side), s, dp in zip(units, scores, dps):
                s = (s + biasb[f]) * (SCALE * LOG2E) - hlse[side, pl.ds(f * 2 + g, 1), :]
                p = jnp.where(oks[side], jnp.exp2(s), 0.0)
                ds = p * (dp - hdst[side, pl.ds(f * 2 + g, 1), :]) * SCALE
                ps.append(p.astype(BF))
                dss.append(jnp.where(oks[side], ds, 0.0).astype(BF))
            dks = [dot(ds, one[0]) for ds, one in zip(dss, have)]
            dvs = [dot(p, one[1]) for p, one in zip(ps, have)]
            held = [edge[edge_rows(g, side, f), :] for f, side in units]
            for (f, side), dk, dv, own in zip(units, dks, dvs, held):
                dk = own[:, :WIDE] + jnp.where(oks[side], dk, 0.0)
                dv = own[:, WIDE:] + jnp.where(oks[side], dv, 0.0)
                grad_joined[span(f, rows[side]), joined(g, 1)] = dk.astype(BF)
                grad_joined[span(f, rows[side]), joined(g, 2)] = dv.astype(BF)

        for h in range(2):
            if g == 0:
                pl.when(has_up)(lambda: arrived(hg.at[0, rim_part(h)], rim_r.at[0, h]))
                pl.when(has_down)(lambda: arrived(hg.at[1, rim_part(h)], rim_r.at[1, h]))
            back_rims(h)
            place(f"X{2 * g + h + 1}")()
        put(pj + 1 + g, 0, D, dot(normed[...], grad_joined[:, 3 * g * WIDE : 3 * (g + 1) * WIDE], TN))
        place(f"C{g}")()

    back_group(0, {i: place(f"A{i}") for i in range(4)})
    back_group(1, {i: place(f"B{i}") for i in range(4)})
    for t in range(tiles):
        nm[rows_at(t), :] = (res[rows_at(t), :] + dot(act[rows_at(t), :], wo[...])).astype(BF)
        place(f"D{t}")()
    layer_copy = pltpu.make_async_copy(nm, out_layer, out_sem.at[0])
    layer_copy.start()

    place("X")()
    back_edges(0, ((l_up, l_dn), (d_up, d_dn)))
    back_edges(1, ())

    attn_gain, attn_bias = zero, zero

    def grad_of(t):
        e = None
        for g in range(2):
            for j in range(3):
                w = wq[:, j * D + g * WIDE : j * D + (g + 1) * WIDE]
                term = dot(grad_joined[rows_at(t), joined(g, j)], w, NT)
                e = term if e is None else e + term
        return e

    grad_in = grad_of(0)
    for t in range(tiles):
        e = grad_in
        if t + 1 < tiles:
            grad_in = grad_of(t + 1)
        n, rstd = normalize(pb[fields_at(t)].reshape(tile, D).astype(F32))
        gres[rows_at(t), :] += norm_pull(e, ga, n, rstd)
        attn_gain, attn_bias = attn_gain + row_sums(e * n), attn_bias + row_sums(e)
        place(f"F{t}")()

    patch_copy = pltpu.make_async_copy(gres, out_patch, out_sem.at[1])
    patch_copy.start()
    vec[...] = jnp.concatenate([attn_gain, attn_bias, mlp_gain, mlp_bias, zero, zero, zero, zero], axis=0)
    place("V0")()

    place("T")()
    while any(a <= b for a, b in zip(reached, last_step)):
        for k in sorted(range(vec_at + 1), key=lambda k: reached[k] - last_step[k], reverse=True):
            hook(codes[k])()

    for to_up, to_dn in halo_copies:
        pl.when(has_up)(to_up.wait_send)
        pl.when(has_down)(to_dn.wait_send)
    for h in range(2):
        pl.when(has_up)(lambda: arrived(hg.at[1, rim_part(h)], rim_s.at[0, h]))
        pl.when(has_down)(lambda: arrived(hg.at[0, rim_part(h)], rim_s.at[1, h]))
    for to_up, to_dn in ((l_up, l_dn), (d_up, d_dn)):
        pl.when(has_up)(to_up.wait_send)
        pl.when(has_down)(to_dn.wait_send)
    layer_copy.wait()
    patch_copy.wait()
    pltpu.make_async_copy(vec, out_vec, in_sem.at[0]).wait()
    for part in every:
        finish(part)


def widen(plan, *refs):
    pn = plan
    np_ = len(pn.sizes)
    ag, vec, layer, patch = refs[:np_], refs[np_], refs[np_ + 1], refs[np_ + 2]
    o_layer, o_patch, o_ag, o_ab, o_qkv, o_proj, o_mg, o_mb, o_hid, o_out = refs[np_ + 3 : np_ + 13]
    sc = list(refs[np_ + 13 :])
    low, wide = sc[:np_], sc[np_ : 2 * np_]
    kept_layer, kept_patch, in_sem, out_sem, pass_sem = sc[2 * np_ :]
    D = pn.width
    loads = [pltpu.make_async_copy(ag[p], low[p], in_sem.at[p]) for p in range(np_)]
    for c in loads:
        c.start()
    through = [
        (pltpu.make_async_copy(a, b, pass_sem.at[2 * i]), pltpu.make_async_copy(b, c, pass_sem.at[2 * i + 1]))
        for i, (a, b, c) in enumerate(((layer, kept_layer, o_layer), (patch, kept_patch, o_patch)))
    ]
    for arrive, _ in through:
        arrive.start()
    for i, o in enumerate((o_ag, o_ab, o_mg, o_mb)):
        o[...] = vec[i : i + 1, :].reshape(D)
    stores = []

    def store(src, dst):
        c = pltpu.make_async_copy(src, dst, out_sem.at[len(stores)])
        c.start()
        stores.append(c)

    def spread(p, start, rows, blocks, col):
        for j in range(blocks):
            wide[p][:, col + j * 128 : col + (j + 1) * 128] = low[p][
                start + j * rows : start + (j + 1) * rows, :
            ].astype(F32)

    for p in range(np_):
        loads[p].wait()
        if p == np_ - 1:
            for arrive, leave in through:
                arrive.wait()
                leave.start()
        if p < pn.chunks:
            spread(p, 0, CHUNK, D // 128, 0)
            store(wide[p].at[:, pl.ds(0, D)], o_out.at[pl.ds(p * CHUNK, CHUNK)])
            spread(p, CHUNK * (D // 128), D, CHUNK // 128, D)
            store(wide[p].at[:, pl.ds(D, CHUNK)], o_hid.at[:, pl.ds(p * CHUNK, CHUNK)])
        elif p == pn.chunks:
            spread(p, 0, D, D // 128, 0)
            store(wide[p], o_proj)
        else:
            g = p - pn.chunks - 1
            spread(p, 0, D, 3 * WIDE // 128, 0)
            for j in range(3):
                store(
                    wide[p].at[:, pl.ds(j * WIDE, WIDE)],
                    o_qkv.at[:, pl.ds(j * D + g * WIDE, WIDE)],
                )
    for c in stores + [leave for _, leave in through]:
        c.wait()


def per_device(mesh, patches, segment_ids, gain_attn, bias_attn, w_qkv, w_proj, gain_mlp, bias_mlp, w_hidden, w_output, cotangent):
    fields, rows, cols, width = patches.shape
    ff = w_hidden.shape[1]
    pn = Plan(mesh, fields, rows, cols, width, ff)
    np_ = len(pn.sizes)
    T, TF, D, C, R, FD = pn.tokens, pn.tf, width, cols, rows, fields
    L, Z = pn.lats, pn.zs
    anywhere = pl.BlockSpec(memory_space=pl.ANY)
    vmem = pl.BlockSpec(memory_space=pltpu.VMEM)
    V = pltpu.VMEM
    dma = pltpu.SemaphoreType.DMA
    scratch = [
        V((D, 3 * D), BF), V((D, D), BF), V((D, ff), BF), V((ff, D), BF),
        V((FD, TF, D), BF), V((T, D), BF), V(segment_ids.shape, jnp.int32), V((2, FD, C, D), BF),
        V((T, D), BF), V((T, D), BF), V((FD, TF + 2 * C, 2 * D), BF), V((FD, 2 * R, 3 * C, WIDE), BF),
        V((T, D), BF), V((T, D), F32), V((T, D), BF), V((T, D), F32),
        V((T, ff), BF), V((T, ff), BF), V((FD, TF, D), BF),
        V((max(4 * FD * C, T), 2 * WIDE), F32),
        V((2, FD * C, D), BF), V((2, FD, C, D), BF),
        V((2, 2 * FD, WIDE), F32), V((2, 2 * FD, WIDE), F32), V((2, 2 * FD, WIDE), F32), V((2, 2 * FD, WIDE), F32),
        V((WIDE, WIDE), BF), V((FD, C, WIDE), F32),
        V((8, D), F32), V((Z, 8, D), F32), V((L, 8, D), F32), V((2, 8, D), F32),
    ]
    scratch += [V((n, 128), BF) for n in pn.sizes]
    scratch += [V((n, 128), BF) for n in pn.landing]
    scratch += [V((n, 128), BF) for n in pn.sizes]
    scratch += [
        dma((7,)), dma((2 + pn.n_subs,)), dma((2, 2)), dma((2, 2)), dma((2, 2)), dma((2, 2)), dma((8,)), dma((8,)),
        dma((pn.n_subs, 8)), dma((pn.n_subs, 8)), dma((3,)), dma((3,)),
    ]
    shape = jax.ShapeDtypeStruct
    outs = pl.pallas_call(
        functools.partial(body, pn),
        out_shape=[shape((T, D), BF), shape((T, D), F32), shape((8, D), F32)]
        + [shape((n, 128), BF) for n in pn.sizes],
        in_specs=[anywhere, anywhere, vmem, vmem, anywhere, anywhere, vmem, vmem, anywhere, anywhere, anywhere],
        out_specs=[anywhere] * (3 + np_),
        scratch_shapes=scratch,
        compiler_params=pltpu.CompilerParams(
            collective_id=0, has_side_effects=True, vmem_limit_bytes=62 * 2**20
        ),
        name="block",
    )(
        patches.reshape(FD, TF, D), segment_ids, gain_attn, bias_attn, w_qkv, w_proj, gain_mlp, bias_mlp,
        w_hidden, w_output, cotangent.reshape(T, D),
    )
    layer, patch, vec = outs[:3]
    ags = outs[3:]
    wides = [(D, D + CHUNK)] * pn.chunks + [(D, D)] + [(D, 3 * WIDE)] * 2
    final = pl.pallas_call(
        functools.partial(widen, pn),
        out_shape=[
            shape((T, D), BF), shape((T, D), F32), shape((D,), F32), shape((D,), F32), shape((D, 3 * D), F32),
            shape((D, D), F32), shape((D,), F32), shape((D,), F32), shape((D, ff), F32), shape((ff, D), F32),
        ],
        in_specs=[anywhere] * np_ + [vmem, anywhere, anywhere],
        out_specs=[anywhere, anywhere, vmem, vmem, anywhere, anywhere, vmem, vmem, anywhere, anywhere],
        scratch_shapes=[V((n, 128), BF) for n in pn.sizes]
        + [V(s, F32) for s in wides]
        + [V((T, D), BF), V((T, D), F32), dma((np_,)), dma((2 * pn.chunks + 7,)), dma((4,))],
        compiler_params=pltpu.CompilerParams(vmem_limit_bytes=62 * 2**20),
        name="widen",
    )(*ags, vec, layer, patch)
    block = (FD, R, C, D)
    return (final[0].reshape(block), final[1].reshape(block)) + tuple(final[2:])


def solution(mesh):
    band = P("fld", "lat", None, None)
    return jax.shard_map(
        functools.partial(per_device, mesh),
        mesh=mesh,
        in_specs=(band, P("fld", None, None)) + (P(),) * 8 + (band,),
        out_specs=(band, band) + (P(),) * 8,
        check_vma=False,
    )
```
